32 devices in a mesh: fsdp: 8 (over z, x), ctx: 2 (over core), tp: 2 (over y).
Axes of the slice: x: 2, y: 2, z: 4, core: 2. Of those that a mesh axis runs over, the one named last changes fastest.
Arguments:
- layer_input: bfloat16 [16, 1500, 768], P('fsdp', 'ctx'), may hold values from -6 to 6
- cotangent: bfloat16 [16, 1500, 768], P('fsdp', 'ctx'), may hold values from -6 to 6
- attend_weight: float32 [768, 3, 768], P('fsdp', None, 'tp'), may hold values from -0.3125 to 0.3125
- attend_moment: float32 [768, 3, 768], P('fsdp', None, 'tp'), may hold values from -96 to 96
- attend_square: float32 [768, 3, 768], P('fsdp', None, 'tp'), may hold values from 24 to 96
- shifts_weight: float32 [2, 12, 64], P(None, 'tp', 'fsdp'), may hold values from -1.75 to 1.75
- shifts_moment: float32 [2, 12, 64], P(None, 'tp', 'fsdp'), may hold values from -96 to 96
- shifts_square: float32 [2, 12, 64], P(None, 'tp', 'fsdp'), may hold values from 24 to 96
- output_weight: float32 [768, 768], P('tp', 'fsdp'), may hold values from -1.25 to 1.25
- output_moment: float32 [768, 768], P('tp', 'fsdp'), may hold values from -32 to 32
- output_square: float32 [768, 768], P('tp', 'fsdp'), may hold values from 2.4 to 9.6
- expand_weight: float32 [768, 3072], P('fsdp', 'tp'), may hold values from -0.21875 to 0.21875
- expand_moment: float32 [768, 3072], P('fsdp', 'tp'), may hold values from -32 to 32
- expand_square: float32 [768, 3072], P('fsdp', 'tp'), may hold values from 2.16 to 8.64
- offset_weight: float32 [48, 64], P('tp', 'fsdp'), may hold values from -1.75 to 1.75
- offset_moment: float32 [48, 64], P('tp', 'fsdp'), may hold values from -32 to 32
- offset_square: float32 [48, 64], P('tp', 'fsdp'), may hold values from 2.16 to 8.64
- reduce_weight: float32 [3072, 768], P('tp', 'fsdp'), may hold values from -0.109375 to 0.109375
- reduce_moment: float32 [3072, 768], P('tp', 'fsdp'), may hold values from -64 to 64
- reduce_square: float32 [3072, 768], P('tp', 'fsdp'), may hold values from 8.64 to 34.56
- vectors_weight: float32 [6, 768], P(None, 'fsdp'), may hold values from -0.9 to 1.4
- vectors_moment: float32 [6, 768], P(None, 'fsdp'), may hold values from -96 to 96
- vectors_square: float32 [6, 768], P(None, 'fsdp'), may hold values from 24 to 96
Outputs:
- block_output: bfloat16 [16, 1500, 768], P('fsdp', 'ctx')
- input_grad: float32 [16, 1500, 768], P('fsdp', 'ctx')
- attend_updated: float32 [768, 3, 768], P('fsdp', None, 'tp')
- attend_momentum: float32 [768, 3, 768], P('fsdp', None, 'tp')
- attend_variance: float32 [768, 3, 768], P('fsdp', None, 'tp')
- shifts_updated: float32 [2, 12, 64], P(None, 'tp', 'fsdp')
- shifts_momentum: float32 [2, 12, 64], P(None, 'tp', 'fsdp')
- shifts_variance: float32 [2, 12, 64], P(None, 'tp', 'fsdp')
- output_updated: float32 [768, 768], P('tp', 'fsdp')
- output_momentum: float32 [768, 768], P('tp', 'fsdp')
- output_variance: float32 [768, 768], P('tp', 'fsdp')
- expand_updated: float32 [768, 3072], P('fsdp', 'tp')
- expand_momentum: float32 [768, 3072], P('fsdp', 'tp')
- expand_variance: float32 [768, 3072], P('fsdp', 'tp')
- offset_updated: float32 [48, 64], P('tp', 'fsdp')
- offset_momentum: float32 [48, 64], P('tp', 'fsdp')
- offset_variance: float32 [48, 64], P('tp', 'fsdp')
- reduce_updated: float32 [3072, 768], P('tp', 'fsdp')
- reduce_momentum: float32 [3072, 768], P('tp', 'fsdp')
- reduce_variance: float32 [3072, 768], P('tp', 'fsdp')
- vectors_updated: float32 [6, 768], P(None, 'fsdp')
- vectors_momentum: float32 [6, 768], P(None, 'fsdp')
- vectors_variance: float32 [6, 768], P(None, 'fsdp')
The draws below stay inside these ranges and needn't reach their ends.
All inputs are finite; a program needn't handle non-finite values.
Results may differ from the reference program's by a relative error of at most 0.014.
The reference program's roundings to bfloat16 on the way count: a program that leaves them out, or rounds other values in their place, can miss the bound.
Values may be sent and summed in bfloat16 or wider, within the bound.
No kernel may reach another device: no remote copies, remote signals or barrier semaphores. Data moves between devices by JAX's collectives and lax.ppermute only.
A program may use at most 192 MiB of HBM per device.

```python
import jax
import jax.numpy as jnp
from jax import lax

D = 768
H = 12
HD = 64
FF = 3072
FRAMES = 1500
STEP = 10
CLIPS = 16


def draw_vectors_weight(key, part):
    key = jax.random.fold_in(key, 7)
    gain_key, shift_key = jax.random.split(key)
    gains = jax.random.uniform(gain_key, (6, D), jnp.float32, 0.6, 1.4)
    shifts = jnp.clip(0.3 * jax.random.normal(shift_key, (6, D), jnp.float32), -0.9, 0.9)
    row_ids = jnp.arange(6)[:, None]
    is_gain = (row_ids == 0) | (row_ids == 3)
    return jnp.where(is_gain, gains, shifts)


def block_scale(own_key, shape, cuts, low, top_value):
    loudness, own = 1.0, jax.random.fold_in(own_key, 6)
    for dim, blocks in cuts:
        draws = jnp.exp(jax.random.uniform(jax.random.fold_in(own, dim), (blocks,), jnp.float32, low / len(cuts), top_value / len(cuts)))
        loudness = loudness * jnp.repeat(draws, shape[dim] // blocks).reshape([-1 if axis == dim else 1 for axis in range(len(shape))])
    return loudness


def noise(key, dims, spread, reach, cuts=(), held_as=jnp.bfloat16):
    array = spread * jax.random.normal(key, dims, jnp.float32)
    if cuts:
        array = array * block_scale(key, dims, cuts, -0.22, 0.18)
    return jnp.clip(array, -reach, reach).astype(held_as)


def setup_inputs(seed: int = 0) -> dict:
    arg_keys = jax.random.split(jax.random.key(seed), 24)
    return {
        "layer_input": noise(arg_keys[0], (CLIPS, FRAMES, D), 1.0, 6.0, ((0, 8), (1, 2))),
        "cotangent": noise(arg_keys[1], (CLIPS, FRAMES, D), 1.0, 6.0, ((0, 8), (1, 2))),
        "attend_weight": noise(arg_keys[2], (D, 3, D), (D // 2) ** -0.5, 0.3125, ((0, 8), (2, 2)), jnp.float32),
        "attend_moment": noise(arg_keys[3], (D, 3, D), (0.11 * (1.0 * CLIPS * FRAMES) ** 0.5), 96.0, ((0, 8), (2, 2)), jnp.float32),
        "attend_square": jnp.clip(24.0 + 72.0 * jax.random.uniform(arg_keys[4], (D, 3, D), jnp.float32) ** block_scale(arg_keys[4], (D, 3, D), ((0, 8), (2, 2)), -0.2, 0.2), 24.0, 96.0),
        "shifts_weight": noise(arg_keys[5], (2, H, HD), 0.3, 1.75, ((1, 2), (2, 8)), jnp.float32),
        "shifts_moment": noise(arg_keys[6], (2, H, HD), (0.11 * (1.0 * CLIPS * FRAMES) ** 0.5), 96.0, ((1, 2), (2, 8)), jnp.float32),
        "shifts_square": jnp.clip(24.0 + 72.0 * jax.random.uniform(arg_keys[7], (2, H, HD), jnp.float32) ** block_scale(arg_keys[7], (2, H, HD), ((1, 2), (2, 8)), -0.2, 0.2), 24.0, 96.0),
        "output_weight": noise(arg_keys[8], (D, D), (D // 32) ** -0.5, 1.25, ((0, 2), (1, 8)), jnp.float32),
        "output_moment": noise(arg_keys[9], (D, D), (0.11 * (0.1 * CLIPS * FRAMES) ** 0.5), 32.0, ((0, 2), (1, 8)), jnp.float32),
        "output_square": jnp.clip(2.4 + 7.2000003 * jax.random.uniform(arg_keys[10], (D, D), jnp.float32) ** block_scale(arg_keys[10], (D, D), ((0, 2), (1, 8)), -0.2, 0.2), 2.4, 9.6),
        "expand_weight": noise(arg_keys[11], (D, FF), D ** -0.5, 0.21875, ((0, 8), (1, 2)), jnp.float32),
        "expand_moment": noise(arg_keys[12], (D, FF), (0.11 * (0.09 * CLIPS * FRAMES) ** 0.5), 32.0, ((0, 8), (1, 2)), jnp.float32),
        "expand_square": jnp.clip(2.16 + 6.4800003 * jax.random.uniform(arg_keys[13], (D, FF), jnp.float32) ** block_scale(arg_keys[13], (D, FF), ((0, 8), (1, 2)), -0.2, 0.2), 2.16, 8.64),
        "offset_weight": noise(arg_keys[14], (FF // HD, HD), 0.3, 1.75, ((0, 2), (1, 8)), jnp.float32),
        "offset_moment": noise(arg_keys[15], (FF // HD, HD), (0.11 * (0.09 * CLIPS * FRAMES) ** 0.5), 32.0, ((0, 2), (1, 8)), jnp.float32),
        "offset_square": jnp.clip(2.16 + 6.4800003 * jax.random.uniform(arg_keys[16], (FF // HD, HD), jnp.float32) ** block_scale(arg_keys[16], (FF // HD, HD), ((0, 2), (1, 8)), -0.2, 0.2), 2.16, 8.64),
        "reduce_weight": noise(arg_keys[17], (FF, D), FF ** -0.5, 0.109375, ((0, 2), (1, 8)), jnp.float32),
        "reduce_moment": noise(arg_keys[18], (FF, D), (0.11 * (0.36 * CLIPS * FRAMES) ** 0.5), 64.0, ((0, 2), (1, 8)), jnp.float32),
        "reduce_square": jnp.clip(8.64 + 25.92000102996826 * jax.random.uniform(arg_keys[19], (FF, D), jnp.float32) ** block_scale(arg_keys[19], (FF, D), ((0, 2), (1, 8)), -0.2, 0.2), 8.64, 34.56),
        "vectors_weight": draw_vectors_weight(jax.random.fold_in(arg_keys[23], 71), 0),
        "vectors_moment": noise(arg_keys[21], (6, D), (0.11 * (1.0 * CLIPS * FRAMES) ** 0.5), 96.0, ((1, 8),), jnp.float32),
        "vectors_square": jnp.clip(24.0 + 72.0 * jax.random.uniform(arg_keys[22], (6, D), jnp.float32) ** block_scale(arg_keys[22], (6, D), ((1, 8),), -0.2, 0.2), 24.0, 96.0),
    }


@jax.custom_vjp
def low(v):
    return lax.optimization_barrier(v.astype(jnp.bfloat16)).astype(jnp.float32)

@jax.custom_vjp
def low_back(v):
    return v

def low_keep(v):
    return (low(v), None)

def low_pass(kept, grad):
    return (grad,)

def back_keep(v):
    return (v, None)

def back_low(kept, grad):
    return (low(grad),)
low.defvjp(low_keep, low_pass)
low_back.defvjp(back_keep, back_low)
norm_eps = 1e-05
beta_first = 0.9
beta_second = 0.999
adam_eps = 1e-08
rate_matrix = 0.05
rate_vector = 0.5
decay_matrix = 0.01

def matmul(left, right):
    return jnp.dot(left, right, precision=lax.Precision.HIGHEST, preferred_element_type=jnp.float32)

def layer_norm(values, gain_row, offset_row):
    average = lax.optimization_barrier(jnp.mean(values, axis=-1, keepdims=True))
    centered = values - average
    variance = lax.optimization_barrier(jnp.mean(centered * centered, axis=-1, keepdims=True))
    return centered * lax.rsqrt(variance + norm_eps) * gain_row + offset_row

def attend_clip(inputs):
    queries, keys_all, values_all = inputs
    scores = jnp.einsum('qhd,khd->hqk', queries, keys_all, precision=lax.Precision.HIGHEST, preferred_element_type=jnp.float32)
    scores = low_back(scores) * HD ** (-0.5)
    row_top = lax.optimization_barrier(jnp.max(scores, axis=-1, keepdims=True))
    raised = jnp.exp(scores - row_top)
    row_sum = lax.optimization_barrier(jnp.sum(raised, axis=-1, keepdims=True))
    probability = low(raised / row_sum)
    return jnp.einsum('hqk,khd->qhd', probability, values_all, precision=lax.Precision.HIGHEST, preferred_element_type=jnp.float32)

def forward(layer_input, attend_weight, shifts_weight, output_weight, expand_weight, offset_weight, reduce_weight, vectors_weight):
    attend_low = low(attend_weight).reshape(D, 3 * D)
    shifts_low = low(shifts_weight).reshape(2, D)
    output_low = low(output_weight)
    expand_low = low(expand_weight)
    offset_low = low(offset_weight).reshape(FF)
    reduce_low = low(reduce_weight)
    vectors_low = low(vectors_weight)
    tokens = layer_input.reshape(CLIPS * FRAMES, D)
    normed_one = low(layer_norm(tokens, vectors_low[0], vectors_low[1]))
    project = matmul(normed_one, attend_low).reshape(CLIPS * FRAMES, 3, D)
    queries = low_back(low(project[:, 0] + shifts_low[0]))
    keys_all = low_back(low(project[:, 1]))
    values_all = low_back(low(project[:, 2] + shifts_low[1]))
    shaped = (CLIPS, FRAMES, H, HD)
    attended = lax.map(jax.checkpoint(attend_clip), (queries.reshape(shaped), keys_all.reshape(shaped), values_all.reshape(shaped)))
    attended = low_back(low(attended.reshape(CLIPS * FRAMES, D)))
    branch = low_back(matmul(attended, output_low) + vectors_low[2])
    hidden_one = tokens + branch
    normed_two = low(layer_norm(hidden_one, vectors_low[3], vectors_low[4]))
    expanded = low_back(matmul(normed_two, expand_low) + offset_low)
    activated = low(jax.nn.gelu(expanded, approximate=False))
    mixed = low_back(matmul(activated, reduce_low) + vectors_low[5])
    return (hidden_one + mixed).reshape(CLIPS, FRAMES, D)

def adamw(param, grad, moment, square, rate, decay):
    moment_new = beta_first * moment + (1.0 - beta_first) * grad
    square_new = beta_second * square + (1.0 - beta_second) * grad * grad
    corrected = moment_new / (1.0 - beta_first ** STEP)
    normal_sq = square_new / (1.0 - beta_second ** STEP)
    param_new = param - rate * (corrected / (jnp.sqrt(normal_sq) + adam_eps) + decay * param)
    return (param_new, moment_new, square_new)

def reference(layer_input, cotangent, attend_weight, attend_moment, attend_square, shifts_weight, shifts_moment, shifts_square, output_weight, output_moment, output_square, expand_weight, expand_moment, expand_square, offset_weight, offset_moment, offset_square, reduce_weight, reduce_moment, reduce_square, vectors_weight, vectors_moment, vectors_square):
    result, pullback = jax.vjp(forward, layer_input.astype(jnp.float32), attend_weight, shifts_weight, output_weight, expand_weight, offset_weight, reduce_weight, vectors_weight)
    grads = pullback(cotangent.astype(jnp.float32))
    attend_new = adamw(attend_weight, grads[1], attend_moment, attend_square, rate_matrix, decay_matrix)
    shifts_new = adamw(shifts_weight, grads[2], shifts_moment, shifts_square, rate_vector, 0.0)
    output_new = adamw(output_weight, grads[3], output_moment, output_square, rate_matrix, decay_matrix)
    expand_new = adamw(expand_weight, grads[4], expand_moment, expand_square, rate_matrix, decay_matrix)
    offset_new = adamw(offset_weight, grads[5], offset_moment, offset_square, rate_vector, 0.0)
    reduce_new = adamw(reduce_weight, grads[6], reduce_moment, reduce_square, rate_matrix, decay_matrix)
    vectors_new = adamw(vectors_weight, grads[7], vectors_moment, vectors_square, rate_vector, 0.0)
    return (result.astype(jnp.bfloat16), grads[0], attend_new[0], attend_new[1], attend_new[2], shifts_new[0], shifts_new[1], shifts_new[2], output_new[0], output_new[1], output_new[2], expand_new[0], expand_new[1], expand_new[2], offset_new[0], offset_new[1], offset_new[2], reduce_new[0], reduce_new[1], reduce_new[2], vectors_new[0], vectors_new[1], vectors_new[2])
```

```python
import functools
import math

import jax
import jax.numpy as jnp
from jax import lax
from jax.experimental import pallas as pl
from jax.experimental.pallas import tpu as pltpu
from jax.sharding import PartitionSpec as P

HD = 64
STEP = 10


norm_eps = 1e-05
beta_first = 0.9
beta_second = 0.999
adam_eps = 1e-08
rate_matrix = 0.05
rate_vector = 0.5
decay_matrix = 0.01

bfloat = jnp.bfloat16
single = jnp.float32
LANES = 128
QUERY_ROWS = 256
KEY_ROWS = 256
TOKEN_ROWS = 256
SWAP = [(0, 1), (1, 0)]
EXP_SCALE = HD ** (-0.5) * math.log2(math.e)
MASK = -1e30
VMEM = 56 * 1024 * 1024
NT = (((1,), (1,)), ((), ()))
TN = (((0,), (0,)), ((), ()))


def dot(left, right, dims=(((1,), (0,)), ((), ()))):
    return lax.dot_general(left, right, dims, preferred_element_type=single)


def adamw(param, grad, moment, square, rate, decay):
    moment_new = beta_first * moment + (1.0 - beta_first) * grad
    square_new = beta_second * square + (1.0 - beta_second) * grad * grad
    corrected = moment_new / (1.0 - beta_first**STEP)
    normal_sq = square_new / (1.0 - beta_second**STEP)
    param_new = param - rate * (corrected / (jnp.sqrt(normal_sq) + adam_eps) + decay * param)
    return (param_new, moment_new, square_new)


def norm_parts(values):
    average = jnp.mean(values, axis=-1, keepdims=True)
    centered = values - average
    variance = jnp.mean(centered * centered, axis=-1, keepdims=True)
    inverse = lax.rsqrt(variance + norm_eps)
    return centered * inverse, inverse


def norm_back(grad, unit, inverse, gain):
    scaled = grad * gain
    first = jnp.mean(scaled, axis=-1, keepdims=True)
    second = jnp.mean(scaled * unit, axis=-1, keepdims=True)
    return (scaled - first - unit * second) * inverse


def split_three(column):
    high = column.astype(bfloat).astype(single)
    rest = column - high
    middle = rest.astype(bfloat).astype(single)
    return high, middle, (rest - middle).astype(bfloat).astype(single)


def beside(values, half, extras):
    lane = lax.broadcasted_iota(jnp.int32, values.shape, 1)
    base = HD * (1 - half)
    mine = (lane >= HD) if half else (lane < HD)
    out = jnp.where(mine, values, 0.0)
    for place, extra in enumerate(extras):
        out = jnp.where(lane == base + place, extra, out)
    return out.astype(bfloat)


def pad_column(first_row, rows, period, valid):
    row = first_row + lax.broadcasted_iota(jnp.int32, (rows, 1), 0)
    return jnp.where(row % period < valid, 0.0, MASK)


def attend_kernel(period, valid, q_ref, k_ref, v_ref, o_ref, lse_ref, keys, values):
    @pl.when(pl.program_id(1) == 0)
    def _():
        k = k_ref[...].astype(single)
        v = v_ref[...].astype(single)
        pad = pad_column(0, k.shape[0], period, valid)
        for half in range(2):
            keys[half] = beside(k, half, (pad,))
            values[half] = beside(v, half, (1.0,))

    q = q_ref[...].astype(single)
    lane = lax.broadcasted_iota(jnp.int32, q.shape, 1)
    outs, tops = [], []
    for half in range(2):
        scores = dot(beside(q, half, (1.0,)), keys[half], NT)
        top = jnp.max(scores, axis=1, keepdims=True)
        raised = jnp.exp2((scores - top) * EXP_SCALE)
        both = dot(raised.astype(bfloat), values[half])
        base = HD * (1 - half)
        total = jnp.sum(jnp.where(lane == base, both, 0.0), axis=1, keepdims=True)
        outs.append(both / total)
        tops.append(top + jnp.log2(total) / EXP_SCALE)
    o_ref[...] = jnp.where(lane < HD, outs[0], outs[1]).astype(bfloat)
    lse_ref[...] = jnp.where(lane < HD, tops[0], tops[1])


def attend(qkv, period, valid):
    rows, width = qkv.shape[0], qkv.shape[1] // 3
    pairs = width // LANES
    whole = lambda part: pl.BlockSpec((rows, LANES), lambda j, i: (0, part * pairs + j))
    block = pl.BlockSpec((QUERY_ROWS, LANES), lambda j, i: (i, j))
    return pl.pallas_call(
        functools.partial(attend_kernel, period, valid),
        grid=(pairs, rows // QUERY_ROWS),
        in_specs=[block, whole(1), whole(2)],
        out_specs=[block, block],
        out_shape=[
            jax.ShapeDtypeStruct((rows, width), bfloat),
            jax.ShapeDtypeStruct((rows, width), single),
        ],
        scratch_shapes=[
            pltpu.VMEM((2, rows, LANES), bfloat),
            pltpu.VMEM((2, rows, LANES), bfloat),
        ],
        compiler_params=pltpu.CompilerParams(vmem_limit_bytes=VMEM),
        cost_estimate=pl.CostEstimate(
            flops=16 * rows * rows * LANES * pairs,
            bytes_accessed=20 * rows * width,
            transcendentals=2 * pairs * rows * rows,
        ),
        name="attend",
    )(qkv, qkv, qkv)


def attend_back_kernel(
    period, valid, q_ref, k_ref, v_ref, o_ref, lse_ref, g_ref,
    dq_ref, dk_ref, dv_ref, queries, grads, total,
):
    step = pl.program_id(1)
    lane_all = lax.broadcasted_iota(jnp.int32, q_ref.shape, 1)

    @pl.when(step == 0)
    def _():
        q = q_ref[...].astype(single)
        g = g_ref[...].astype(single)
        product = g * o_ref[...].astype(single)
        for half in range(2):
            mine = (lane_all >= HD) if half else (lane_all < HD)
            inner = jnp.sum(jnp.where(mine, product, 0.0), axis=1, keepdims=True)
            low = jnp.max(jnp.where(mine, lse_ref[...], -jnp.inf), axis=1, keepdims=True)
            queries[half] = beside(q, half, (1.0,) + split_three(-low))
            grads[half] = beside(g, half, (0.0,) + split_three(-inner))
        total[...] = jnp.zeros_like(total)

    k = k_ref[...].astype(single)
    v = v_ref[...].astype(single)
    pad = pad_column(step * k.shape[0], k.shape[0], period, valid)
    lane = lax.broadcasted_iota(jnp.int32, k.shape, 1)
    dks, dvs, dqs = [], [], []
    for half in range(2):
        keys = beside(k, half, (pad, 1.0, 1.0, 1.0))
        values = beside(v, half, (1.0, 1.0, 1.0, 1.0))
        weights = jnp.exp2(dot(keys, queries[half], NT) * EXP_SCALE)
        inner = weights * dot(values, grads[half], NT)
        dvs.append(dot(weights.astype(bfloat), grads[half]))
        low = inner.astype(bfloat)
        dks.append(dot(low, queries[half]))
        dqs.append(dot(keys, low, TN))
    scale = HD ** (-0.5)
    dk_ref[...] = (jnp.where(lane < HD, dks[0], dks[1]) * scale).astype(bfloat)
    dv_ref[...] = jnp.where(lane < HD, dvs[0], dvs[1]).astype(bfloat)
    row = lax.broadcasted_iota(jnp.int32, total.shape, 0)
    total[...] += jnp.where(row < HD, dqs[0], dqs[1])

    @pl.when(step == pl.num_programs(1) - 1)
    def _():
        dq_ref[...] = (total[...].T * scale).astype(bfloat)


def attend_back(qkv, o, lse, grad, period, valid):
    rows, width = o.shape
    pairs = width // LANES
    whole = pl.BlockSpec((rows, LANES), lambda j, i: (0, j))
    part = lambda at: pl.BlockSpec((KEY_ROWS, LANES), lambda j, i: (i, at * pairs + j))
    block = pl.BlockSpec((KEY_ROWS, LANES), lambda j, i: (i, j))
    return pl.pallas_call(
        functools.partial(attend_back_kernel, period, valid),
        grid=(pairs, rows // KEY_ROWS),
        in_specs=[whole, part(1), part(2), whole, whole, whole],
        out_specs=[whole, block, block],
        out_shape=[jax.ShapeDtypeStruct((rows, width), bfloat)] * 3,
        scratch_shapes=[
            pltpu.VMEM((2, rows, LANES), bfloat),
            pltpu.VMEM((2, rows, LANES), bfloat),
            pltpu.VMEM((LANES, rows), single),
        ],
        compiler_params=pltpu.CompilerParams(vmem_limit_bytes=VMEM),
        cost_estimate=pl.CostEstimate(
            flops=40 * rows * rows * LANES * pairs,
            bytes_accessed=20 * rows * width,
            transcendentals=2 * pairs * rows * rows,
        ),
        name="attend_back",
    )(qkv, qkv, qkv, o, lse, grad)


def forward_kernel(n_ref, g_ref, w1_ref, w2_ref, b_ref, y_ref, dn_ref, act_ref, du_ref):
    normed = n_ref[...]
    grad = g_ref[...]
    count, _, units = w1_ref.shape
    mixed = back = 0.0
    for part in range(count):
        cols = slice(part * units, (part + 1) * units)
        u = dot(normed, w1_ref[part]) + b_ref[:, cols]
        phi = 0.5 * (1.0 + lax.erf(u * (0.5**0.5)))
        act = (u * phi).astype(bfloat)
        slope = phi + u * (jnp.exp(-0.5 * u * u) * ((2.0 * math.pi) ** -0.5))
        du = (dot(grad, w2_ref[part]) * slope).astype(bfloat)
        act_ref[:, cols] = act
        du_ref[:, cols] = du
        mixed = mixed + dot(act, w2_ref[part], NT)
        back = back + dot(du, w1_ref[part], NT)
    y_ref[...] = mixed.astype(bfloat)
    dn_ref[...] = back.astype(bfloat)


def feed_forward(normed, grad, weights, bias):
    rows, width = normed.shape
    count = weights.shape[0]
    hidden = bias.shape[1]
    units = hidden // count
    tokens = pl.BlockSpec((TOKEN_ROWS, width), lambda i: (i, 0))
    wide = pl.BlockSpec((TOKEN_ROWS, hidden), lambda i: (i, 0))
    weight = lambda at: pl.BlockSpec((count, width, units), lambda i: (0, 0, at))
    return pl.pallas_call(
        forward_kernel,
        grid=(rows // TOKEN_ROWS,),
        in_specs=[tokens, tokens, weight(0), weight(1), pl.BlockSpec((1, hidden), lambda i: (0, 0))],
        out_specs=[tokens, tokens, wide, wide],
        out_shape=[
            jax.ShapeDtypeStruct((rows, width), bfloat),
            jax.ShapeDtypeStruct((rows, width), bfloat),
            jax.ShapeDtypeStruct((rows, hidden), bfloat),
            jax.ShapeDtypeStruct((rows, hidden), bfloat),
        ],
        compiler_params=pltpu.CompilerParams(vmem_limit_bytes=VMEM),
        cost_estimate=pl.CostEstimate(
            flops=8 * rows * width * hidden,
            bytes_accessed=8 * rows * width + 4 * rows * hidden + 4 * width * hidden,
            transcendentals=2 * rows * hidden,
        ),
        name="feed_forward",
    )(normed, grad, weights, weights, bias)


def swap_core(value):
    return lax.ppermute(value, "ctx", SWAP)


def join(mine, other, first, axis):
    return jnp.concatenate([jnp.where(first, mine, other), jnp.where(first, other, mine)], axis=axis)


def take(value, index, axis=0):
    return lax.dynamic_index_in_dim(value, index, axis, keepdims=False)


def sum_over_tp(value):
    at = lax.axis_index("tp")
    away = lax.ppermute(take(value, 1 - at).astype(bfloat), "tp", SWAP)
    return take(value, at) + away.astype(single)


def sum_over_near(value, axis):
    at = lax.axis_index("fsdp") % 2
    pairs = [(i, i ^ 1) for i in range(lax.axis_size("fsdp"))]
    away = lax.ppermute(take(value, 1 - at, axis).astype(bfloat), "fsdp", pairs)
    return take(value, at, axis) + away.astype(single)


def sum_over_far(value):
    size = lax.axis_size("fsdp")
    far = size // 2
    at = lax.axis_index("fsdp") // 2
    low = value.astype(bfloat)
    total = take(value, at)
    for step in range(1, far):
        pairs = [(i, (i + 2 * step) % size) for i in range(size)]
        total = total + lax.ppermute(take(low, (at + step) % far), "fsdp", pairs).astype(single)
    return total


def scatter(value, near_first):
    size = lax.axis_size("fsdp")
    count, width, columns = value.shape
    rows = width // size
    if near_first:
        value = sum_over_near(value.reshape(count, size // 2, 2, rows, columns), 2)
        value = sum_over_tp(value)
    else:
        value = sum_over_tp(value.reshape(count, size // 2, 2, rows, columns))
        value = sum_over_near(value, 1)
    return sum_over_far(value)


def local(
    layer_input,
    cotangent,
    attend_weight,
    attend_moment,
    attend_square,
    shifts_weight,
    shifts_moment,
    shifts_square,
    output_weight,
    output_moment,
    output_square,
    expand_weight,
    expand_moment,
    expand_square,
    offset_weight,
    offset_moment,
    offset_square,
    reduce_weight,
    reduce_moment,
    reduce_square,
    vectors_weight,
    vectors_moment,
    vectors_square,
):
    size = lax.axis_size("fsdp")
    tps = lax.axis_size("tp")
    core, half = lax.axis_index("ctx"), lax.axis_index("tp")
    first_core, first_tp = core == 0, half == 0
    _, frames, width = layer_input.shape
    period = -(-frames // TOKEN_ROWS) * TOKEN_ROWS
    pad = lambda a: jnp.pad(a, ((0, period - frames), (0, 0)))
    shard = attend_weight.shape[0]
    cols = attend_weight.shape[2] // 2
    heads = cols // HD
    units = expand_weight.shape[1] // 2
    hidden = tps * units

    low = lambda a: a.astype(bfloat)
    attend_mine = lax.dynamic_slice_in_dim(low(attend_weight), core * cols, cols, 2)
    small_mine = jnp.concatenate(
        [low(shifts_weight).reshape(-1), low(offset_weight).reshape(-1), low(vectors_weight).reshape(-1)]
    )
    small_cols = small_mine.size // shard
    pack_one = jnp.concatenate(
        [
            attend_mine.reshape(shard, 3 * cols),
            small_mine.reshape(shard, small_cols),
            jnp.zeros((shard, HD - small_cols), bfloat),
        ],
        axis=1,
    )
    all_one = lax.all_gather(pack_one, ("tp", "fsdp"), axis=0, tiled=True)
    expand_mine = lax.dynamic_slice_in_dim(low(expand_weight), core * units, units, 1)
    reduce_mine = lax.dynamic_slice_in_dim(low(reduce_weight), core * units, units, 0).T
    output_mine = lax.dynamic_slice_in_dim(low(output_weight), core * cols, cols, 0).T
    pack_two = jnp.concatenate(
        [expand_mine, reduce_mine, output_mine, jnp.zeros((shard, HD), bfloat)], axis=1
    )
    pack_two, all_one = lax.optimization_barrier((pack_two, all_one))
    all_two = lax.all_gather(pack_two, ("tp", "fsdp"), axis=0, tiled=True)

    x_mine = pad(take(layer_input, half))
    g_mine = pad(take(cotangent, half))
    tokens = jnp.concatenate([x_mine, swap_core(x_mine)]).astype(single)
    grad_mixed = jnp.concatenate([g_mine, swap_core(g_mine)])

    all_one = all_one.reshape(tps, width, 3 * cols + HD)
    w_attend = all_one[:, :, : 3 * cols].reshape(tps, width, 3, cols)
    w_attend = w_attend.transpose(1, 2, 0, 3).reshape(width, 3 * tps * cols)
    small = all_one[:, :, 3 * cols : 3 * cols + small_cols].reshape(tps, size, -1)
    n_shift, n_offset = shifts_weight.size, offset_weight.size
    shifts = small[:, :, :n_shift].reshape((tps, size) + shifts_weight.shape)
    shifts = shifts.transpose(2, 0, 3, 1, 4).reshape(2, tps, 2 * heads, HD)
    shifts = lax.dynamic_slice_in_dim(shifts, core * heads, heads, 2).reshape(2, 1, tps * cols)
    offset = small[:, :, n_shift : n_shift + n_offset].reshape((tps, size) + offset_weight.shape)
    offset = offset.transpose(0, 2, 1, 3).reshape(tps, 2, units)
    offset = take(offset, core, 1).reshape(1, hidden).astype(single)
    vectors = small[0, :, n_shift + n_offset :].reshape((size,) + vectors_weight.shape)
    vectors = vectors.transpose(1, 0, 2).reshape(-1, 1, width).astype(single)
    bias = jnp.concatenate([shifts[0], jnp.zeros_like(shifts[0]), shifts[1]], axis=1).astype(single)

    unit_one, inverse_one = norm_parts(tokens)
    normed_one = low(unit_one * vectors[0] + vectors[1])
    qkv = low(dot(normed_one, w_attend) + bias)
    attended, lse = attend(qkv, period, frames)

    all_two = all_two.reshape(tps, width, -1)
    w_output = all_two[:, :, 2 * units : 2 * units + cols].transpose(1, 0, 2)
    w_output = w_output.reshape(width, tps * cols)
    branch = low(dot(attended, w_output, NT))
    other = swap_core(branch)

    def with_other(mine, other):
        turned = jnp.concatenate([other[period:], other[:period]])
        return mine.astype(single) + turned.astype(single)

    hidden_one = tokens + with_other(branch, other) + vectors[2]
    unit_two, inverse_two = norm_parts(hidden_one)
    normed_two = low(unit_two * vectors[3] + vectors[4])
    mixed, back, act, du = feed_forward(normed_two, grad_mixed, all_two, offset)
    back_other = swap_core(back)
    mixed_other = swap_core(mixed[period:])
    block = hidden_one[:period] + mixed[:period].astype(single) + mixed_other.astype(single)
    block = low(block + vectors[5])[:frames]
    block_output = join(block[None], lax.ppermute(block, "tp", SWAP)[None], first_tp, 0)

    grad_expand = jnp.stack([dot(normed_two, du[:, t * units : (t + 1) * units], TN) for t in range(tps)])
    grad_reduce = jnp.stack([dot(grad_mixed, act[:, t * units : (t + 1) * units], TN) for t in range(tps)])
    grad_offset = jnp.sum(du.astype(single), axis=0)

    grad_normed = with_other(back, back_other)
    grad_hidden = grad_mixed.astype(single) + norm_back(grad_normed, unit_two, inverse_two, vectors[3])
    grad_branch = low(grad_hidden)
    grad_attended = low(dot(grad_branch, w_output))
    dq, dk, dv = attend_back(qkv, attended, lse, grad_attended, period, frames)
    grad_output = dot(grad_branch, attended, TN).reshape(width, tps, cols).transpose(1, 0, 2)
    grad_qkv = jnp.concatenate([dq, dk, dv], axis=1)
    grad_attend = dot(normed_one, grad_qkv, TN).reshape(width, 3, tps, cols)
    grad_attend = grad_attend.transpose(2, 0, 1, 3).reshape(tps, width, 3 * cols)
    back_one = low(dot(grad_qkv, w_attend, NT))
    back_one = back_one[:period].astype(single) + swap_core(back_one[period:]).astype(single)
    unit_own = unit_one[:period]
    grad_tokens = norm_back(back_one, unit_own, inverse_one[:period], vectors[0])
    input_own = low(grad_hidden[:period] + grad_tokens)[:frames]
    input_grad = join(input_own[None], lax.ppermute(input_own, "tp", SWAP)[None], first_tp, 0)
    input_grad = input_grad.astype(single)

    total = lambda a: jnp.sum(a, axis=0)
    own = grad_normed[:period]
    grad_vectors = jnp.stack(
        [
            total(back_one * unit_own),
            total(back_one),
            total(grad_branch[:period].astype(single)),
            total(own * unit_two[:period]),
            total(own),
            total(g_mine.astype(single)),
        ]
    )
    grad_shifts = jnp.stack([total(dq.astype(single)), total(dv.astype(single))])
    grad_shifts = grad_shifts.reshape(2, tps, 1, cols)
    grad_shifts = jnp.where(jnp.arange(2).reshape(1, 1, 2, 1) == core, grad_shifts, 0.0)
    grad_offset = grad_offset.reshape(tps, 1, units)
    grad_offset = jnp.where(jnp.arange(2).reshape(1, 2, 1) == core, grad_offset, 0.0)
    flat = jnp.concatenate([grad_vectors.reshape(-1), grad_shifts.reshape(-1), grad_offset.reshape(-1)])
    flat = lax.psum(flat.reshape(-1, LANES), ("fsdp", "ctx", "tp")).reshape(-1)
    n_vectors, n_shifts = grad_vectors.size, grad_shifts.size
    at = lax.axis_index("fsdp")
    total_vectors = take(flat[:n_vectors].reshape(6, size, -1), at, 1)
    total_shifts = take(flat[n_vectors : n_vectors + n_shifts].reshape(2, tps, 2 * heads, HD), half, 1)
    total_shifts = take(total_shifts.reshape(2, 2 * heads, size, -1), at, 2)
    total_offset = take(flat[n_vectors + n_shifts :].reshape((tps,) + offset_weight.shape[:1] + (size, -1)), half)
    total_offset = take(total_offset, at, 1)

    sums = [
        scatter(grad_expand, False),
        scatter(grad_reduce, True),
        scatter(jnp.concatenate([grad_attend, grad_output], axis=2), False),
    ]
    mine = jnp.concatenate(sums, axis=1)
    other = swap_core(mine)

    def both(lo, hi, shape=()):
        a, b = mine[:, lo:hi], other[:, lo:hi]
        if shape:
            a, b = a.reshape(shape), b.reshape(shape)
        return join(a, b, first_core, a.ndim - 1)

    total_expand = both(0, units)
    total_reduce = both(units, 2 * units).T
    total_attend = both(2 * units, 2 * units + 3 * cols, (shard, 3, cols))
    total_output = both(2 * units + 3 * cols, 2 * units + 4 * cols).T

    attend_new = adamw(
        attend_weight, total_attend, attend_moment, attend_square, rate_matrix, decay_matrix
    )
    shifts_new = adamw(shifts_weight, total_shifts, shifts_moment, shifts_square, rate_vector, 0.0)
    output_new = adamw(
        output_weight, total_output, output_moment, output_square, rate_matrix, decay_matrix
    )
    expand_new = adamw(
        expand_weight, total_expand, expand_moment, expand_square, rate_matrix, decay_matrix
    )
    offset_new = adamw(offset_weight, total_offset, offset_moment, offset_square, rate_vector, 0.0)
    reduce_new = adamw(
        reduce_weight, total_reduce, reduce_moment, reduce_square, rate_matrix, decay_matrix
    )
    vectors_new = adamw(
        vectors_weight, total_vectors, vectors_moment, vectors_square, rate_vector, 0.0
    )
    return (
        block_output,
        input_grad,
        *attend_new,
        *shifts_new,
        *output_new,
        *expand_new,
        *offset_new,
        *reduce_new,
        *vectors_new,
    )


def solution(mesh):
    tokens = (P("fsdp", "ctx", None),) * 2
    params = (
        (P("fsdp", None, "tp"),) * 3
        + (P(None, "tp", "fsdp"),) * 3
        + (P("tp", "fsdp"),) * 3
        + (P("fsdp", "tp"),) * 3
        + (P("tp", "fsdp"),) * 3
        + (P("tp", "fsdp"),) * 3
        + (P(None, "fsdp"),) * 3
    )
    return jax.shard_map(
        local,
        mesh=mesh,
        in_specs=tokens + params,
        out_specs=tokens + params,
        check_vma=False,
    )
```

```python
import functools
import math

import jax
import jax.numpy as jnp
from jax import lax
from jax.experimental import pallas as pl
from jax.experimental.pallas import tpu as pltpu
from jax.sharding import PartitionSpec as P

HD = 64
STEP = 10


norm_eps = 1e-05
beta_first = 0.9
beta_second = 0.999
adam_eps = 1e-08
rate_matrix = 0.05
rate_vector = 0.5
decay_matrix = 0.01

bfloat = jnp.bfloat16
single = jnp.float32
LANES = 128
TRIPLE = 3 * LANES
PAIRS = 3
ROWS = 384
COLS = 256
FEED_ROWS = 256
QUERY_ROWS = 768
KEY_ROWS = 512
SAFE_EXPONENT = 100.0
SWAP = [(0, 1), (1, 0)]
EXP_SCALE = HD ** (-0.5) * math.log2(math.e)
MASK = -1e30
VMEM = 56 * 1024 * 1024
NT = (((1,), (1,)), ((), ()))
TN = (((0,), (0,)), ((), ()))
PARAMS = pltpu.CompilerParams(vmem_limit_bytes=VMEM)


def dot(left, right, dims=(((1,), (0,)), ((), ()))):
    return lax.dot_general(left, right, dims, preferred_element_type=single)


def adamw(param, grad, moment, square, rate, decay):
    moment_new = beta_first * moment + (1.0 - beta_first) * grad
    square_new = beta_second * square + (1.0 - beta_second) * grad * grad
    corrected = moment_new / (1.0 - beta_first**STEP)
    normal_sq = square_new / (1.0 - beta_second**STEP)
    param_new = param - rate * (corrected / (jnp.sqrt(normal_sq) + adam_eps) + decay * param)
    return (param_new, moment_new, square_new)


def norm_parts(values):
    average = jnp.mean(values, axis=-1, keepdims=True)
    centered = values - average
    variance = jnp.mean(centered * centered, axis=-1, keepdims=True)
    inverse = lax.rsqrt(variance + norm_eps)
    return centered * inverse, inverse


def norm_back(grad, unit, inverse, gain):
    scaled = grad * gain
    first = jnp.mean(scaled, axis=-1, keepdims=True)
    second = jnp.mean(scaled * unit, axis=-1, keepdims=True)
    return (scaled - first - unit * second) * inverse


def column_sum(values):
    return jnp.sum(values, axis=0, keepdims=True)


def turned(value):
    return pltpu.roll(value, HD, 1)


def split_three(column):
    high = column.astype(bfloat).astype(single)
    rest = column - high
    middle = rest.astype(bfloat).astype(single)
    return high, middle, (rest - middle).astype(bfloat).astype(single)


def beside(values, half, extras):
    lane = lax.broadcasted_iota(jnp.int32, values.shape, 1)
    base = HD * (1 - half)
    mine = (lane >= HD) if half else (lane < HD)
    out = jnp.where(mine, values, 0.0)
    for place, extra in enumerate(extras):
        out = jnp.where(lane == base + place, extra, out)
    return out.astype(bfloat)


def pad_column(first_row, rows, period, valid):
    row = first_row + lax.broadcasted_iota(jnp.int32, (rows, 1), 0)
    return jnp.where(row % period < valid, 0.0, MASK)


def whole(shape):
    return pl.BlockSpec(shape, lambda *_: (0,) * len(shape))


def struct(shape, dtype):
    return jax.ShapeDtypeStruct(shape, dtype)


def cost(flops, bytes_accessed, transcendentals=0):
    share = 32
    return pl.CostEstimate(
        flops=int(flops) // share,
        bytes_accessed=int(bytes_accessed) // share,
        transcendentals=int(transcendentals) // share,
    )


def project_kernel(base, x_ref, o_ref, *refs):
    pieces, (bias_ref, vec_ref, qkv_ref, nt_ref, w_ref) = refs[:8], refs[8:]
    step = pl.program_id(0)
    cut, rows, _ = pieces[0].shape
    far = vec_ref.shape[1] // (2 * rows)

    @pl.when(step == 0)
    def _():
        flip = base[2] == 1
        swap = base[0] == 1
        lane = lax.broadcasted_iota(jnp.int32, (rows, LANES), 1)
        for z in range(far):
            at = lax.rem(z - base[1] + far, far)
            inner = lax.rem(at, cut)
            read = lambda n: jnp.where(at < cut, pieces[2 * n][inner], pieces[2 * n + 1][inner])
            own, near, away, across = (read(n) for n in range(4))
            for x in range(2):
                here = jnp.where(flip, own, near) if x else jnp.where(flip, near, own)
                there = jnp.where(flip, away, across) if x else jnp.where(flip, across, away)
                both = (jnp.where(swap, there, here), jnp.where(swap, here, there))
                place = slice((2 * z + x) * rows, (2 * z + x + 1) * rows)
                w_ref[0, place, :] = both[0][:, :TRIPLE]
                w_ref[1, place, :] = both[1][:, :TRIPLE]
                mixed = [b[:, TRIPLE : TRIPLE + LANES].astype(single) for b in both]
                last = [b[:, TRIPLE + LANES :].astype(single) for b in both]
                q = jnp.where(lane < HD, mixed[0], turned(mixed[1]))
                k = jnp.where(lane < HD, turned(mixed[0]), mixed[1])
                v = jnp.where(lane < HD, last[0], turned(last[1]))
                for part, value in enumerate((q, k, v)):
                    w_ref[2, place, part * LANES : (part + 1) * LANES] = value.astype(bfloat)

    x = jnp.where(step < pl.num_programs(0) // 2, x_ref[...], o_ref[...]).astype(single)
    unit, _ = norm_parts(x)
    normed = unit * vec_ref[0:1, :] + vec_ref[1:2, :]
    nt_ref[...] = normed.astype(bfloat).T
    normed = normed.astype(bfloat)
    for j in range(PAIRS):
        cols = slice(j * TRIPLE, (j + 1) * TRIPLE)
        qkv_ref[:, cols] = (dot(normed, w_ref[j]) + bias_ref[:, cols]).astype(bfloat)


def own_block(blocks):
    return lambda i, *_: (jnp.minimum(i, blocks - 1), 0)


def other_block(blocks):
    return lambda i, *_: (jnp.maximum(i - blocks, 0), 0)


def project(base, x_mine, x_other, pieces, bias, vectors):
    period, width = x_mine.shape
    blocks = period // ROWS
    rows = 2 * period
    out = PAIRS * TRIPLE
    return pl.pallas_call(
        project_kernel,
        grid_spec=pltpu.PrefetchScalarGridSpec(
            num_scalar_prefetch=1,
            grid=(2 * blocks,),
            in_specs=[
                pl.BlockSpec((ROWS, width), own_block(blocks)),
                pl.BlockSpec((ROWS, width), other_block(blocks)),
                *[whole(p.shape) for p in pieces],
                whole(bias.shape),
                whole(vectors.shape),
            ],
            out_specs=[
                pl.BlockSpec((ROWS, out), lambda i, *_: (i, 0)),
                pl.BlockSpec((width, ROWS), lambda i, *_: (0, i)),
                whole((PAIRS, width, TRIPLE)),
            ],
        ),
        out_shape=[
            struct((rows, out), bfloat),
            struct((width, rows), bfloat),
            struct((PAIRS, width, TRIPLE), bfloat),
        ],
        compiler_params=PARAMS,
        cost_estimate=cost(2 * rows * width * out, 2 * rows * (2 * width + out) + 4 * width * out),
        name="project",
    )(base, x_mine, x_other, *pieces, bias, vectors)


def attend_kernel(period, valid, q_ref, k_ref, v_ref, o_ref, lse_ref, keys, values, longest):
    def norms(value):
        square = value * value
        lane = lax.broadcasted_iota(jnp.int32, value.shape, 1)
        sums = [jnp.sum(jnp.where(mine, square, 0.0), axis=1) for mine in (lane < HD, lane >= HD)]
        return jnp.maximum(jnp.max(sums[0]), jnp.max(sums[1]))

    @pl.when(pl.program_id(1) == 0)
    def _():
        k = k_ref[...].astype(single)
        v = v_ref[...].astype(single)
        pad = pad_column(0, k.shape[0], period, valid)
        for half in range(2):
            keys[half] = beside(k, half, (pad,))
            values[half] = beside(v, half, (1.0,)).T
        longest[0] = norms(k)

    q = q_ref[...].astype(single)
    bound = norms(q) * longest[0] * (EXP_SCALE * EXP_SCALE)
    safe = bound < SAFE_EXPONENT * SAFE_EXPONENT

    def run(shift):
        outs, tops = [], []
        for half in range(2):
            scores = dot(keys[half], beside(q, half, (1.0,)), NT)
            if shift:
                top = jnp.max(scores, axis=0, keepdims=True)
                scores = scores - top
            raised = jnp.exp2(scores * EXP_SCALE)
            both = dot(values[half], raised.astype(bfloat))
            base = HD * (1 - half)
            total = both[base : base + 1, :]
            outs.append(both / total)
            low = jnp.log2(total) / EXP_SCALE
            tops.append(top + low if shift else low)
        row = lax.broadcasted_iota(jnp.int32, outs[0].shape, 0)
        o_ref[...] = jnp.where(row < HD, outs[0], outs[1]).T.astype(bfloat)
        lse_ref[...] = jnp.where(row < HD, tops[0], tops[1]).T

    @pl.when(safe)
    def _():
        run(False)

    @pl.when(jnp.logical_not(safe))
    def _():
        run(True)


def attend(qkv, period, valid):
    rows = qkv.shape[0]
    width = PAIRS * LANES
    part = lambda at: pl.BlockSpec((rows, LANES), lambda j, i: (0, 3 * j + at))
    block = pl.BlockSpec((QUERY_ROWS, LANES), lambda j, i: (i, j))
    return pl.pallas_call(
        functools.partial(attend_kernel, period, valid),
        grid=(PAIRS, rows // QUERY_ROWS),
        in_specs=[pl.BlockSpec((QUERY_ROWS, LANES), lambda j, i: (i, 3 * j)), part(1), part(2)],
        out_specs=[block, block],
        out_shape=[struct((rows, width), bfloat), struct((rows, width), single)],
        scratch_shapes=[
            pltpu.VMEM((2, rows, LANES), bfloat),
            pltpu.VMEM((2, LANES, rows), bfloat),
            pltpu.SMEM((1,), single),
        ],
        compiler_params=PARAMS,
        cost_estimate=cost(16 * rows * rows * LANES * PAIRS, 20 * rows * width, 2 * PAIRS * rows * rows),
        name="attend",
    )(qkv, qkv, qkv)


def attend_back_kernel(
    period, valid, q_ref, k_ref, v_ref, o_ref, lse_ref, g_ref,
    out_ref, queries, queries_turned, grads, grads_turned, total,
):
    step = pl.program_id(0)
    lane_all = lax.broadcasted_iota(jnp.int32, q_ref.shape, 1)

    @pl.when(step == 0)
    def _():
        q = q_ref[...].astype(single)
        g = g_ref[...].astype(single)
        product = g * o_ref[...].astype(single)
        for half in range(2):
            mine = (lane_all >= HD) if half else (lane_all < HD)
            inner = jnp.sum(jnp.where(mine, product, 0.0), axis=1, keepdims=True)
            low = jnp.max(jnp.where(mine, lse_ref[...], -jnp.inf), axis=1, keepdims=True)
            queries[half] = beside(q, half, (1.0,) + split_three(-low))
            grads[half] = beside(g, half, (0.0,) + split_three(-inner))
            queries_turned[half] = queries[half].T
            grads_turned[half] = grads[half].T
        total[...] = jnp.zeros_like(total)

    k = k_ref[...].astype(single)
    v = v_ref[...].astype(single)
    pad = pad_column(step * k.shape[0], k.shape[0], period, valid)
    dks, dvs, dqs = [], [], []
    for half in range(2):
        keys = beside(k, half, (pad, 1.0, 1.0, 1.0))
        values = beside(v, half, (1.0, 1.0, 1.0, 1.0))
        weights = jnp.exp2(dot(queries[half], keys, NT) * EXP_SCALE)
        inner = weights * dot(grads[half], values, NT)
        dvs.append(dot(grads_turned[half], weights.astype(bfloat)))
        low = inner.astype(bfloat)
        dks.append(dot(queries_turned[half], low))
        dqs.append(dot(low, keys))
    scale = HD ** (-0.5)
    here = pl.ds(pl.multiple_of(step * KEY_ROWS, KEY_ROWS), KEY_ROWS)
    row = lax.broadcasted_iota(jnp.int32, dks[0].shape, 0)
    dk = jnp.where(row < HD, dks[0], dks[1]) * scale
    out_ref[here, LANES : 2 * LANES] = dk.T.astype(bfloat)
    out_ref[here, 2 * LANES :] = jnp.where(row < HD, dvs[0], dvs[1]).T.astype(bfloat)
    total[...] += jnp.where(lane_all < HD, dqs[0], dqs[1])

    @pl.when(step == pl.num_programs(0) - 1)
    def _():
        out_ref[:, :LANES] = (total[...] * scale).astype(bfloat)


def attend_back(j, qkv, o, lse, grad, period, valid):
    rows = qkv.shape[0]
    column = lambda at: pl.BlockSpec((rows, LANES), lambda i: (0, at))
    block = lambda at: pl.BlockSpec((KEY_ROWS, LANES), lambda i: (i, at))
    return pl.pallas_call(
        functools.partial(attend_back_kernel, period, valid),
        grid=(rows // KEY_ROWS,),
        in_specs=[column(3 * j), block(3 * j + 1), block(3 * j + 2), column(j), column(j), column(j)],
        out_specs=whole((rows, TRIPLE)),
        out_shape=struct((rows, TRIPLE), bfloat),
        scratch_shapes=[
            pltpu.VMEM((2, rows, LANES), bfloat),
            pltpu.VMEM((2, LANES, rows), bfloat),
            pltpu.VMEM((2, rows, LANES), bfloat),
            pltpu.VMEM((2, LANES, rows), bfloat),
            pltpu.VMEM((rows, LANES), single),
        ],
        compiler_params=PARAMS,
        cost_estimate=cost(40 * rows * rows * LANES, 20 * rows * LANES, 2 * rows * rows),
        name=f"attend_back_{j}",
    )(qkv, qkv, qkv, o, lse, grad)


def output_kernel(o_ref, w_ref, out_ref, full_ref):
    @pl.when(pl.program_id(0) == 0)
    def _():
        lane = lax.broadcasted_iota(jnp.int32, (w_ref.shape[1], LANES), 1)
        full_ref[:, :LANES] = w_ref[0, :, :LANES]
        full_ref[:, LANES : 2 * LANES] = w_ref[1, :, :LANES]
        last = [w_ref[t, :, LANES:].astype(single) for t in range(2)]
        full_ref[:, 2 * LANES :] = jnp.where(lane < HD, last[0], turned(last[1])).astype(bfloat)

    out_ref[...] = dot(o_ref[...], full_ref[...], NT).astype(bfloat)


def output_project(o, weights, place):
    rows, width = o.shape[0], weights.shape[1]
    columns = o.shape[1]
    return pl.pallas_call(
        output_kernel,
        grid=(rows // ROWS,),
        in_specs=[
            pl.BlockSpec((ROWS, columns), lambda i: (i, 0)),
            pl.BlockSpec((2, width, 2 * LANES), lambda i: (0, 0, place // (2 * LANES))),
        ],
        out_specs=[pl.BlockSpec((ROWS, width), lambda i: (i, 0)), whole((width, columns))],
        out_shape=[struct((rows, width), bfloat), struct((width, columns), bfloat)],
        compiler_params=PARAMS,
        cost_estimate=cost(2 * rows * width * columns, 2 * rows * (width + columns)),
        name="output_project",
    )(o, weights)


def feed_kernel(
    x_ref, xo_ref, p_ref, po_ref, g_ref, go_ref, w1_ref, w2_ref, b_ref, vec_ref,
    h_ref, nt_ref, gt_ref, y_ref, yo_ref, dn_ref, act_ref, du_ref, db_ref,
):
    step = pl.program_id(0)
    mine = step < pl.num_programs(0) // 2
    x = jnp.where(mine, x_ref[...], xo_ref[...]).astype(single)
    grad = jnp.where(mine, g_ref[...], go_ref[...])
    hidden = x + (p_ref[...].astype(single) + po_ref[...].astype(single)) + vec_ref[2:3, :]
    h_ref[...] = hidden
    unit, _ = norm_parts(hidden)
    normed = unit * vec_ref[3:4, :] + vec_ref[4:5, :]
    nt_ref[...] = normed.astype(bfloat).T
    gt_ref[...] = grad.T
    normed = normed.astype(bfloat)
    count, _, units = w1_ref.shape
    mixed = back = 0.0

    @pl.when(step == 0)
    def _():
        db_ref[...] = jnp.zeros_like(db_ref)

    for part in range(count):
        cols = slice(part * units, (part + 1) * units)
        u = dot(normed, w1_ref[part]) + b_ref[:, cols]
        phi = 0.5 * (1.0 + lax.erf(u * (0.5**0.5)))
        act = (u * phi).astype(bfloat)
        slope = phi + u * (jnp.exp(-0.5 * u * u) * ((2.0 * math.pi) ** -0.5))
        du = (dot(grad, w2_ref[part]) * slope).astype(bfloat)
        act_ref[:, cols] = act
        du_ref[:, cols] = du
        db_ref[:, cols] += column_sum(du.astype(single))
        mixed = mixed + dot(act, w2_ref[part], NT)
        back = back + dot(du, w1_ref[part], NT)
    dn_ref[...] = back.astype(bfloat)

    @pl.when(mine)
    def _():
        y_ref[...] = mixed.astype(bfloat)

    @pl.when(jnp.logical_not(mine))
    def _():
        yo_ref[...] = mixed.astype(bfloat)


def feed_forward(x_mine, x_other, part, part_other, g_mine, g_other, weights, bias, vectors):
    rows, width = part.shape
    blocks = rows // FEED_ROWS // 2
    count, hidden = weights.shape[0], bias.shape[1]
    units = hidden // count
    tokens = pl.BlockSpec((FEED_ROWS, width), lambda i: (i, 0))
    crossed = pl.BlockSpec((FEED_ROWS, width), lambda i: ((i + blocks) % (2 * blocks), 0))
    wide = pl.BlockSpec((FEED_ROWS, hidden), lambda i: (i, 0))
    tall = pl.BlockSpec((width, FEED_ROWS), lambda i: (0, i))
    own = pl.BlockSpec((FEED_ROWS, width), own_block(blocks))
    other = pl.BlockSpec((FEED_ROWS, width), other_block(blocks))
    weight = lambda at: pl.BlockSpec((count, width, units), lambda i: (0, 0, at))
    return pl.pallas_call(
        feed_kernel,
        grid=(2 * blocks,),
        in_specs=[
            own, other, tokens, crossed, own, other, weight(0), weight(1),
            whole(bias.shape), whole(vectors.shape),
        ],
        out_specs=[tokens, tall, tall, own, other, tokens, wide, wide, whole((1, hidden))],
        out_shape=[
            struct((rows, width), single),
            struct((width, rows), bfloat),
            struct((width, rows), bfloat),
            struct((rows // 2, width), bfloat),
            struct((rows // 2, width), bfloat),
            struct((rows, width), bfloat),
            struct((rows, hidden), bfloat),
            struct((rows, hidden), bfloat),
            struct((1, hidden), single),
        ],
        compiler_params=PARAMS,
        cost_estimate=cost(
            8 * rows * width * hidden,
            18 * rows * width + 4 * rows * hidden + 4 * width * hidden,
            2 * rows * hidden,
        ),
        name="feed_forward",
    )(x_mine, x_other, part, part_other, g_mine, g_other, weights, weights, bias, vectors)


def put(base, keep_ref, send_ref, t, value, cols):
    far, rows = keep_ref.shape[1], keep_ref.shape[2]
    first = base[2] == 0
    for z in range(far):
        at = jnp.bitwise_xor(z, base[1])
        lo = value[2 * z * rows : (2 * z + 1) * rows].astype(bfloat)
        hi = value[(2 * z + 1) * rows : (2 * z + 2) * rows].astype(bfloat)
        keep_ref[t, at, :, cols] = jnp.where(first, lo, hi)
        send_ref[t, at, :, cols] = jnp.where(first, hi, lo)


def expand_grad_kernel(base, left_ref, right_ref, keep_ref, send_ref):
    put(base, keep_ref, send_ref, 0, dot(left_ref[...], right_ref[...]), slice(0, COLS))


def expand_grad(base, layout, left, right):
    width, rows = left.shape
    units = right.shape[1] // 2
    tiles = units // COLS
    shape = (2,) + layout + (units,)
    out = pl.BlockSpec((1,) + layout + (COLS,), lambda t, j, base: (t, 0, 0, j))
    return pl.pallas_call(
        expand_grad_kernel,
        grid_spec=pltpu.PrefetchScalarGridSpec(
            num_scalar_prefetch=1,
            grid=(2, tiles),
            in_specs=[
                whole(left.shape),
                pl.BlockSpec((rows, COLS), lambda t, j, base: (0, (t + base[0]) % 2 * tiles + j)),
            ],
            out_specs=[out, out],
        ),
        out_shape=[struct(shape, bfloat)] * 2,
        compiler_params=PARAMS,
        cost_estimate=cost(4 * rows * width * units, 2 * rows * (width + 2 * units) + 4 * width * units),
        name="expand_grad",
    )(base, left, right)


def reduce_grad_kernel(base, left_ref, right_ref, branch_ref, o_ref, keep_ref, send_ref):
    t, j = pl.program_id(0), pl.program_id(1)
    cols = slice(0, COLS)
    last = pl.num_programs(1) - 1

    @pl.when(j < last)
    def _():
        put(base, keep_ref, send_ref, 0, dot(left_ref[...], right_ref[...]), cols)

    @pl.when(j == last)
    def _():
        at = lax.rem(t + base[0], 2)
        mine = dot(branch_ref[...], o_ref[:, pl.ds(pl.multiple_of(at * LANES, LANES), LANES)])
        mixed = dot(branch_ref[...], o_ref[:, 2 * LANES :])
        mixed = jnp.where(at == 0, mixed, turned(mixed))
        put(base, keep_ref, send_ref, 0, jnp.concatenate([mine, mixed], axis=1), cols)


def reduce_grad(base, layout, left, right, branch, o):
    width, rows = left.shape
    units = right.shape[1] // 2
    tiles = units // COLS
    total = units + COLS
    shape = (2,) + layout + (total,)
    out = pl.BlockSpec((1,) + layout + (COLS,), lambda t, j, base: (t, 0, 0, j))
    place = lambda t, j, base: (0, (t + base[0]) % 2 * tiles + jnp.minimum(j, tiles - 1))
    return pl.pallas_call(
        reduce_grad_kernel,
        grid_spec=pltpu.PrefetchScalarGridSpec(
            num_scalar_prefetch=1,
            grid=(2, tiles + 1),
            in_specs=[
                whole(left.shape), pl.BlockSpec((rows, COLS), place), whole(branch.shape), whole(o.shape)
            ],
            out_specs=[out, out],
        ),
        out_shape=[struct(shape, bfloat)] * 2,
        compiler_params=PARAMS,
        cost_estimate=cost(4 * rows * width * total, 2 * rows * (2 * width + 2 * total) + 4 * width * total),
        name="reduce_grad",
    )(base, left, right, branch, o)


def pair_grad_kernel(base, left_ref, a_ref, b_ref, keep_ref, send_ref):
    left = left_ref[...]
    pairs = [dot(left, ref[...]) for ref in (a_ref, b_ref)]
    same = base[0] == 0
    for t in range(2):
        put(base, keep_ref, send_ref, t, jnp.where(same, pairs[t], pairs[1 - t]), slice(0, TRIPLE))


def mixed_grad_kernel(base, left_ref, ref, keep_ref, send_ref):
    full = dot(left_ref[...], ref[...])
    q, k, v = (full[:, part * LANES : (part + 1) * LANES] for part in range(3))
    lane = lax.broadcasted_iota(jnp.int32, q.shape, 1)
    mixed = [
        (jnp.where(lane < HD, q, turned(k)), v),
        (jnp.where(lane < HD, turned(q), k), turned(v)),
    ]
    same = base[0] == 0
    for t in range(2):
        for place in range(2):
            cols = slice(place * LANES, (place + 1) * LANES)
            value = jnp.where(same, mixed[t][place], mixed[1 - t][place])
            put(base, keep_ref, send_ref, t, value, cols)


def attend_grad(base, layout, left, grads):
    width, rows = left.shape
    count = len(grads)
    columns = TRIPLE if count == 2 else 2 * LANES
    shape = (2,) + layout + (columns,)
    return pl.pallas_call(
        pair_grad_kernel if count == 2 else mixed_grad_kernel,
        grid_spec=pltpu.PrefetchScalarGridSpec(
            num_scalar_prefetch=1,
            grid=(1,),
            in_specs=[whole(left.shape)] + [whole(g.shape) for g in grads],
            out_specs=[whole(shape)] * 2,
        ),
        out_shape=[struct(shape, bfloat)] * 2,
        compiler_params=PARAMS,
        cost_estimate=cost(
            2 * count * rows * width * TRIPLE, 2 * rows * (width + count * TRIPLE) + 8 * width * columns
        ),
        name=f"attend_grad_{count}",
    )(base, left, *grads)


def middle_kernel(
    p_ref, po_ref, h_ref, g_ref, go_ref, y_ref, yo_ref, w_ref, vec_ref,
    out_ref, dh_ref, bt_ref, do_ref, sums_ref,
):
    step = pl.program_id(0)
    mine = step < pl.num_programs(0) // 2
    grad = jnp.where(mine, g_ref[...], go_ref[...]).astype(single)
    hidden = h_ref[...]
    unit, inverse = norm_parts(hidden)
    normed = p_ref[...].astype(single) + po_ref[...].astype(single)
    after = grad + norm_back(normed, unit, inverse, vec_ref[3:4, :])
    bt_ref[...] = after.astype(bfloat).T
    branch = after.astype(bfloat)
    do_ref[...] = dot(branch, w_ref[...]).astype(bfloat)

    @pl.when(step == 0)
    def _():
        sums_ref[...] = jnp.zeros_like(sums_ref)

    @pl.when(mine)
    def _():
        dh_ref[...] = after
        mixed = y_ref[...].astype(single) + yo_ref[...].astype(single)
        out_ref[...] = (hidden + mixed + vec_ref[5:6, :]).astype(bfloat)
        sums_ref[2:3, :] += column_sum(branch.astype(single))
        sums_ref[3:4, :] += column_sum(normed * unit)
        sums_ref[4:5, :] += column_sum(normed)
        sums_ref[5:6, :] += column_sum(grad)


def middle(part, part_other, hidden, g_mine, g_other, mixed, mixed_other, weight, vectors):
    rows, width = part.shape
    blocks = rows // ROWS // 2
    tokens = pl.BlockSpec((ROWS, width), lambda i: (i, 0))
    crossed = pl.BlockSpec((ROWS, width), lambda i: ((i + blocks) % (2 * blocks), 0))
    own = pl.BlockSpec((ROWS, width), own_block(blocks))
    other = pl.BlockSpec((ROWS, width), other_block(blocks))
    columns = weight.shape[1]
    return pl.pallas_call(
        middle_kernel,
        grid=(2 * blocks,),
        in_specs=[
            tokens, crossed, tokens, own, other, own, own, whole(weight.shape), whole(vectors.shape)
        ],
        out_specs=[
            own,
            own,
            pl.BlockSpec((width, ROWS), lambda i: (0, i)),
            pl.BlockSpec((ROWS, columns), lambda i: (i, 0)),
            whole((8, width)),
        ],
        out_shape=[
            struct((rows // 2, width), bfloat),
            struct((rows // 2, width), single),
            struct((width, rows), bfloat),
            struct((rows, columns), bfloat),
            struct((8, width), single),
        ],
        compiler_params=PARAMS,
        cost_estimate=cost(2 * rows * width * columns, 16 * rows * width),
        name="middle",
    )(part, part_other, hidden, g_mine, g_other, mixed, mixed_other, weight, vectors)


def project_back_kernel(a_ref, b_ref, c_ref, w_ref, out_ref, other_ref, sums_ref):
    @pl.when(pl.program_id(0) == 0)
    def _():
        sums_ref[...] = jnp.zeros_like(sums_ref)

    total = 0.0
    for j, ref in enumerate((a_ref, b_ref, c_ref)):
        grad = ref[...]
        total = total + dot(grad, w_ref[j], NT)
        cols = slice(j * TRIPLE, (j + 1) * TRIPLE)
        sums_ref[:, cols] += column_sum(grad.astype(single))
    mine = pl.program_id(0) < pl.num_programs(0) // 2

    @pl.when(mine)
    def _():
        out_ref[...] = total.astype(bfloat)

    @pl.when(jnp.logical_not(mine))
    def _():
        other_ref[...] = total.astype(bfloat)


def project_back(grads, weight):
    rows = grads[0].shape[0]
    width = weight.shape[1]
    block = pl.BlockSpec((ROWS, TRIPLE), lambda i: (i, 0))
    return pl.pallas_call(
        project_back_kernel,
        grid=(rows // ROWS,),
        in_specs=[block, block, block, whole(weight.shape)],
        out_specs=[
            pl.BlockSpec((ROWS, width), own_block(rows // ROWS // 2)),
            pl.BlockSpec((ROWS, width), other_block(rows // ROWS // 2)),
            whole((1, PAIRS * TRIPLE)),
        ],
        out_shape=[struct((rows // 2, width), bfloat)] * 2 + [struct((1, PAIRS * TRIPLE), single)],
        compiler_params=PARAMS,
        cost_estimate=cost(6 * rows * width * TRIPLE, 2 * rows * (width + 3 * TRIPLE)),
        name="project_back",
    )(*grads, weight)


def first_back_kernel(p_ref, po_ref, x_ref, dh_ref, vec_ref, out_ref, sums_ref):
    @pl.when(pl.program_id(0) == 0)
    def _():
        sums_ref[...] = jnp.zeros_like(sums_ref)

    unit, inverse = norm_parts(x_ref[...].astype(single))
    normed = p_ref[...].astype(single) + po_ref[...].astype(single)
    out_ref[...] = (dh_ref[...] + norm_back(normed, unit, inverse, vec_ref[0:1, :])).astype(bfloat)
    sums_ref[0:1, :] += column_sum(normed * unit)
    sums_ref[1:2, :] += column_sum(normed)


def first_back(part, part_other, x_mine, grad_hidden, vectors):
    rows, width = x_mine.shape
    tokens = pl.BlockSpec((ROWS, width), lambda i: (i, 0))
    return pl.pallas_call(
        first_back_kernel,
        grid=(rows // ROWS,),
        in_specs=[tokens, tokens, tokens, tokens, whole(vectors.shape)],
        out_specs=[tokens, whole((8, width))],
        out_shape=[struct((rows, width), bfloat), struct((8, width), single)],
        compiler_params=PARAMS,
        cost_estimate=cost(20 * rows * width, 12 * rows * width),
        name="first_back",
    )(part, part_other, x_mine, grad_hidden, vectors)


def assemble_kernel(place, mine_ref, other_ref, out_ref):
    here = pl.program_id(0) == place[0]
    value = jnp.where(here, mine_ref[...], other_ref[...]).astype(out_ref.dtype)
    out_ref[0] = value[: out_ref.shape[1]]


def assemble(place, mine, other, frames, dtype):
    rows, width = mine.shape
    return pl.pallas_call(
        assemble_kernel,
        grid_spec=pltpu.PrefetchScalarGridSpec(
            num_scalar_prefetch=1,
            grid=(2,),
            in_specs=[whole(mine.shape), whole(other.shape)],
            out_specs=pl.BlockSpec((1, frames, width), lambda i, place: (i, 0, 0)),
        ),
        out_shape=struct((2, frames, width), dtype),
        compiler_params=PARAMS,
        cost_estimate=cost(0, 12 * rows * width),
        name="assemble",
    )(place, mine, other)


def swap_core(value):
    return lax.ppermute(value, "ctx", SWAP)


def swap_tp(value):
    return lax.ppermute(value, "tp", SWAP)


def send_fsdp(value, target):
    size = lax.axis_size("fsdp")
    return lax.ppermute(value, "fsdp", [(i, target(i) % size) for i in range(size)])


def swap_near(value):
    return send_fsdp(value, lambda i: i ^ 1)


def after(value, *others):
    return lax.optimization_barrier((value,) + others)[0]


def wide(value):
    return value.astype(single)


def low(value):
    return value.astype(bfloat)


def join(mine, other, first, axis):
    return jnp.concatenate([jnp.where(first, mine, other), jnp.where(first, other, mine)], axis=axis)


def take(value, index, axis=0):
    return lax.dynamic_index_in_dim(value, index, axis, keepdims=False)


def gather_quick(shard):
    size = lax.axis_size("fsdp")
    far = size // 2
    if size != 8:
        full = lax.all_gather(shard, ("tp", "fsdp"), axis=0, tiled=True)
        return [p[None] for p in jnp.split(full, 4) for _ in range(2)]
    steps = [send_fsdp(shard, lambda i, k=k: i + 2 * k) for k in range(1, far)]
    own = [shard] + steps[::-1]
    cut = far // 2
    lo, hi = jnp.stack(own[:cut]), jnp.stack(own[cut:])
    near_lo, away_lo, away_hi, near_hi = swap_near(lo), swap_tp(lo), swap_tp(hi), swap_near(hi)
    return [lo, hi, near_lo, near_hi, away_lo, away_hi, swap_near(away_lo), swap_tp(near_hi)]


def fold(value, stride, axis):
    shape = value.shape
    halves = value.reshape(shape[:axis] + (shape[axis] // 2, 2) + shape[axis + 1 :])
    away = low(lax.index_in_dim(halves, 1, axis + 1, keepdims=False))
    return lax.index_in_dim(halves, 0, axis + 1, keepdims=False), away, send_fsdp(away, lambda i: i ^ stride)


def sum_all(value):
    stride = 2
    while stride < lax.axis_size("fsdp"):
        value = value + send_fsdp(value, lambda i: i ^ stride)
        stride *= 2
    value = value + swap_near(value)
    return value + swap_tp(value)


def scatter_any(keep, send):
    full = wide(jnp.concatenate([keep, send], axis=2)[:, 0])
    full = lax.psum_scatter(full, "tp", scatter_dimension=0, tiled=True)
    return lax.psum_scatter(full, "fsdp", scatter_dimension=1, tiled=True)[0]


def local(
    layer_input,
    cotangent,
    attend_weight,
    attend_moment,
    attend_square,
    shifts_weight,
    shifts_moment,
    shifts_square,
    output_weight,
    output_moment,
    output_square,
    expand_weight,
    expand_moment,
    expand_square,
    offset_weight,
    offset_moment,
    offset_square,
    reduce_weight,
    reduce_moment,
    reduce_square,
    vectors_weight,
    vectors_moment,
    vectors_square,
):
    size = lax.axis_size("fsdp")
    quick = size == 8
    core, half, at = lax.axis_index("ctx"), lax.axis_index("tp"), lax.axis_index("fsdp")
    first_core, first_tp = core == 0, half == 0
    _, frames, width = layer_input.shape
    period = -(-frames // ROWS) * ROWS
    pad = lambda a: jnp.pad(a, ((0, period - frames), (0, 0)))
    shard = attend_weight.shape[0]
    cols = attend_weight.shape[2] // 2
    units = expand_weight.shape[1] // 2
    layout = (size // 2, shard) if quick else (1, width // 2)
    base = jnp.stack([half, at // 2, at % 2]).astype(jnp.int32)
    if not quick:
        base = jnp.zeros_like(base)

    small = jnp.concatenate(
        [low(shifts_weight).reshape(-1), low(offset_weight).reshape(-1), low(vectors_weight).reshape(-1)]
    )
    small = small.reshape(shard, -1)
    small_cols = small.shape[1]
    mine = lax.dynamic_slice_in_dim(low(attend_weight), core * cols, cols, 2)
    pack_one = jnp.concatenate(
        [mine[:, p, :LANES] for p in range(3)]
        + [mine[:, p, LANES:] for p in range(3)]
        + [small, jnp.zeros((shard, HD - small_cols), bfloat)],
        axis=1,
    )
    pieces = gather_quick(pack_one)
    core_next = after(core, pack_one)
    expand_mine = lax.dynamic_slice_in_dim(low(expand_weight), core_next * units, units, 1)
    reduce_mine = lax.dynamic_slice_in_dim(low(reduce_weight), core_next * units, units, 0).T
    output_mine = lax.dynamic_slice_in_dim(low(output_weight), core_next * cols, cols, 0).T
    pack_two = jnp.concatenate(
        [expand_mine, reduce_mine, output_mine, jnp.zeros((shard, HD), bfloat)], axis=1
    )
    all_two = lax.all_gather(pack_two, ("tp", "fsdp"), axis=0, tiled=True).reshape(2, width, -1)

    x_mine, g_mine = pad(take(layer_input, half)), pad(take(cotangent, half))
    x_other, g_other = swap_core(x_mine), swap_core(g_mine)

    n_shift, n_offset = shifts_weight.size, offset_weight.size
    n_other = n_shift + n_offset

    def table(places):
        out = []
        for n in places:
            halves = pieces[2 * n : 2 * n + 2] if quick else pieces[2 * n : 2 * n + 1]
            out += [p[:, :, 3 * cols : 3 * cols + small_cols].reshape(p.shape[0], -1) for p in halves]
        out = jnp.concatenate(out).reshape(len(places) // 2, 2, -1, small_cols * shard)
        if not quick:
            return out.reshape(-1, size, small_cols * shard)
        out = jnp.where(at % 2 == 0, out, out[:, ::-1])
        turn = lax.rem(size // 2 - at // 2, size // 2)
        out = lax.dynamic_slice_in_dim(jnp.concatenate([out, out], axis=2), turn, size // 2, 2)
        return out.transpose(0, 2, 1, 3).reshape(-1, size, small_cols * shard)

    vectors = table((0, 1))[0, :, n_other:].reshape((size,) + vectors_weight.shape)
    vectors = wide(vectors.transpose(1, 0, 2).reshape(-1, width))
    rest = table((0, 1, 2, 3))[:, :, :n_other]
    if quick:
        rest = jnp.where(first_tp, rest, rest[::-1])
    shifts = rest[:, :, :n_shift].reshape((2, size) + shifts_weight.shape)
    shifts = shifts.transpose(0, 2, 3, 1, 4).reshape(2, 2, 2, cols)
    shifts = wide(take(shifts, core, 2))
    blank = jnp.zeros((LANES,), single)
    bias = [[shifts[t, 0, :LANES], blank, shifts[t, 1, :LANES]] for t in range(2)]
    last = [shifts[0, 0, LANES:], shifts[1, 0, LANES:], blank, shifts[0, 1, LANES:], shifts[1, 1, LANES:]]
    bias = jnp.concatenate(bias[0] + bias[1] + last).reshape(1, -1)
    offset = rest[:, :, n_shift:].reshape((2, size) + offset_weight.shape)
    offset = offset.transpose(0, 2, 1, 3).reshape(2, 2, units)
    offset = wide(take(offset, core, 1)).reshape(1, 2 * units)

    qkv, normed_one, w_attend = project(base, x_mine, x_other, pieces, bias, vectors)
    attended, lse = attend(qkv, period, frames)
    branch, w_output = output_project(attended, all_two, 2 * units)
    hidden_one, normed_two, mixed_turned, mixed, mixed_away, back, act, du, grad_offset = feed_forward(
        x_mine, x_other, branch, swap_core(branch), g_mine, g_other, all_two, offset, vectors
    )

    back_other, mixed_other = swap_core(back), swap_core(mixed_away)
    keep_a, send_a = expand_grad(base, layout, after(normed_two, back, mixed), du)
    block, grad_hidden, branch_turned, grad_attended, sums = middle(
        back, back_other, hidden_one, g_mine, g_other, mixed, mixed_other, w_output, vectors
    )
    block_other = swap_tp(block)
    keep_b, send_b = reduce_grad(base, layout, mixed_turned, act, branch_turned, attended)
    step = lambda j, *gates: attend_back(
        j, after(qkv, *gates), attended, lse, grad_attended, period, frames
    )
    if quick:
        near_a, near_b = swap_near(send_a), swap_near(send_b)
        grad_0 = step(0, send_a, send_b, block)
        near_a = wide(after(near_a, grad_0)) + wide(keep_a)
        away_a = low(near_a[1])
        tp_a = swap_tp(away_a)
        block_other = after(block_other, grad_0)
        grad_1 = step(1, grad_0, away_a, block_other)
        keep_c, send_c = attend_grad(base, layout, normed_one, (grad_0, grad_1))
        near_c = swap_near(send_c)
        near_b = wide(after(near_b, grad_1)) + wide(keep_b)
        away_b = low(near_b[1])
        tp_b = swap_tp(away_b)
        part_a = near_a[0] + wide(after(tp_a, grad_1))
        part_a, far_a, got_a = fold(part_a, 2, 0)
        grad_2 = step(2, grad_1, send_c, away_b, far_a)
        part_a, far_a, got_a = fold(part_a + wide(after(got_a, grad_2)), 4, 0)
        part_b, far_b, got_b = fold(near_b[0] + wide(after(tp_b, grad_2)), 2, 0)
        part_c, far_c, got_c = fold(wide(after(near_c, grad_2)) + wide(keep_c), 2, 1)
        grad_2 = after(grad_2, far_a, far_b, far_c)
    else:
        grad_0, grad_1, grad_2 = step(0), step(1), step(2)
        total_a, total_b = scatter_any(keep_a, send_a), scatter_any(keep_b, send_b)
    part, part_away, shift_sums = project_back((grad_0, grad_1, grad_2), w_attend)
    part_other = swap_core(part_away)
    keep_d, send_d = attend_grad(base, layout, after(normed_one, part), (grad_2,))
    near_d = swap_near(send_d) if quick else send_d
    input_own, first_sums = first_back(part, part_other, x_mine, grad_hidden, vectors)
    input_other = swap_tp(input_own)
    def small_sums():
        vector_sums = jnp.concatenate([first_sums[:2], sums[2:6]]).reshape(-1)
        mine_sums = jnp.concatenate([shift_sums[0], grad_offset[0]])
        flat = jnp.concatenate([vector_sums, mine_sums]).reshape(-1, LANES)
        other = swap_core(flat).reshape(-1)
        other_vectors, other_sums = other[: vector_sums.size], other[vector_sums.size :]
        return jnp.concatenate(
            [
                vector_sums + other_vectors,
                jnp.where(first_core, mine_sums, other_sums),
                jnp.where(first_core, other_sums, mine_sums),
            ]
        ).reshape(-1, LANES)

    if quick:
        total_a = (part_a + wide(after(got_a, input_own)))[0]
        part_b, _, got_b = fold(part_b + wide(after(got_b, input_own)), 4, 0)
        part_c, _, got_c = fold(part_c + wide(after(got_c, input_own)), 4, 1)
        part_d = wide(after(near_d, input_own)) + wide(keep_d)
        flat, flat_got = small_sums(), None
        flat_got = swap_near(flat)
        part_d, far_d, got_d = fold(part_d, 2, 1)
        flat = flat + after(flat_got, far_d)
        flat_got = send_fsdp(flat, lambda i: i ^ 2)
        part_d, far_d, got_d = fold(part_d + wide(got_d), 4, 1)
        flat = flat + after(flat_got, far_d)
        flat_got = send_fsdp(flat, lambda i: i ^ 4)
        part_c = jnp.concatenate([part_c + wide(got_c), part_d + wide(got_d)], axis=3)[:, 0]
        away_c = low(after(part_c[1], input_other))
        tp_c = swap_tp(away_c)
        flat = flat + after(flat_got, away_c)
        flat = flat + swap_tp(flat)
        total_b = (part_b + wide(got_b))[0]
        total_c = part_c[0] + wide(tp_c)
    else:
        keep_c, send_c = attend_grad(base, layout, normed_one, (grad_0, grad_1))
        total_c = [scatter_any(keep_c, send_c), scatter_any(keep_d, send_d)]
        total_c = jnp.concatenate(total_c, axis=1)
        flat = sum_all(small_sums())

    flat = flat.reshape(-1)
    n_vectors = 6 * width
    total_vectors = take(flat[:n_vectors].reshape(6, size, -1), at, 1)
    slots = flat[n_vectors:].reshape(2, -1)
    slot_shift = slots[:, : PAIRS * TRIPLE].reshape(2, PAIRS, 3, LANES)[:, :, ::2]
    tail = jnp.where(first_tp, slot_shift[:, 2, :, :HD], slot_shift[:, 2, :, HD:])
    total_shifts = jnp.concatenate([take(slot_shift, half, 1), tail], axis=2)
    total_shifts = total_shifts.transpose(1, 0, 2).reshape(2, -1, size, HD // size)
    total_shifts = take(total_shifts, at, 2)
    total_offset = take(slots[:, PAIRS * TRIPLE :].reshape(2, 2, units), half, 1)
    total_offset = take(total_offset.reshape(-1, size, HD // size), at, 1)

    def both(mine, other, axis):
        return join(mine, other, first_core, axis)

    other_a, other_b, other_c = swap_core(total_a), swap_core(total_b), swap_core(total_c)
    total_expand = both(total_a, other_a, 1)
    total_reduce = both(total_b[:, :units], other_b[:, :units], 1).T
    total_output = both(total_b[:, units : units + cols], other_b[:, units : units + cols], 1).T

    def parts(total):
        rows = [
            jnp.concatenate(
                [
                    total[:, p * LANES : (p + 1) * LANES],
                    total[:, TRIPLE + p * HD : TRIPLE + (p + 1) * HD],
                ],
                axis=1,
            )
            for p in range(3)
        ]
        return jnp.stack(rows, axis=1)

    total_attend = both(parts(total_c), parts(other_c), 2)

    attend_new = adamw(
        attend_weight, total_attend, attend_moment, attend_square, rate_matrix, decay_matrix
    )
    shifts_new = adamw(shifts_weight, total_shifts, shifts_moment, shifts_square, rate_vector, 0.0)
    output_new = adamw(
        output_weight, total_output, output_moment, output_square, rate_matrix, decay_matrix
    )
    expand_new = adamw(
        expand_weight, total_expand, expand_moment, expand_square, rate_matrix, decay_matrix
    )
    offset_new = adamw(offset_weight, total_offset, offset_moment, offset_square, rate_vector, 0.0)
    reduce_new = adamw(
        reduce_weight, total_reduce, reduce_moment, reduce_square, rate_matrix, decay_matrix
    )
    vectors_new = adamw(
        vectors_weight, total_vectors, vectors_moment, vectors_square, rate_vector, 0.0
    )
    block_output = join(block[None, :frames], block_other[None, :frames], first_tp, 0)
    input_grad = assemble(half.astype(jnp.int32)[None], input_own, input_other, frames, single)
    return (
        block_output,
        input_grad,
        *attend_new,
        *shifts_new,
        *output_new,
        *expand_new,
        *offset_new,
        *reduce_new,
        *vectors_new,
    )


def solution(mesh):
    tokens = (P("fsdp", "ctx", None),) * 2
    params = (
        (P("fsdp", None, "tp"),) * 3
        + (P(None, "tp", "fsdp"),) * 3
        + (P("tp", "fsdp"),) * 3
        + (P("fsdp", "tp"),) * 3
        + (P("tp", "fsdp"),) * 3
        + (P("tp", "fsdp"),) * 3
        + (P(None, "fsdp"),) * 3
    )
    return jax.shard_map(
        local,
        mesh=mesh,
        in_specs=tokens + params,
        out_specs=tokens + params,
        check_vma=False,
    )
```

```python
import functools
import math

import jax
import jax.numpy as jnp
from jax import lax
from jax.experimental import pallas as pl
from jax.experimental.pallas import tpu as pltpu
from jax.sharding import PartitionSpec as P

HD = 64
STEP = 10


norm_eps = 1e-05
beta_first = 0.9
beta_second = 0.999
adam_eps = 1e-08
rate_matrix = 0.05
rate_vector = 0.5
decay_matrix = 0.01

bfloat = jnp.bfloat16
single = jnp.float32
LANES = 128
TRIPLE = 3 * LANES
PAIRS = 3
ROWS = 384
FEED_ROWS = 256
QUERY_ROWS = 768
KEY_ROWS = 512
SAFE_EXPONENT = 100.0
SWAP = [(0, 1), (1, 0)]
EXP_SCALE = HD ** (-0.5) * math.log2(math.e)
MASK = -1e30
VMEM = 56 * 1024 * 1024
NT = (((1,), (1,)), ((), ()))
TN = (((0,), (0,)), ((), ()))
PARAMS = pltpu.CompilerParams(vmem_limit_bytes=VMEM)


def dot(left, right, dims=(((1,), (0,)), ((), ()))):
    return lax.dot_general(left, right, dims, preferred_element_type=single)


def adamw(param, grad, moment, square, rate, decay):
    moment_new = beta_first * moment + (1.0 - beta_first) * grad
    square_new = beta_second * square + (1.0 - beta_second) * grad * grad
    corrected = moment_new / (1.0 - beta_first**STEP)
    normal_sq = square_new / (1.0 - beta_second**STEP)
    param_new = param - rate * (corrected / (jnp.sqrt(normal_sq) + adam_eps) + decay * param)
    return (param_new, moment_new, square_new)


def norm_parts(values):
    average = jnp.mean(values, axis=-1, keepdims=True)
    centered = values - average
    variance = jnp.mean(centered * centered, axis=-1, keepdims=True)
    inverse = lax.rsqrt(variance + norm_eps)
    return centered * inverse, inverse


def norm_back(grad, unit, inverse, gain):
    scaled = grad * gain
    first = jnp.mean(scaled, axis=-1, keepdims=True)
    second = jnp.mean(scaled * unit, axis=-1, keepdims=True)
    return (scaled - first - unit * second) * inverse


def column_sum(values):
    return jnp.sum(values, axis=0, keepdims=True)


def turned(value):
    return pltpu.roll(value, HD, 1)


def split_three(column):
    high = column.astype(bfloat).astype(single)
    rest = column - high
    middle = rest.astype(bfloat).astype(single)
    return high, middle, (rest - middle).astype(bfloat).astype(single)


def beside(values, half, extras):
    lane = lax.broadcasted_iota(jnp.int32, values.shape, 1)
    base = HD * (1 - half)
    mine = (lane >= HD) if half else (lane < HD)
    out = jnp.where(mine, values, 0.0)
    for place, extra in enumerate(extras):
        out = jnp.where(lane == base + place, extra, out)
    return out.astype(bfloat)


def pad_column(first_row, rows, period, valid):
    row = first_row + lax.broadcasted_iota(jnp.int32, (rows, 1), 0)
    return jnp.where(row % period < valid, 0.0, MASK)


def whole(shape):
    return pl.BlockSpec(shape, lambda *_: (0,) * len(shape))


def struct(shape, dtype):
    return jax.ShapeDtypeStruct(shape, dtype)


def cost(flops, bytes_accessed, transcendentals=0):
    share = 32
    return pl.CostEstimate(
        flops=int(flops) // share,
        bytes_accessed=int(bytes_accessed) // share,
        transcendentals=int(transcendentals) // share,
    )


def project_kernel(base, x_ref, o_ref, *refs):
    pieces, (bias_ref, vec_ref, qkv_ref, nt_ref, w_ref) = refs[:8], refs[8:]
    step = pl.program_id(0)
    cut, rows, _ = pieces[0].shape
    far = vec_ref.shape[1] // (2 * rows)

    @pl.when(step == 0)
    def _():
        flip = base[2] == 1
        swap = base[0] == 1
        lane = lax.broadcasted_iota(jnp.int32, (rows, LANES), 1)
        for z in range(far):
            at = lax.rem(z - base[1] + far, far)
            inner = lax.rem(at, cut)
            read = lambda n: jnp.where(at < cut, pieces[2 * n][inner], pieces[2 * n + 1][inner])
            own, near, away, across = (read(n) for n in range(4))
            for x in range(2):
                here = jnp.where(flip, own, near) if x else jnp.where(flip, near, own)
                there = jnp.where(flip, away, across) if x else jnp.where(flip, across, away)
                both = (jnp.where(swap, there, here), jnp.where(swap, here, there))
                place = slice((2 * z + x) * rows, (2 * z + x + 1) * rows)
                w_ref[0, place, :] = both[0][:, :TRIPLE]
                w_ref[1, place, :] = both[1][:, :TRIPLE]
                mixed = [b[:, TRIPLE : TRIPLE + LANES].astype(single) for b in both]
                last = [b[:, TRIPLE + LANES :].astype(single) for b in both]
                q = jnp.where(lane < HD, mixed[0], turned(mixed[1]))
                k = jnp.where(lane < HD, turned(mixed[0]), mixed[1])
                v = jnp.where(lane < HD, last[0], turned(last[1]))
                for part, value in enumerate((q, k, v)):
                    w_ref[2, place, part * LANES : (part + 1) * LANES] = value.astype(bfloat)

    x = jnp.where(step < pl.num_programs(0) // 2, x_ref[...], o_ref[...]).astype(single)
    unit, _ = norm_parts(x)
    normed = unit * vec_ref[0:1, :] + vec_ref[1:2, :]
    nt_ref[...] = normed.astype(bfloat).T
    normed = normed.astype(bfloat)
    for j in range(PAIRS):
        cols = slice(j * TRIPLE, (j + 1) * TRIPLE)
        qkv_ref[:, cols] = (dot(normed, w_ref[j]) + bias_ref[:, cols]).astype(bfloat)


def own_block(blocks):
    return lambda i, *_: (jnp.minimum(i, blocks - 1), 0)


def other_block(blocks):
    return lambda i, *_: (jnp.maximum(i - blocks, 0), 0)


def project(base, x_mine, x_other, pieces, bias, vectors):
    period, width = x_mine.shape
    blocks = period // ROWS
    rows = 2 * period
    out = PAIRS * TRIPLE
    return pl.pallas_call(
        project_kernel,
        grid_spec=pltpu.PrefetchScalarGridSpec(
            num_scalar_prefetch=1,
            grid=(2 * blocks,),
            in_specs=[
                pl.BlockSpec((ROWS, width), own_block(blocks)),
                pl.BlockSpec((ROWS, width), other_block(blocks)),
                *[whole(p.shape) for p in pieces],
                whole(bias.shape),
                whole(vectors.shape),
            ],
            out_specs=[
                pl.BlockSpec((ROWS, out), lambda i, *_: (i, 0)),
                pl.BlockSpec((width, ROWS), lambda i, *_: (0, i)),
                whole((PAIRS, width, TRIPLE)),
            ],
        ),
        out_shape=[
            struct((rows, out), bfloat),
            struct((width, rows), bfloat),
            struct((PAIRS, width, TRIPLE), bfloat),
        ],
        compiler_params=PARAMS,
        cost_estimate=cost(2 * rows * width * out, 2 * rows * (2 * width + out) + 4 * width * out),
        name="project",
    )(base, x_mine, x_other, *pieces, bias, vectors)


def attend_kernel(period, valid, q_ref, k_ref, v_ref, o_ref, lse_ref, keys, values, longest):
    def norms(value):
        square = value * value
        lane = lax.broadcasted_iota(jnp.int32, value.shape, 1)
        sums = [jnp.sum(jnp.where(mine, square, 0.0), axis=1) for mine in (lane < HD, lane >= HD)]
        return jnp.maximum(jnp.max(sums[0]), jnp.max(sums[1]))

    @pl.when(pl.program_id(1) == 0)
    def _():
        k = k_ref[...].astype(single)
        v = v_ref[...].astype(single)
        pad = pad_column(0, k.shape[0], period, valid)
        for half in range(2):
            keys[half] = beside(k, half, (pad,))
            values[half] = beside(v, half, (1.0,)).T
        longest[0] = norms(k)

    q = q_ref[...].astype(single)
    bound = norms(q) * longest[0] * (EXP_SCALE * EXP_SCALE)
    safe = bound < SAFE_EXPONENT * SAFE_EXPONENT

    def run(shift):
        outs, tops = [], []
        for half in range(2):
            scores = dot(keys[half], beside(q, half, (1.0,)), NT)
            if shift:
                top = jnp.max(scores, axis=0, keepdims=True)
                scores = scores - top
            raised = jnp.exp2(scores * EXP_SCALE)
            both = dot(values[half], raised.astype(bfloat))
            base = HD * (1 - half)
            total = both[base : base + 1, :]
            outs.append(both / total)
            low = jnp.log2(total) / EXP_SCALE
            tops.append(top + low if shift else low)
        row = lax.broadcasted_iota(jnp.int32, outs[0].shape, 0)
        o_ref[...] = jnp.where(row < HD, outs[0], outs[1]).T.astype(bfloat)
        lse_ref[...] = jnp.where(row < HD, tops[0], tops[1]).T

    @pl.when(safe)
    def _():
        run(False)

    @pl.when(jnp.logical_not(safe))
    def _():
        run(True)


def attend(qkv, period, valid):
    rows = qkv.shape[0]
    width = PAIRS * LANES
    part = lambda at: pl.BlockSpec((rows, LANES), lambda j, i: (0, 3 * j + at))
    block = pl.BlockSpec((QUERY_ROWS, LANES), lambda j, i: (i, j))
    return pl.pallas_call(
        functools.partial(attend_kernel, period, valid),
        grid=(PAIRS, rows // QUERY_ROWS),
        in_specs=[pl.BlockSpec((QUERY_ROWS, LANES), lambda j, i: (i, 3 * j)), part(1), part(2)],
        out_specs=[block, block],
        out_shape=[struct((rows, width), bfloat), struct((rows, width), single)],
        scratch_shapes=[
            pltpu.VMEM((2, rows, LANES), bfloat),
            pltpu.VMEM((2, LANES, rows), bfloat),
            pltpu.SMEM((1,), single),
        ],
        compiler_params=PARAMS,
        cost_estimate=cost(16 * rows * rows * LANES * PAIRS, 20 * rows * width, 2 * PAIRS * rows * rows),
        name="attend",
    )(qkv, qkv, qkv)


def attend_back_kernel(
    period, valid, q_ref, k_ref, v_ref, o_ref, lse_ref, g_ref,
    out_ref, queries, queries_turned, grads, grads_turned, total,
):
    step = pl.program_id(0)
    lane_all = lax.broadcasted_iota(jnp.int32, q_ref.shape, 1)

    @pl.when(step == 0)
    def _():
        q = q_ref[...].astype(single)
        g = g_ref[...].astype(single)
        product = g * o_ref[...].astype(single)
        for half in range(2):
            mine = (lane_all >= HD) if half else (lane_all < HD)
            inner = jnp.sum(jnp.where(mine, product, 0.0), axis=1, keepdims=True)
            low = jnp.max(jnp.where(mine, lse_ref[...], -jnp.inf), axis=1, keepdims=True)
            queries[half] = beside(q, half, (1.0,) + split_three(-low))
            grads[half] = beside(g, half, (0.0,) + split_three(-inner))
            queries_turned[half] = queries[half].T
            grads_turned[half] = grads[half].T
        total[...] = jnp.zeros_like(total)

    k = k_ref[...].astype(single)
    v = v_ref[...].astype(single)
    pad = pad_column(step * k.shape[0], k.shape[0], period, valid)
    dks, dvs, dqs = [], [], []
    for half in range(2):
        keys = beside(k, half, (pad, 1.0, 1.0, 1.0))
        values = beside(v, half, (1.0, 1.0, 1.0, 1.0))
        weights = jnp.exp2(dot(queries[half], keys, NT) * EXP_SCALE)
        inner = weights * dot(grads[half], values, NT)
        dvs.append(dot(grads_turned[half], weights.astype(bfloat)))
        low = inner.astype(bfloat)
        dks.append(dot(queries_turned[half], low))
        dqs.append(dot(low, keys))
    scale = HD ** (-0.5)
    here = pl.ds(pl.multiple_of(step * KEY_ROWS, KEY_ROWS), KEY_ROWS)
    row = lax.broadcasted_iota(jnp.int32, dks[0].shape, 0)
    dk = jnp.where(row < HD, dks[0], dks[1]) * scale
    out_ref[here, LANES : 2 * LANES] = dk.T.astype(bfloat)
    out_ref[here, 2 * LANES :] = jnp.where(row < HD, dvs[0], dvs[1]).T.astype(bfloat)
    total[...] += jnp.where(lane_all < HD, dqs[0], dqs[1])

    @pl.when(step == pl.num_programs(0) - 1)
    def _():
        out_ref[:, :LANES] = (total[...] * scale).astype(bfloat)


def attend_back(j, qkv, o, lse, grad, period, valid):
    rows = qkv.shape[0]
    column = lambda at: pl.BlockSpec((rows, LANES), lambda i: (0, at))
    block = lambda at: pl.BlockSpec((KEY_ROWS, LANES), lambda i: (i, at))
    return pl.pallas_call(
        functools.partial(attend_back_kernel, period, valid),
        grid=(rows // KEY_ROWS,),
        in_specs=[column(3 * j), block(3 * j + 1), block(3 * j + 2), column(j), column(j), column(j)],
        out_specs=whole((rows, TRIPLE)),
        out_shape=struct((rows, TRIPLE), bfloat),
        scratch_shapes=[
            pltpu.VMEM((2, rows, LANES), bfloat),
            pltpu.VMEM((2, LANES, rows), bfloat),
            pltpu.VMEM((2, rows, LANES), bfloat),
            pltpu.VMEM((2, LANES, rows), bfloat),
            pltpu.VMEM((rows, LANES), single),
        ],
        compiler_params=PARAMS,
        cost_estimate=cost(40 * rows * rows * LANES, 20 * rows * LANES, 2 * rows * rows),
        name=f"attend_back_{j}",
    )(qkv, qkv, qkv, o, lse, grad)


def output_kernel(o_ref, w_ref, out_ref, full_ref):
    @pl.when(pl.program_id(0) == 0)
    def _():
        lane = lax.broadcasted_iota(jnp.int32, (w_ref.shape[1], LANES), 1)
        full_ref[:, :LANES] = w_ref[0, :, :LANES]
        full_ref[:, LANES : 2 * LANES] = w_ref[1, :, :LANES]
        last = [w_ref[t, :, LANES:].astype(single) for t in range(2)]
        full_ref[:, 2 * LANES :] = jnp.where(lane < HD, last[0], turned(last[1])).astype(bfloat)

    out_ref[...] = dot(o_ref[...], full_ref[...], NT).astype(bfloat)


def output_project(o, weights, place):
    rows, width = o.shape[0], weights.shape[1]
    columns = o.shape[1]
    return pl.pallas_call(
        output_kernel,
        grid=(rows // ROWS,),
        in_specs=[
            pl.BlockSpec((ROWS, columns), lambda i: (i, 0)),
            pl.BlockSpec((2, width, 2 * LANES), lambda i: (0, 0, place // (2 * LANES))),
        ],
        out_specs=[pl.BlockSpec((ROWS, width), lambda i: (i, 0)), whole((width, columns))],
        out_shape=[struct((rows, width), bfloat), struct((width, columns), bfloat)],
        compiler_params=PARAMS,
        cost_estimate=cost(2 * rows * width * columns, 2 * rows * (width + columns)),
        name="output_project",
    )(o, weights)


def feed_kernel(
    x_ref, xo_ref, p_ref, po_ref, g_ref, go_ref, w1_ref, w2_ref, b_ref, vec_ref,
    h_ref, nt_ref, gt_ref, y_ref, yo_ref, dn_ref, act_ref, du_ref, db_ref,
):
    step = pl.program_id(0)
    mine = step < pl.num_programs(0) // 2
    x = jnp.where(mine, x_ref[...], xo_ref[...]).astype(single)
    grad = jnp.where(mine, g_ref[...], go_ref[...])
    hidden = x + (p_ref[...].astype(single) + po_ref[...].astype(single)) + vec_ref[2:3, :]
    h_ref[...] = hidden
    unit, _ = norm_parts(hidden)
    normed = unit * vec_ref[3:4, :] + vec_ref[4:5, :]
    nt_ref[...] = normed.astype(bfloat).T
    gt_ref[...] = grad.T
    normed = normed.astype(bfloat)
    count, _, units = w1_ref.shape
    mixed = back = 0.0

    @pl.when(step == 0)
    def _():
        db_ref[...] = jnp.zeros_like(db_ref)

    for part in range(count):
        cols = slice(part * units, (part + 1) * units)
        u = dot(normed, w1_ref[part]) + b_ref[:, cols]
        phi = 0.5 * (1.0 + lax.erf(u * (0.5**0.5)))
        act = (u * phi).astype(bfloat)
        slope = phi + u * (jnp.exp(-0.5 * u * u) * ((2.0 * math.pi) ** -0.5))
        du = (dot(grad, w2_ref[part]) * slope).astype(bfloat)
        act_ref[:, cols] = act
        du_ref[:, cols] = du
        db_ref[:, cols] += column_sum(du.astype(single))
        mixed = mixed + dot(act, w2_ref[part], NT)
        back = back + dot(du, w1_ref[part], NT)
    dn_ref[...] = back.astype(bfloat)

    @pl.when(mine)
    def _():
        y_ref[...] = mixed.astype(bfloat)

    @pl.when(jnp.logical_not(mine))
    def _():
        yo_ref[...] = mixed.astype(bfloat)


def feed_forward(x_mine, x_other, part, part_other, g_mine, g_other, weights, bias, vectors):
    rows, width = part.shape
    blocks = rows // FEED_ROWS // 2
    count, hidden = weights.shape[0], bias.shape[1]
    units = hidden // count
    tokens = pl.BlockSpec((FEED_ROWS, width), lambda i: (i, 0))
    crossed = pl.BlockSpec((FEED_ROWS, width), lambda i: ((i + blocks) % (2 * blocks), 0))
    wide = pl.BlockSpec((FEED_ROWS, hidden), lambda i: (i, 0))
    tall = pl.BlockSpec((width, FEED_ROWS), lambda i: (0, i))
    own = pl.BlockSpec((FEED_ROWS, width), own_block(blocks))
    other = pl.BlockSpec((FEED_ROWS, width), other_block(blocks))
    weight = lambda at: pl.BlockSpec((count, width, units), lambda i: (0, 0, at))
    return pl.pallas_call(
        feed_kernel,
        grid=(2 * blocks,),
        in_specs=[
            own, other, tokens, crossed, own, other, weight(0), weight(1),
            whole(bias.shape), whole(vectors.shape),
        ],
        out_specs=[tokens, tall, tall, own, other, tokens, wide, wide, whole((1, hidden))],
        out_shape=[
            struct((rows, width), single),
            struct((width, rows), bfloat),
            struct((width, rows), bfloat),
            struct((rows // 2, width), bfloat),
            struct((rows // 2, width), bfloat),
            struct((rows, width), bfloat),
            struct((rows, hidden), bfloat),
            struct((rows, hidden), bfloat),
            struct((1, hidden), single),
        ],
        compiler_params=PARAMS,
        cost_estimate=cost(
            8 * rows * width * hidden,
            18 * rows * width + 4 * rows * hidden + 4 * width * hidden,
            2 * rows * hidden,
        ),
        name="feed_forward",
    )(x_mine, x_other, part, part_other, g_mine, g_other, weights, weights, bias, vectors)


def put(base, keep_ref, send_ref, t, value, cols):
    far, rows = keep_ref.shape[1], keep_ref.shape[2]
    first = base[2] == 0
    for z in range(far):
        at = jnp.bitwise_xor(z, base[1])
        lo = value[2 * z * rows : (2 * z + 1) * rows].astype(bfloat)
        hi = value[(2 * z + 1) * rows : (2 * z + 2) * rows].astype(bfloat)
        keep_ref[t, at, :, cols] = jnp.where(first, lo, hi)
        send_ref[t, at, :, cols] = jnp.where(first, hi, lo)


def expand_grad_kernel(base, left_ref, right_ref, keep_ref, send_ref):
    put(base, keep_ref, send_ref, 0, dot(left_ref[...], right_ref[...]), slice(None))


def expand_grad(base, layout, left, right):
    width, rows = left.shape
    units = right.shape[1] // 2
    shape = (2,) + layout + (units,)
    out = pl.BlockSpec((1,) + layout + (units,), lambda t, base: (t, 0, 0, 0))
    return pl.pallas_call(
        expand_grad_kernel,
        grid_spec=pltpu.PrefetchScalarGridSpec(
            num_scalar_prefetch=1,
            grid=(2,),
            in_specs=[
                whole(left.shape),
                pl.BlockSpec((rows, units), lambda t, base: (0, (t + base[0]) % 2)),
            ],
            out_specs=[out, out],
        ),
        out_shape=[struct(shape, bfloat)] * 2,
        compiler_params=PARAMS,
        cost_estimate=cost(4 * rows * width * units, 2 * rows * (width + 2 * units) + 4 * width * units),
        name="expand_grad",
    )(base, left, right)


def reduce_grad_kernel(base, left_ref, right_ref, branch_ref, o_ref, keep_ref, send_ref):
    at = lax.rem(pl.program_id(0) + base[0], 2)
    units = right_ref.shape[1]
    put(base, keep_ref, send_ref, 0, dot(left_ref[...], right_ref[...]), slice(0, units))
    mine = dot(branch_ref[...], o_ref[:, pl.ds(pl.multiple_of(at * LANES, LANES), LANES)])
    put(base, keep_ref, send_ref, 0, mine, slice(units, units + LANES))
    mixed = dot(branch_ref[...], o_ref[:, 2 * LANES :])
    mixed = jnp.where(at == 0, mixed, turned(mixed))
    put(base, keep_ref, send_ref, 0, mixed, slice(units + LANES, units + 2 * LANES))


def reduce_grad(base, layout, left, right, branch, o):
    width, rows = left.shape
    units = right.shape[1] // 2
    total = units + 2 * LANES
    shape = (2,) + layout + (total,)
    out = pl.BlockSpec((1,) + layout + (total,), lambda t, base: (t, 0, 0, 0))
    return pl.pallas_call(
        reduce_grad_kernel,
        grid_spec=pltpu.PrefetchScalarGridSpec(
            num_scalar_prefetch=1,
            grid=(2,),
            in_specs=[
                whole(left.shape),
                pl.BlockSpec((rows, units), lambda t, base: (0, (t + base[0]) % 2)),
                whole(branch.shape),
                whole(o.shape),
            ],
            out_specs=[out, out],
        ),
        out_shape=[struct(shape, bfloat)] * 2,
        compiler_params=PARAMS,
        cost_estimate=cost(4 * rows * width * total, 2 * rows * (2 * width + 2 * total) + 4 * width * total),
        name="reduce_grad",
    )(base, left, right, branch, o)


def pair_grad_kernel(base, left_ref, a_ref, b_ref, keep_ref, send_ref):
    left = left_ref[...]
    pairs = [dot(left, ref[...]) for ref in (a_ref, b_ref)]
    same = base[0] == 0
    for t in range(2):
        put(base, keep_ref, send_ref, t, jnp.where(same, pairs[t], pairs[1 - t]), slice(0, TRIPLE))


def mixed_grad_kernel(base, left_ref, ref, keep_ref, send_ref):
    full = dot(left_ref[...], ref[...])
    q, k, v = (full[:, part * LANES : (part + 1) * LANES] for part in range(3))
    lane = lax.broadcasted_iota(jnp.int32, q.shape, 1)
    mixed = [
        (jnp.where(lane < HD, q, turned(k)), v),
        (jnp.where(lane < HD, turned(q), k), turned(v)),
    ]
    same = base[0] == 0
    for t in range(2):
        for place in range(2):
            cols = slice(place * LANES, (place + 1) * LANES)
            value = jnp.where(same, mixed[t][place], mixed[1 - t][place])
            put(base, keep_ref, send_ref, t, value, cols)


def attend_grad(base, layout, left, grads):
    width, rows = left.shape
    count = len(grads)
    columns = TRIPLE if count == 2 else 2 * LANES
    shape = (2,) + layout + (columns,)
    return pl.pallas_call(
        pair_grad_kernel if count == 2 else mixed_grad_kernel,
        grid_spec=pltpu.PrefetchScalarGridSpec(
            num_scalar_prefetch=1,
            grid=(1,),
            in_specs=[whole(left.shape)] + [whole(g.shape) for g in grads],
            out_specs=[whole(shape)] * 2,
        ),
        out_shape=[struct(shape, bfloat)] * 2,
        compiler_params=PARAMS,
        cost_estimate=cost(
            2 * count * rows * width * TRIPLE, 2 * rows * (width + count * TRIPLE) + 8 * width * columns
        ),
        name=f"attend_grad_{count}",
    )(base, left, *grads)


def middle_kernel(
    p_ref, po_ref, h_ref, g_ref, go_ref, y_ref, yo_ref, w_ref, vec_ref,
    out_ref, dh_ref, bt_ref, do_ref, sums_ref,
):
    step = pl.program_id(0)
    mine = step < pl.num_programs(0) // 2
    grad = jnp.where(mine, g_ref[...], go_ref[...]).astype(single)
    hidden = h_ref[...]
    unit, inverse = norm_parts(hidden)
    normed = p_ref[...].astype(single) + po_ref[...].astype(single)
    after = grad + norm_back(normed, unit, inverse, vec_ref[3:4, :])
    bt_ref[...] = after.astype(bfloat).T
    branch = after.astype(bfloat)
    do_ref[...] = dot(branch, w_ref[...]).astype(bfloat)

    @pl.when(step == 0)
    def _():
        sums_ref[...] = jnp.zeros_like(sums_ref)

    @pl.when(mine)
    def _():
        dh_ref[...] = after
        mixed = y_ref[...].astype(single) + yo_ref[...].astype(single)
        out_ref[...] = (hidden + mixed + vec_ref[5:6, :]).astype(bfloat)
        sums_ref[2:3, :] += column_sum(branch.astype(single))
        sums_ref[3:4, :] += column_sum(normed * unit)
        sums_ref[4:5, :] += column_sum(normed)
        sums_ref[5:6, :] += column_sum(grad)


def middle(part, part_other, hidden, g_mine, g_other, mixed, mixed_other, weight, vectors):
    rows, width = part.shape
    blocks = rows // ROWS // 2
    tokens = pl.BlockSpec((ROWS, width), lambda i: (i, 0))
    crossed = pl.BlockSpec((ROWS, width), lambda i: ((i + blocks) % (2 * blocks), 0))
    own = pl.BlockSpec((ROWS, width), own_block(blocks))
    other = pl.BlockSpec((ROWS, width), other_block(blocks))
    columns = weight.shape[1]
    return pl.pallas_call(
        middle_kernel,
        grid=(2 * blocks,),
        in_specs=[
            tokens, crossed, tokens, own, other, own, own, whole(weight.shape), whole(vectors.shape)
        ],
        out_specs=[
            own,
            own,
            pl.BlockSpec((width, ROWS), lambda i: (0, i)),
            pl.BlockSpec((ROWS, columns), lambda i: (i, 0)),
            whole((8, width)),
        ],
        out_shape=[
            struct((rows // 2, width), bfloat),
            struct((rows // 2, width), single),
            struct((width, rows), bfloat),
            struct((rows, columns), bfloat),
            struct((8, width), single),
        ],
        compiler_params=PARAMS,
        cost_estimate=cost(2 * rows * width * columns, 16 * rows * width),
        name="middle",
    )(part, part_other, hidden, g_mine, g_other, mixed, mixed_other, weight, vectors)


def project_back_kernel(a_ref, b_ref, c_ref, w_ref, out_ref, other_ref, sums_ref):
    @pl.when(pl.program_id(0) == 0)
    def _():
        sums_ref[...] = jnp.zeros_like(sums_ref)

    total = 0.0
    for j, ref in enumerate((a_ref, b_ref, c_ref)):
        grad = ref[...]
        total = total + dot(grad, w_ref[j], NT)
        cols = slice(j * TRIPLE, (j + 1) * TRIPLE)
        sums_ref[:, cols] += column_sum(grad.astype(single))
    mine = pl.program_id(0) < pl.num_programs(0) // 2

    @pl.when(mine)
    def _():
        out_ref[...] = total.astype(bfloat)

    @pl.when(jnp.logical_not(mine))
    def _():
        other_ref[...] = total.astype(bfloat)


def project_back(grads, weight):
    rows = grads[0].shape[0]
    width = weight.shape[1]
    block = pl.BlockSpec((ROWS, TRIPLE), lambda i: (i, 0))
    return pl.pallas_call(
        project_back_kernel,
        grid=(rows // ROWS,),
        in_specs=[block, block, block, whole(weight.shape)],
        out_specs=[
            pl.BlockSpec((ROWS, width), own_block(rows // ROWS // 2)),
            pl.BlockSpec((ROWS, width), other_block(rows // ROWS // 2)),
            whole((1, PAIRS * TRIPLE)),
        ],
        out_shape=[struct((rows // 2, width), bfloat)] * 2 + [struct((1, PAIRS * TRIPLE), single)],
        compiler_params=PARAMS,
        cost_estimate=cost(6 * rows * width * TRIPLE, 2 * rows * (width + 3 * TRIPLE)),
        name="project_back",
    )(*grads, weight)


def first_back_kernel(p_ref, po_ref, x_ref, dh_ref, vec_ref, out_ref, sums_ref):
    @pl.when(pl.program_id(0) == 0)
    def _():
        sums_ref[...] = jnp.zeros_like(sums_ref)

    unit, inverse = norm_parts(x_ref[...].astype(single))
    normed = p_ref[...].astype(single) + po_ref[...].astype(single)
    out_ref[...] = (dh_ref[...] + norm_back(normed, unit, inverse, vec_ref[0:1, :])).astype(bfloat)
    sums_ref[0:1, :] += column_sum(normed * unit)
    sums_ref[1:2, :] += column_sum(normed)


def first_back(part, part_other, x_mine, grad_hidden, vectors):
    rows, width = x_mine.shape
    tokens = pl.BlockSpec((ROWS, width), lambda i: (i, 0))
    return pl.pallas_call(
        first_back_kernel,
        grid=(rows // ROWS,),
        in_specs=[tokens, tokens, tokens, tokens, whole(vectors.shape)],
        out_specs=[tokens, whole((8, width))],
        out_shape=[struct((rows, width), bfloat), struct((8, width), single)],
        compiler_params=PARAMS,
        cost_estimate=cost(20 * rows * width, 12 * rows * width),
        name="first_back",
    )(part, part_other, x_mine, grad_hidden, vectors)


def assemble_kernel(place, mine_ref, other_ref, out_ref):
    first = place[0] == 0
    frames = out_ref.shape[0]
    mine, other = mine_ref[...].astype(single), other_ref[...].astype(single)
    out_ref[:, 0, :] = jnp.where(first, mine, other)[:frames].astype(out_ref.dtype)
    out_ref[:, 1, :] = jnp.where(first, other, mine)[:frames].astype(out_ref.dtype)


def assemble(place, mine, other, frames, dtype):
    rows, width = mine.shape
    out = pl.pallas_call(
        assemble_kernel,
        grid_spec=pltpu.PrefetchScalarGridSpec(
            num_scalar_prefetch=1,
            grid=(2,),
            in_specs=[pl.BlockSpec((rows, width // 2), lambda i, place: (0, i))] * 2,
            out_specs=pl.BlockSpec((frames, 2, width // 2), lambda i, place: (0, 0, i)),
        ),
        out_shape=struct((frames, 2, width), dtype),
        compiler_params=PARAMS,
        cost_estimate=cost(0, 12 * rows * width),
        name="assemble",
    )(place, mine, other)
    return out.transpose(1, 0, 2)


def swap_core(value):
    return lax.ppermute(value, "ctx", SWAP)


def swap_tp(value):
    return lax.ppermute(value, "tp", SWAP)


def send_fsdp(value, target):
    size = lax.axis_size("fsdp")
    return lax.ppermute(value, "fsdp", [(i, target(i) % size) for i in range(size)])


def swap_near(value):
    return send_fsdp(value, lambda i: i ^ 1)


def after(value, *others):
    return lax.optimization_barrier((value,) + others)[0]


def wide(value):
    return value.astype(single)


def low(value):
    return value.astype(bfloat)


def join(mine, other, first, axis):
    return jnp.concatenate([jnp.where(first, mine, other), jnp.where(first, other, mine)], axis=axis)


def take(value, index, axis=0):
    return lax.dynamic_index_in_dim(value, index, axis, keepdims=False)


def gather_quick(shard):
    size = lax.axis_size("fsdp")
    far = size // 2
    if size != 8:
        full = lax.all_gather(shard, ("tp", "fsdp"), axis=0, tiled=True)
        return [p[None] for p in jnp.split(full, 4) for _ in range(2)]
    steps = [send_fsdp(shard, lambda i, k=k: i + 2 * k) for k in range(1, far)]
    own = [shard] + steps[::-1]
    cut = far // 2
    lo, hi = jnp.stack(own[:cut]), jnp.stack(own[cut:])
    near_lo, away_lo, away_hi, near_hi = swap_near(lo), swap_tp(lo), swap_tp(hi), swap_near(hi)
    return [lo, hi, near_lo, near_hi, away_lo, away_hi, swap_near(away_lo), swap_tp(near_hi)]


def fold(value, stride, axis):
    shape = value.shape
    halves = value.reshape(shape[:axis] + (shape[axis] // 2, 2) + shape[axis + 1 :])
    away = low(lax.index_in_dim(halves, 1, axis + 1, keepdims=False))
    return lax.index_in_dim(halves, 0, axis + 1, keepdims=False), away, send_fsdp(away, lambda i: i ^ stride)


def sum_all(value):
    stride = 2
    while stride < lax.axis_size("fsdp"):
        value = value + send_fsdp(value, lambda i: i ^ stride)
        stride *= 2
    value = value + swap_near(value)
    return value + swap_tp(value)


def scatter_any(keep, send):
    full = wide(jnp.concatenate([keep, send], axis=2)[:, 0])
    full = lax.psum_scatter(full, "tp", scatter_dimension=0, tiled=True)
    return lax.psum_scatter(full, "fsdp", scatter_dimension=1, tiled=True)[0]


def local(
    layer_input,
    cotangent,
    attend_weight,
    attend_moment,
    attend_square,
    shifts_weight,
    shifts_moment,
    shifts_square,
    output_weight,
    output_moment,
    output_square,
    expand_weight,
    expand_moment,
    expand_square,
    offset_weight,
    offset_moment,
    offset_square,
    reduce_weight,
    reduce_moment,
    reduce_square,
    vectors_weight,
    vectors_moment,
    vectors_square,
):
    size = lax.axis_size("fsdp")
    quick = size == 8
    core, half, at = lax.axis_index("ctx"), lax.axis_index("tp"), lax.axis_index("fsdp")
    first_core, first_tp = core == 0, half == 0
    _, frames, width = layer_input.shape
    period = -(-frames // ROWS) * ROWS
    pad = lambda a: jnp.pad(a, ((0, period - frames), (0, 0)))
    shard = attend_weight.shape[0]
    cols = attend_weight.shape[2] // 2
    units = expand_weight.shape[1] // 2
    layout = (size // 2, shard) if quick else (1, width // 2)
    base = jnp.stack([half, at // 2, at % 2]).astype(jnp.int32)
    if not quick:
        base = jnp.zeros_like(base)

    small = jnp.concatenate(
        [low(shifts_weight).reshape(-1), low(offset_weight).reshape(-1), low(vectors_weight).reshape(-1)]
    )
    small = small.reshape(shard, -1)
    small_cols = small.shape[1]
    mine = lax.dynamic_slice_in_dim(low(attend_weight), core * cols, cols, 2)
    pack_one = jnp.concatenate(
        [mine[:, p, :LANES] for p in range(3)]
        + [mine[:, p, LANES:] for p in range(3)]
        + [small, jnp.zeros((shard, HD - small_cols), bfloat)],
        axis=1,
    )
    pieces = gather_quick(pack_one)
    core_next = after(core, pack_one)
    expand_mine = lax.dynamic_slice_in_dim(low(expand_weight), core_next * units, units, 1)
    reduce_mine = lax.dynamic_slice_in_dim(low(reduce_weight), core_next * units, units, 0).T
    output_mine = lax.dynamic_slice_in_dim(low(output_weight), core_next * cols, cols, 0).T
    pack_two = jnp.concatenate(
        [expand_mine, reduce_mine, output_mine, jnp.zeros((shard, HD), bfloat)], axis=1
    )
    all_two = lax.all_gather(pack_two, ("tp", "fsdp"), axis=0, tiled=True).reshape(2, width, -1)

    x_mine, g_mine = pad(take(layer_input, half)), pad(take(cotangent, half))
    x_other, g_other = swap_core(x_mine), swap_core(g_mine)

    n_shift, n_offset = shifts_weight.size, offset_weight.size
    n_other = n_shift + n_offset

    def table(places):
        out = []
        for n in places:
            halves = pieces[2 * n : 2 * n + 2] if quick else pieces[2 * n : 2 * n + 1]
            out += [p[:, :, 3 * cols : 3 * cols + small_cols].reshape(p.shape[0], -1) for p in halves]
        out = jnp.concatenate(out).reshape(len(places) // 2, 2, -1, small_cols * shard)
        if not quick:
            return out.reshape(-1, size, small_cols * shard)
        out = jnp.where(at % 2 == 0, out, out[:, ::-1])
        turn = lax.rem(size // 2 - at // 2, size // 2)
        out = lax.dynamic_slice_in_dim(jnp.concatenate([out, out], axis=2), turn, size // 2, 2)
        return out.transpose(0, 2, 1, 3).reshape(-1, size, small_cols * shard)

    vectors = table((0, 1))[0, :, n_other:].reshape((size,) + vectors_weight.shape)
    vectors = wide(vectors.transpose(1, 0, 2).reshape(-1, width))
    rest = table((0, 1, 2, 3))[:, :, :n_other]
    if quick:
        rest = jnp.where(first_tp, rest, rest[::-1])
    shifts = rest[:, :, :n_shift].reshape((2, size) + shifts_weight.shape)
    shifts = shifts.transpose(0, 2, 3, 1, 4).reshape(2, 2, 2, cols)
    shifts = wide(take(shifts, core, 2))
    blank = jnp.zeros((LANES,), single)
    bias = [[shifts[t, 0, :LANES], blank, shifts[t, 1, :LANES]] for t in range(2)]
    last = [shifts[0, 0, LANES:], shifts[1, 0, LANES:], blank, shifts[0, 1, LANES:], shifts[1, 1, LANES:]]
    bias = jnp.concatenate(bias[0] + bias[1] + last).reshape(1, -1)
    offset = rest[:, :, n_shift:].reshape((2, size) + offset_weight.shape)
    offset = offset.transpose(0, 2, 1, 3).reshape(2, 2, units)
    offset = wide(take(offset, core, 1)).reshape(1, 2 * units)

    qkv, normed_one, w_attend = project(base, x_mine, x_other, pieces, bias, vectors)
    attended, lse = attend(qkv, period, frames)
    branch, w_output = output_project(attended, all_two, 2 * units)
    hidden_one, normed_two, mixed_turned, mixed, mixed_away, back, act, du, grad_offset = feed_forward(
        x_mine, x_other, branch, swap_core(branch), g_mine, g_other, all_two, offset, vectors
    )

    back_other, mixed_other = swap_core(back), swap_core(mixed_away)
    keep_a, send_a = expand_grad(base, layout, after(normed_two, back, mixed), du)
    block, grad_hidden, branch_turned, grad_attended, sums = middle(
        back, back_other, hidden_one, g_mine, g_other, mixed, mixed_other, w_output, vectors
    )
    block_other = swap_tp(block)
    keep_b, send_b = reduce_grad(base, layout, mixed_turned, act, branch_turned, attended)
    step = lambda j, *gates: attend_back(
        j, after(qkv, *gates), attended, lse, grad_attended, period, frames
    )
    if quick:
        near_a, near_b = swap_near(send_a), swap_near(send_b)
        grad_0 = step(0, send_a, send_b, block)
        near_a = wide(after(near_a, grad_0)) + wide(keep_a)
        away_a = low(near_a[1])
        tp_a = swap_tp(away_a)
        block_other = after(block_other, grad_0)
        grad_1 = step(1, grad_0, away_a, block_other)
        keep_c, send_c = attend_grad(base, layout, normed_one, (grad_0, grad_1))
        near_c = swap_near(send_c)
        near_b = wide(after(near_b, grad_1)) + wide(keep_b)
        away_b = low(near_b[1])
        tp_b = swap_tp(away_b)
        part_a = near_a[0] + wide(after(tp_a, grad_1))
        part_a, far_a, got_a = fold(part_a, 2, 0)
        grad_2 = step(2, grad_1, send_c, away_b, far_a)
    else:
        grad_0, grad_1, grad_2 = step(0), step(1), step(2)
        total_a, total_b = scatter_any(keep_a, send_a), scatter_any(keep_b, send_b)
    part, part_away, shift_sums = project_back((grad_0, grad_1, grad_2), w_attend)
    part_other = swap_core(part_away)
    if quick:
        part_b, far_b, got_b = fold(near_b[0] + wide(after(tp_b, part)), 2, 0)
        part_c, far_c, got_c = fold(wide(after(near_c, part)) + wide(keep_c), 2, 1)
        part_a, far_a, got_a = fold(part_a + wide(after(got_a, part)), 4, 0)
        part_other = after(part_other, far_a, far_b, far_c)
    input_own, first_sums = first_back(part, part_other, x_mine, grad_hidden, vectors)
    input_other = swap_tp(input_own)
    keep_d, send_d = attend_grad(base, layout, after(normed_one, input_own), (grad_2,))
    if quick:
        near_d = swap_near(send_d)
        part_b, far_b, got_b = fold(part_b + wide(after(got_b, send_d)), 4, 0)
        part_c, far_c, got_c = fold(part_c + wide(after(got_c, send_d)), 4, 1)

    flat = jnp.concatenate(
        [first_sums[:2].reshape(-1), sums[2:6].reshape(-1), shift_sums[0], grad_offset[0]]
    )
    n_vectors, n_flat = 6 * width, flat.size
    total_cols = TRIPLE + 2 * LANES
    flat = jnp.pad(flat, (0, 16 * total_cols - n_flat)).reshape(16, total_cols)

    if quick:
        flat = flat + swap_near(flat)

        def ride(stay, away, flat, send):
            columns = away.shape[-1]
            rows = flat.size // columns
            away = low(jnp.concatenate([away.reshape(-1, columns), flat.reshape(-1, columns)]))
            got = wide(send(away))
            return stay + got[:-rows].reshape(stay.shape), flat + got[-rows:].reshape(flat.shape), away

        part_d = wide(after(near_d, far_b, far_c)) + wide(keep_d)
        for stride in (2, 4):
            halves = part_d.reshape(2, -1, 2, *part_d.shape[2:])
            send = functools.partial(send_fsdp, target=lambda i: i ^ stride)
            part_d, flat, away_d = ride(halves[:, :, 0], halves[:, :, 1], flat, send)
        part_c = part_c + wide(after(got_c, away_d))
        part_c = jnp.concatenate([part_c, part_d], axis=3)[:, 0]
        total_c, flat, away_c = ride(part_c[0], part_c[1], flat, swap_tp)
        total_a = (part_a + wide(after(got_a, away_d)))[0]
        total_b = (part_b + wide(after(got_b, away_d)))[0]
    else:
        keep_c, send_c = attend_grad(base, layout, normed_one, (grad_0, grad_1))
        total_c = [scatter_any(keep_c, send_c), scatter_any(keep_d, send_d)]
        total_c = jnp.concatenate(total_c, axis=1)
        flat = sum_all(flat)
    last = swap_core(jnp.concatenate([total_c, flat]))
    other_c, other_flat = last[:-16], last[-16:].reshape(-1)[:n_flat]
    flat = flat.reshape(-1)[:n_flat]
    total_vectors = take((flat + other_flat)[:n_vectors].reshape(6, size, -1), at, 1)
    slots = join(flat[None, n_vectors:], other_flat[None, n_vectors:], first_core, 0)
    slot_shift = slots[:, : PAIRS * TRIPLE].reshape(2, PAIRS, 3, LANES)[:, :, ::2]
    tail = jnp.where(first_tp, slot_shift[:, 2, :, :HD], slot_shift[:, 2, :, HD:])
    total_shifts = jnp.concatenate([take(slot_shift, half, 1), tail], axis=2)
    total_shifts = total_shifts.transpose(1, 0, 2).reshape(2, -1, size, HD // size)
    total_shifts = take(total_shifts, at, 2)
    total_offset = take(slots[:, PAIRS * TRIPLE :].reshape(2, 2, units), half, 1)
    total_offset = take(total_offset.reshape(-1, size, HD // size), at, 1)

    def both(mine, other, axis):
        return join(mine, other, first_core, axis)

    other_a, other_b = swap_core(total_a), swap_core(total_b)
    total_expand = both(total_a, other_a, 1)
    total_reduce = both(total_b[:, :units], other_b[:, :units], 1).T
    total_output = both(total_b[:, units : units + cols], other_b[:, units : units + cols], 1).T

    def parts(total):
        rows = [
            jnp.concatenate(
                [
                    total[:, p * LANES : (p + 1) * LANES],
                    total[:, TRIPLE + p * HD : TRIPLE + (p + 1) * HD],
                ],
                axis=1,
            )
            for p in range(3)
        ]
        return jnp.stack(rows, axis=1)

    total_attend = both(parts(total_c), parts(other_c), 2)

    attend_new = adamw(
        attend_weight, total_attend, attend_moment, attend_square, rate_matrix, decay_matrix
    )
    shifts_new = adamw(shifts_weight, total_shifts, shifts_moment, shifts_square, rate_vector, 0.0)
    output_new = adamw(
        output_weight, total_output, output_moment, output_square, rate_matrix, decay_matrix
    )
    expand_new = adamw(
        expand_weight, total_expand, expand_moment, expand_square, rate_matrix, decay_matrix
    )
    offset_new = adamw(offset_weight, total_offset, offset_moment, offset_square, rate_vector, 0.0)
    reduce_new = adamw(
        reduce_weight, total_reduce, reduce_moment, reduce_square, rate_matrix, decay_matrix
    )
    vectors_new = adamw(
        vectors_weight, total_vectors, vectors_moment, vectors_square, rate_vector, 0.0
    )
    block = after(block, input_own)
    block_output = join(block[None, :frames], block_other[None, :frames], first_tp, 0)
    input_grad = assemble(half.astype(jnp.int32)[None], input_own, input_other, frames, single)
    return (
        block_output,
        input_grad,
        *attend_new,
        *shifts_new,
        *output_new,
        *expand_new,
        *offset_new,
        *reduce_new,
        *vectors_new,
    )


def solution(mesh):
    tokens = (P("fsdp", "ctx", None),) * 2
    params = (
        (P("fsdp", None, "tp"),) * 3
        + (P(None, "tp", "fsdp"),) * 3
        + (P("tp", "fsdp"),) * 3
        + (P("fsdp", "tp"),) * 3
        + (P("tp", "fsdp"),) * 3
        + (P("tp", "fsdp"),) * 3
        + (P(None, "fsdp"),) * 3
    )
    return jax.shard_map(
        local,
        mesh=mesh,
        in_specs=tokens + params,
        out_specs=tokens + params,
        check_vma=False,
    )
```

```python
import functools
import math

import jax
import jax.numpy as jnp
from jax import lax
from jax.experimental import pallas as pl
from jax.experimental.pallas import tpu as pltpu
from jax.sharding import PartitionSpec as P

HD = 64
STEP = 10


norm_eps = 1e-05
beta_first = 0.9
beta_second = 0.999
adam_eps = 1e-08
rate_matrix = 0.05
rate_vector = 0.5
decay_matrix = 0.01

bfloat = jnp.bfloat16
single = jnp.float32
LANES = 128
TRIPLE = 3 * LANES
PAIRS = 3
ROWS = 384
FEED_ROWS = 256
QUERY_ROWS = 768
KEY_ROWS = 512
SAFE_EXPONENT = 100.0
SWAP = [(0, 1), (1, 0)]
EXP_SCALE = HD ** (-0.5) * math.log2(math.e)
MASK = -1e30
VMEM = 56 * 1024 * 1024
NT = (((1,), (1,)), ((), ()))
TN = (((0,), (0,)), ((), ()))
PARAMS = pltpu.CompilerParams(vmem_limit_bytes=VMEM)


def dot(left, right, dims=(((1,), (0,)), ((), ()))):
    return lax.dot_general(left, right, dims, preferred_element_type=single)


def adamw(param, grad, moment, square, rate, decay):
    moment_new = beta_first * moment + (1.0 - beta_first) * grad
    square_new = beta_second * square + (1.0 - beta_second) * grad * grad
    corrected = moment_new / (1.0 - beta_first**STEP)
    normal_sq = square_new / (1.0 - beta_second**STEP)
    param_new = param - rate * (corrected / (jnp.sqrt(normal_sq) + adam_eps) + decay * param)
    return (param_new, moment_new, square_new)


def norm_parts(values):
    average = jnp.mean(values, axis=-1, keepdims=True)
    centered = values - average
    variance = jnp.mean(centered * centered, axis=-1, keepdims=True)
    inverse = lax.rsqrt(variance + norm_eps)
    return centered * inverse, inverse


def norm_back(grad, unit, inverse, gain):
    scaled = grad * gain
    first = jnp.mean(scaled, axis=-1, keepdims=True)
    second = jnp.mean(scaled * unit, axis=-1, keepdims=True)
    return (scaled - first - unit * second) * inverse


def column_sum(values):
    return jnp.sum(values, axis=0, keepdims=True)


def turned(value):
    return pltpu.roll(value, HD, 1)


def split_three(column):
    high = column.astype(bfloat).astype(single)
    rest = column - high
    middle = rest.astype(bfloat).astype(single)
    return high, middle, (rest - middle).astype(bfloat).astype(single)


def beside(values, half, extras):
    lane = lax.broadcasted_iota(jnp.int32, values.shape, 1)
    base = HD * (1 - half)
    mine = (lane >= HD) if half else (lane < HD)
    out = jnp.where(mine, values, 0.0)
    for place, extra in enumerate(extras):
        out = jnp.where(lane == base + place, extra, out)
    return out.astype(bfloat)


def pad_column(first_row, rows, period, valid):
    row = first_row + lax.broadcasted_iota(jnp.int32, (rows, 1), 0)
    return jnp.where(row % period < valid, 0.0, MASK)


def whole(shape):
    return pl.BlockSpec(shape, lambda *_: (0,) * len(shape))


def struct(shape, dtype):
    return jax.ShapeDtypeStruct(shape, dtype)


def cost(flops, bytes_accessed, transcendentals=0):
    share = 32
    return pl.CostEstimate(
        flops=int(flops) // share,
        bytes_accessed=int(bytes_accessed) // share,
        transcendentals=int(transcendentals) // share,
    )


def project_kernel(base, x_ref, o_ref, *refs):
    pieces, (bias_ref, vec_ref, qkv_ref, nt_ref, w_ref) = refs[:8], refs[8:]
    step = pl.program_id(0)
    cut, rows, _ = pieces[0].shape
    far = vec_ref.shape[1] // (2 * rows)

    @pl.when(step == 0)
    def _():
        flip = base[2] == 1
        swap = base[0] == 1
        lane = lax.broadcasted_iota(jnp.int32, (rows, LANES), 1)
        for z in range(far):
            at = lax.rem(z - base[1] + far, far)
            inner = lax.rem(at, cut)
            read = lambda n: jnp.where(at < cut, pieces[2 * n][inner], pieces[2 * n + 1][inner])
            own, near, away, across = (read(n) for n in range(4))
            for x in range(2):
                here = jnp.where(flip, own, near) if x else jnp.where(flip, near, own)
                there = jnp.where(flip, away, across) if x else jnp.where(flip, across, away)
                both = (jnp.where(swap, there, here), jnp.where(swap, here, there))
                place = slice((2 * z + x) * rows, (2 * z + x + 1) * rows)
                w_ref[0, place, :] = both[0][:, :TRIPLE]
                w_ref[1, place, :] = both[1][:, :TRIPLE]
                mixed = [b[:, TRIPLE : TRIPLE + LANES].astype(single) for b in both]
                last = [b[:, TRIPLE + LANES :].astype(single) for b in both]
                q = jnp.where(lane < HD, mixed[0], turned(mixed[1]))
                k = jnp.where(lane < HD, turned(mixed[0]), mixed[1])
                v = jnp.where(lane < HD, last[0], turned(last[1]))
                for part, value in enumerate((q, k, v)):
                    w_ref[2, place, part * LANES : (part + 1) * LANES] = value.astype(bfloat)

    x = jnp.where(step < pl.num_programs(0) // 2, x_ref[...], o_ref[...]).astype(single)
    unit, _ = norm_parts(x)
    normed = unit * vec_ref[0:1, :] + vec_ref[1:2, :]
    nt_ref[...] = normed.astype(bfloat).T
    normed = normed.astype(bfloat)
    for j in range(PAIRS):
        cols = slice(j * TRIPLE, (j + 1) * TRIPLE)
        qkv_ref[:, cols] = (dot(normed, w_ref[j]) + bias_ref[:, cols]).astype(bfloat)


def own_block(blocks):
    return lambda i, *_: (jnp.minimum(i, blocks - 1), 0)


def other_block(blocks):
    return lambda i, *_: (jnp.maximum(i - blocks, 0), 0)


def project(base, x_mine, x_other, pieces, bias, vectors):
    period, width = x_mine.shape
    blocks = period // ROWS
    rows = 2 * period
    out = PAIRS * TRIPLE
    return pl.pallas_call(
        project_kernel,
        grid_spec=pltpu.PrefetchScalarGridSpec(
            num_scalar_prefetch=1,
            grid=(2 * blocks,),
            in_specs=[
                pl.BlockSpec((ROWS, width), own_block(blocks)),
                pl.BlockSpec((ROWS, width), other_block(blocks)),
                *[whole(p.shape) for p in pieces],
                whole(bias.shape),
                whole(vectors.shape),
            ],
            out_specs=[
                pl.BlockSpec((ROWS, out), lambda i, *_: (i, 0)),
                pl.BlockSpec((width, ROWS), lambda i, *_: (0, i)),
                whole((PAIRS, width, TRIPLE)),
            ],
        ),
        out_shape=[
            struct((rows, out), bfloat),
            struct((width, rows), bfloat),
            struct((PAIRS, width, TRIPLE), bfloat),
        ],
        compiler_params=PARAMS,
        cost_estimate=cost(2 * rows * width * out, 2 * rows * (2 * width + out) + 4 * width * out),
        name="project",
    )(base, x_mine, x_other, *pieces, bias, vectors)


def attend_kernel(period, valid, q_ref, k_ref, v_ref, o_ref, lse_ref, keys, values, longest):
    def norms(value):
        square = value * value
        lane = lax.broadcasted_iota(jnp.int32, value.shape, 1)
        sums = [jnp.sum(jnp.where(mine, square, 0.0), axis=1) for mine in (lane < HD, lane >= HD)]
        return jnp.maximum(jnp.max(sums[0]), jnp.max(sums[1]))

    @pl.when(pl.program_id(1) == 0)
    def _():
        k = k_ref[...].astype(single)
        v = v_ref[...].astype(single)
        pad = pad_column(0, k.shape[0], period, valid)
        for half in range(2):
            keys[half] = beside(k, half, (pad,))
            values[half] = beside(v, half, (1.0,)).T
        longest[0] = norms(k)

    q = q_ref[...].astype(single)
    bound = norms(q) * longest[0] * (EXP_SCALE * EXP_SCALE)
    safe = bound < SAFE_EXPONENT * SAFE_EXPONENT

    def run(shift):
        outs, tops = [], []
        for half in range(2):
            scores = dot(keys[half], beside(q, half, (1.0,)), NT)
            if shift:
                top = jnp.max(scores, axis=0, keepdims=True)
                scores = scores - top
            raised = jnp.exp2(scores * EXP_SCALE)
            both = dot(values[half], raised.astype(bfloat))
            base = HD * (1 - half)
            total = both[base : base + 1, :]
            outs.append(both / total)
            low = jnp.log2(total) / EXP_SCALE
            tops.append(top + low if shift else low)
        row = lax.broadcasted_iota(jnp.int32, outs[0].shape, 0)
        o_ref[...] = jnp.where(row < HD, outs[0], outs[1]).T.astype(bfloat)
        lse_ref[...] = jnp.where(row < HD, tops[0], tops[1]).T

    @pl.when(safe)
    def _():
        run(False)

    @pl.when(jnp.logical_not(safe))
    def _():
        run(True)


def attend(qkv, period, valid):
    rows = qkv.shape[0]
    width = PAIRS * LANES
    part = lambda at: pl.BlockSpec((rows, LANES), lambda j, i: (0, 3 * j + at))
    block = pl.BlockSpec((QUERY_ROWS, LANES), lambda j, i: (i, j))
    return pl.pallas_call(
        functools.partial(attend_kernel, period, valid),
        grid=(PAIRS, rows // QUERY_ROWS),
        in_specs=[pl.BlockSpec((QUERY_ROWS, LANES), lambda j, i: (i, 3 * j)), part(1), part(2)],
        out_specs=[block, block],
        out_shape=[struct((rows, width), bfloat), struct((rows, width), single)],
        scratch_shapes=[
            pltpu.VMEM((2, rows, LANES), bfloat),
            pltpu.VMEM((2, LANES, rows), bfloat),
            pltpu.SMEM((1,), single),
        ],
        compiler_params=PARAMS,
        cost_estimate=cost(16 * rows * rows * LANES * PAIRS, 20 * rows * width, 2 * PAIRS * rows * rows),
        name="attend",
    )(qkv, qkv, qkv)


def attend_back_kernel(
    period, valid, q_ref, k_ref, v_ref, o_ref, lse_ref, g_ref,
    out_ref, queries, queries_turned, grads, grads_turned, total,
):
    step = pl.program_id(0)
    lane_all = lax.broadcasted_iota(jnp.int32, q_ref.shape, 1)

    @pl.when(step == 0)
    def _():
        q = q_ref[...].astype(single)
        g = g_ref[...].astype(single)
        product = g * o_ref[...].astype(single)
        for half in range(2):
            mine = (lane_all >= HD) if half else (lane_all < HD)
            inner = jnp.sum(jnp.where(mine, product, 0.0), axis=1, keepdims=True)
            low = jnp.max(jnp.where(mine, lse_ref[...], -jnp.inf), axis=1, keepdims=True)
            queries[half] = beside(q, half, (1.0,) + split_three(-low))
            grads[half] = beside(g, half, (0.0,) + split_three(-inner))
            queries_turned[half] = queries[half].T
            grads_turned[half] = grads[half].T
        total[...] = jnp.zeros_like(total)

    k = k_ref[...].astype(single)
    v = v_ref[...].astype(single)
    pad = pad_column(step * k.shape[0], k.shape[0], period, valid)
    dks, dvs, dqs = [], [], []
    for half in range(2):
        keys = beside(k, half, (pad, 1.0, 1.0, 1.0))
        values = beside(v, half, (1.0, 1.0, 1.0, 1.0))
        weights = jnp.exp2(dot(queries[half], keys, NT) * EXP_SCALE)
        inner = weights * dot(grads[half], values, NT)
        dvs.append(dot(grads_turned[half], weights.astype(bfloat)))
        low = inner.astype(bfloat)
        dks.append(dot(queries_turned[half], low))
        dqs.append(dot(low, keys))
    scale = HD ** (-0.5)
    here = pl.ds(pl.multiple_of(step * KEY_ROWS, KEY_ROWS), KEY_ROWS)
    row = lax.broadcasted_iota(jnp.int32, dks[0].shape, 0)
    dk = jnp.where(row < HD, dks[0], dks[1]) * scale
    out_ref[here, LANES : 2 * LANES] = dk.T.astype(bfloat)
    out_ref[here, 2 * LANES :] = jnp.where(row < HD, dvs[0], dvs[1]).T.astype(bfloat)
    total[...] += jnp.where(lane_all < HD, dqs[0], dqs[1])

    @pl.when(step == pl.num_programs(0) - 1)
    def _():
        out_ref[:, :LANES] = (total[...] * scale).astype(bfloat)


def attend_back(j, qkv, o, lse, grad, period, valid):
    rows = qkv.shape[0]
    column = lambda at: pl.BlockSpec((rows, LANES), lambda i: (0, at))
    block = lambda at: pl.BlockSpec((KEY_ROWS, LANES), lambda i: (i, at))
    return pl.pallas_call(
        functools.partial(attend_back_kernel, period, valid),
        grid=(rows // KEY_ROWS,),
        in_specs=[column(3 * j), block(3 * j + 1), block(3 * j + 2), column(j), column(j), column(j)],
        out_specs=whole((rows, TRIPLE)),
        out_shape=struct((rows, TRIPLE), bfloat),
        scratch_shapes=[
            pltpu.VMEM((2, rows, LANES), bfloat),
            pltpu.VMEM((2, LANES, rows), bfloat),
            pltpu.VMEM((2, rows, LANES), bfloat),
            pltpu.VMEM((2, LANES, rows), bfloat),
            pltpu.VMEM((rows, LANES), single),
        ],
        compiler_params=PARAMS,
        cost_estimate=cost(40 * rows * rows * LANES, 20 * rows * LANES, 2 * rows * rows),
        name=f"attend_back_{j}",
    )(qkv, qkv, qkv, o, lse, grad)


def output_kernel(o_ref, w_ref, out_ref, full_ref):
    @pl.when(pl.program_id(0) == 0)
    def _():
        lane = lax.broadcasted_iota(jnp.int32, (w_ref.shape[1], LANES), 1)
        full_ref[:, :LANES] = w_ref[0, :, :LANES]
        full_ref[:, LANES : 2 * LANES] = w_ref[1, :, :LANES]
        last = [w_ref[t, :, LANES:].astype(single) for t in range(2)]
        full_ref[:, 2 * LANES :] = jnp.where(lane < HD, last[0], turned(last[1])).astype(bfloat)

    out_ref[...] = dot(o_ref[...], full_ref[...], NT).astype(bfloat)


def output_project(o, weights, place):
    rows, width = o.shape[0], weights.shape[1]
    columns = o.shape[1]
    return pl.pallas_call(
        output_kernel,
        grid=(rows // ROWS,),
        in_specs=[
            pl.BlockSpec((ROWS, columns), lambda i: (i, 0)),
            pl.BlockSpec((2, width, 2 * LANES), lambda i: (0, 0, place // (2 * LANES))),
        ],
        out_specs=[pl.BlockSpec((ROWS, width), lambda i: (i, 0)), whole((width, columns))],
        out_shape=[struct((rows, width), bfloat), struct((width, columns), bfloat)],
        compiler_params=PARAMS,
        cost_estimate=cost(2 * rows * width * columns, 2 * rows * (width + columns)),
        name="output_project",
    )(o, weights)


def feed_kernel(
    x_ref, xo_ref, p_ref, po_ref, g_ref, go_ref, w1_ref, w2_ref, b_ref, vec_ref,
    h_ref, nt_ref, gt_ref, y_ref, yo_ref, dn_ref, act_ref, du_ref, db_ref,
):
    step = pl.program_id(0)
    mine = step < pl.num_programs(0) // 2
    x = jnp.where(mine, x_ref[...], xo_ref[...]).astype(single)
    grad = jnp.where(mine, g_ref[...], go_ref[...])
    hidden = x + (p_ref[...].astype(single) + po_ref[...].astype(single)) + vec_ref[2:3, :]
    h_ref[...] = hidden
    unit, _ = norm_parts(hidden)
    normed = unit * vec_ref[3:4, :] + vec_ref[4:5, :]
    nt_ref[...] = normed.astype(bfloat).T
    gt_ref[...] = grad.T
    normed = normed.astype(bfloat)
    count, _, units = w1_ref.shape
    mixed = back = 0.0

    @pl.when(step == 0)
    def _():
        db_ref[...] = jnp.zeros_like(db_ref)

    for part in range(count):
        cols = slice(part * units, (part + 1) * units)
        u = dot(normed, w1_ref[part]) + b_ref[:, cols]
        phi = 0.5 * (1.0 + lax.erf(u * (0.5**0.5)))
        act = (u * phi).astype(bfloat)
        slope = phi + u * (jnp.exp(-0.5 * u * u) * ((2.0 * math.pi) ** -0.5))
        du = (dot(grad, w2_ref[part]) * slope).astype(bfloat)
        act_ref[:, cols] = act
        du_ref[:, cols] = du
        db_ref[:, cols] += column_sum(du.astype(single))
        mixed = mixed + dot(act, w2_ref[part], NT)
        back = back + dot(du, w1_ref[part], NT)
    dn_ref[...] = back.astype(bfloat)

    @pl.when(mine)
    def _():
        y_ref[...] = mixed.astype(bfloat)

    @pl.when(jnp.logical_not(mine))
    def _():
        yo_ref[...] = mixed.astype(bfloat)


def feed_forward(x_mine, x_other, part, part_other, g_mine, g_other, weights, bias, vectors):
    rows, width = part.shape
    blocks = rows // FEED_ROWS // 2
    count, hidden = weights.shape[0], bias.shape[1]
    units = hidden // count
    tokens = pl.BlockSpec((FEED_ROWS, width), lambda i: (i, 0))
    crossed = pl.BlockSpec((FEED_ROWS, width), lambda i: ((i + blocks) % (2 * blocks), 0))
    wide = pl.BlockSpec((FEED_ROWS, hidden), lambda i: (i, 0))
    tall = pl.BlockSpec((width, FEED_ROWS), lambda i: (0, i))
    own = pl.BlockSpec((FEED_ROWS, width), own_block(blocks))
    other = pl.BlockSpec((FEED_ROWS, width), other_block(blocks))
    weight = lambda at: pl.BlockSpec((count, width, units), lambda i: (0, 0, at))
    return pl.pallas_call(
        feed_kernel,
        grid=(2 * blocks,),
        in_specs=[
            own, other, tokens, crossed, own, other, weight(0), weight(1),
            whole(bias.shape), whole(vectors.shape),
        ],
        out_specs=[tokens, tall, tall, own, other, tokens, wide, wide, whole((1, hidden))],
        out_shape=[
            struct((rows, width), single),
            struct((width, rows), bfloat),
            struct((width, rows), bfloat),
            struct((rows // 2, width), bfloat),
            struct((rows // 2, width), bfloat),
            struct((rows, width), bfloat),
            struct((rows, hidden), bfloat),
            struct((rows, hidden), bfloat),
            struct((1, hidden), single),
        ],
        compiler_params=PARAMS,
        cost_estimate=cost(
            8 * rows * width * hidden,
            18 * rows * width + 4 * rows * hidden + 4 * width * hidden,
            2 * rows * hidden,
        ),
        name="feed_forward",
    )(x_mine, x_other, part, part_other, g_mine, g_other, weights, weights, bias, vectors)


def put(base, keep_ref, send_ref, t, value, cols):
    far, rows = keep_ref.shape[1], keep_ref.shape[2]
    first = base[2] == 0
    for z in range(far):
        at = jnp.bitwise_xor(z, base[1])
        lo = value[2 * z * rows : (2 * z + 1) * rows].astype(bfloat)
        hi = value[(2 * z + 1) * rows : (2 * z + 2) * rows].astype(bfloat)
        keep_ref[t, at, :, cols] = jnp.where(first, lo, hi)
        send_ref[t, at, :, cols] = jnp.where(first, hi, lo)


def expand_grad_kernel(base, left_ref, right_ref, keep_ref, send_ref):
    put(base, keep_ref, send_ref, 0, dot(left_ref[...], right_ref[...]), slice(None))


def expand_grad(base, layout, left, right):
    width, rows = left.shape
    units = right.shape[1] // 2
    shape = (2,) + layout + (units,)
    out = pl.BlockSpec((1,) + layout + (units,), lambda t, base: (t, 0, 0, 0))
    return pl.pallas_call(
        expand_grad_kernel,
        grid_spec=pltpu.PrefetchScalarGridSpec(
            num_scalar_prefetch=1,
            grid=(2,),
            in_specs=[
                whole(left.shape),
                pl.BlockSpec((rows, units), lambda t, base: (0, (t + base[0]) % 2)),
            ],
            out_specs=[out, out],
        ),
        out_shape=[struct(shape, bfloat)] * 2,
        compiler_params=PARAMS,
        cost_estimate=cost(4 * rows * width * units, 2 * rows * (width + 2 * units) + 4 * width * units),
        name="expand_grad",
    )(base, left, right)


def reduce_grad_kernel(base, left_ref, right_ref, branch_ref, o_ref, keep_ref, send_ref, output):
    @pl.when(pl.program_id(0) == 0)
    def _():
        output[...] = dot(branch_ref[...], o_ref[...])

    at = lax.rem(pl.program_id(0) + base[0], 2)
    units = right_ref.shape[1]
    put(base, keep_ref, send_ref, 0, dot(left_ref[...], right_ref[...]), slice(0, units))
    mine = output[:, pl.ds(pl.multiple_of(at * LANES, LANES), LANES)]
    put(base, keep_ref, send_ref, 0, mine, slice(units, units + LANES))
    mixed = output[:, 2 * LANES :]
    mixed = jnp.where(at == 0, mixed, turned(mixed))
    put(base, keep_ref, send_ref, 0, mixed, slice(units + LANES, units + 2 * LANES))


def reduce_grad(base, layout, left, right, branch, o):
    width, rows = left.shape
    units = right.shape[1] // 2
    total = units + 2 * LANES
    shape = (2,) + layout + (total,)
    out = pl.BlockSpec((1,) + layout + (total,), lambda t, base: (t, 0, 0, 0))
    return pl.pallas_call(
        reduce_grad_kernel,
        grid_spec=pltpu.PrefetchScalarGridSpec(
            num_scalar_prefetch=1,
            grid=(2,),
            in_specs=[
                whole(left.shape),
                pl.BlockSpec((rows, units), lambda t, base: (0, (t + base[0]) % 2)),
                whole(branch.shape),
                whole(o.shape),
            ],
            out_specs=[out, out],
            scratch_shapes=[pltpu.VMEM((width, o.shape[1]), single)],
        ),
        out_shape=[struct(shape, bfloat)] * 2,
        compiler_params=PARAMS,
        cost_estimate=cost(4 * rows * width * total, 2 * rows * (2 * width + 2 * total) + 4 * width * total),
        name="reduce_grad",
    )(base, left, right, branch, o)


def pair_grad_kernel(base, left_ref, a_ref, b_ref, keep_ref, send_ref):
    left = left_ref[...]
    pairs = [dot(left, ref[...]) for ref in (a_ref, b_ref)]
    for t in range(2):
        put(base, keep_ref, send_ref, jnp.bitwise_xor(t, base[0]), pairs[t], slice(0, TRIPLE))


def mixed_grad_kernel(base, left_ref, ref, keep_ref, send_ref):
    full = dot(left_ref[...], ref[...])
    q, k, v = (full[:, part * LANES : (part + 1) * LANES] for part in range(3))
    lane = lax.broadcasted_iota(jnp.int32, q.shape, 1)
    mixed = [
        (jnp.where(lane < HD, q, turned(k)), v),
        (jnp.where(lane < HD, turned(q), k), turned(v)),
    ]
    for t in range(2):
        for place in range(2):
            cols = slice(place * LANES, (place + 1) * LANES)
            put(base, keep_ref, send_ref, jnp.bitwise_xor(t, base[0]), mixed[t][place], cols)


def attend_grad(base, layout, left, grads):
    width, rows = left.shape
    count = len(grads)
    columns = TRIPLE if count == 2 else 2 * LANES
    shape = (2,) + layout + (columns,)
    return pl.pallas_call(
        pair_grad_kernel if count == 2 else mixed_grad_kernel,
        grid_spec=pltpu.PrefetchScalarGridSpec(
            num_scalar_prefetch=1,
            grid=(1,),
            in_specs=[whole(left.shape)] + [whole(g.shape) for g in grads],
            out_specs=[whole(shape)] * 2,
        ),
        out_shape=[struct(shape, bfloat)] * 2,
        compiler_params=PARAMS,
        cost_estimate=cost(
            2 * count * rows * width * TRIPLE, 2 * rows * (width + count * TRIPLE) + 8 * width * columns
        ),
        name=f"attend_grad_{count}",
    )(base, left, *grads)


def middle_kernel(
    p_ref, po_ref, h_ref, g_ref, go_ref, y_ref, yo_ref, w_ref, vec_ref,
    out_ref, dh_ref, bt_ref, do_ref, sums_ref,
):
    step = pl.program_id(0)
    mine = step < pl.num_programs(0) // 2
    grad = jnp.where(mine, g_ref[...], go_ref[...]).astype(single)
    hidden = h_ref[...]
    unit, inverse = norm_parts(hidden)
    normed = p_ref[...].astype(single) + po_ref[...].astype(single)
    after = grad + norm_back(normed, unit, inverse, vec_ref[3:4, :])
    bt_ref[...] = after.astype(bfloat).T
    branch = after.astype(bfloat)
    do_ref[...] = dot(branch, w_ref[...]).astype(bfloat)

    @pl.when(step == 0)
    def _():
        sums_ref[...] = jnp.zeros_like(sums_ref)

    @pl.when(mine)
    def _():
        dh_ref[...] = after
        mixed = y_ref[...].astype(single) + yo_ref[...].astype(single)
        out_ref[...] = (hidden + mixed + vec_ref[5:6, :]).astype(bfloat)
        sums_ref[2:3, :] += column_sum(branch.astype(single))
        sums_ref[3:4, :] += column_sum(normed * unit)
        sums_ref[4:5, :] += column_sum(normed)
        sums_ref[5:6, :] += column_sum(grad)


def middle(part, part_other, hidden, g_mine, g_other, mixed, mixed_other, weight, vectors):
    rows, width = part.shape
    blocks = rows // ROWS // 2
    tokens = pl.BlockSpec((ROWS, width), lambda i: (i, 0))
    crossed = pl.BlockSpec((ROWS, width), lambda i: ((i + blocks) % (2 * blocks), 0))
    own = pl.BlockSpec((ROWS, width), own_block(blocks))
    other = pl.BlockSpec((ROWS, width), other_block(blocks))
    columns = weight.shape[1]
    return pl.pallas_call(
        middle_kernel,
        grid=(2 * blocks,),
        in_specs=[
            tokens, crossed, tokens, own, other, own, own, whole(weight.shape), whole(vectors.shape)
        ],
        out_specs=[
            own,
            own,
            pl.BlockSpec((width, ROWS), lambda i: (0, i)),
            pl.BlockSpec((ROWS, columns), lambda i: (i, 0)),
            whole((8, width)),
        ],
        out_shape=[
            struct((rows // 2, width), bfloat),
            struct((rows // 2, width), single),
            struct((width, rows), bfloat),
            struct((rows, columns), bfloat),
            struct((8, width), single),
        ],
        compiler_params=PARAMS,
        cost_estimate=cost(2 * rows * width * columns, 16 * rows * width),
        name="middle",
    )(part, part_other, hidden, g_mine, g_other, mixed, mixed_other, weight, vectors)


def project_back_kernel(a_ref, b_ref, c_ref, w_ref, out_ref, other_ref, sums_ref):
    @pl.when(pl.program_id(0) == 0)
    def _():
        sums_ref[...] = jnp.zeros_like(sums_ref)

    total = 0.0
    for j, ref in enumerate((a_ref, b_ref, c_ref)):
        grad = ref[...]
        total = total + dot(grad, w_ref[j], NT)
        cols = slice(j * TRIPLE, (j + 1) * TRIPLE)
        sums_ref[:, cols] += column_sum(grad.astype(single))
    mine = pl.program_id(0) < pl.num_programs(0) // 2

    @pl.when(mine)
    def _():
        out_ref[...] = total.astype(bfloat)

    @pl.when(jnp.logical_not(mine))
    def _():
        other_ref[...] = total.astype(bfloat)


def project_back(grads, weight):
    rows = grads[0].shape[0]
    width = weight.shape[1]
    block = pl.BlockSpec((ROWS, TRIPLE), lambda i: (i, 0))
    return pl.pallas_call(
        project_back_kernel,
        grid=(rows // ROWS,),
        in_specs=[block, block, block, whole(weight.shape)],
        out_specs=[
            pl.BlockSpec((ROWS, width), own_block(rows // ROWS // 2)),
            pl.BlockSpec((ROWS, width), other_block(rows // ROWS // 2)),
            whole((1, PAIRS * TRIPLE)),
        ],
        out_shape=[struct((rows // 2, width), bfloat)] * 2 + [struct((1, PAIRS * TRIPLE), single)],
        compiler_params=PARAMS,
        cost_estimate=cost(6 * rows * width * TRIPLE, 2 * rows * (width + 3 * TRIPLE)),
        name="project_back",
    )(*grads, weight)


def first_back_kernel(p_ref, po_ref, x_ref, dh_ref, vec_ref, out_ref, sums_ref):
    @pl.when(pl.program_id(0) == 0)
    def _():
        sums_ref[...] = jnp.zeros_like(sums_ref)

    unit, inverse = norm_parts(x_ref[...].astype(single))
    normed = p_ref[...].astype(single) + po_ref[...].astype(single)
    out_ref[...] = (dh_ref[...] + norm_back(normed, unit, inverse, vec_ref[0:1, :])).astype(bfloat)
    sums_ref[0:1, :] += column_sum(normed * unit)
    sums_ref[1:2, :] += column_sum(normed)


def first_back(part, part_other, x_mine, grad_hidden, vectors):
    rows, width = x_mine.shape
    tokens = pl.BlockSpec((ROWS, width), lambda i: (i, 0))
    return pl.pallas_call(
        first_back_kernel,
        grid=(rows // ROWS,),
        in_specs=[tokens, tokens, tokens, tokens, whole(vectors.shape)],
        out_specs=[tokens, whole((8, width))],
        out_shape=[struct((rows, width), bfloat), struct((8, width), single)],
        compiler_params=PARAMS,
        cost_estimate=cost(20 * rows * width, 12 * rows * width),
        name="first_back",
    )(part, part_other, x_mine, grad_hidden, vectors)


def assemble_kernel(place, mine_ref, other_ref, out_ref):
    first = place[0] == 0
    frames = out_ref.shape[0]
    mine, other = mine_ref[...].astype(single), other_ref[...].astype(single)
    out_ref[:, 0, :] = jnp.where(first, mine, other)[:frames].astype(out_ref.dtype)
    out_ref[:, 1, :] = jnp.where(first, other, mine)[:frames].astype(out_ref.dtype)


def assemble(place, mine, other, frames, dtype):
    rows, width = mine.shape
    out = pl.pallas_call(
        assemble_kernel,
        grid_spec=pltpu.PrefetchScalarGridSpec(
            num_scalar_prefetch=1,
            grid=(2,),
            in_specs=[pl.BlockSpec((rows, width // 2), lambda i, place: (0, i))] * 2,
            out_specs=pl.BlockSpec((frames, 2, width // 2), lambda i, place: (0, 0, i)),
        ),
        out_shape=struct((frames, 2, width), dtype),
        compiler_params=PARAMS,
        cost_estimate=cost(0, 12 * rows * width),
        name="assemble",
    )(place, mine, other)
    return out.transpose(1, 0, 2)


def swap_core(value):
    return lax.ppermute(value, "ctx", SWAP)


def swap_tp(value):
    return lax.ppermute(value, "tp", SWAP)


def send_fsdp(value, target):
    size = lax.axis_size("fsdp")
    return lax.ppermute(value, "fsdp", [(i, target(i) % size) for i in range(size)])


def swap_near(value):
    return send_fsdp(value, lambda i: i ^ 1)


def after(value, *others):
    return lax.optimization_barrier((value,) + others)[0]


def wide(value):
    return value.astype(single)


def low(value):
    return value.astype(bfloat)


def join(mine, other, first, axis):
    return jnp.concatenate([jnp.where(first, mine, other), jnp.where(first, other, mine)], axis=axis)


def take(value, index, axis=0):
    return lax.dynamic_index_in_dim(value, index, axis, keepdims=False)


def gather_quick(shard):
    size = lax.axis_size("fsdp")
    far = size // 2
    if size != 8:
        full = lax.all_gather(shard, ("tp", "fsdp"), axis=0, tiled=True)
        return [p[None] for p in jnp.split(full, 4) for _ in range(2)]
    steps = [send_fsdp(shard, lambda i, k=k: i + 2 * k) for k in range(1, far)]
    own = [shard] + steps[::-1]
    cut = far // 2
    lo, hi = jnp.stack(own[:cut]), jnp.stack(own[cut:])
    near_lo, away_lo, away_hi, near_hi = swap_near(lo), swap_tp(lo), swap_tp(hi), swap_near(hi)
    return [lo, hi, near_lo, near_hi, away_lo, away_hi, swap_near(away_lo), swap_tp(near_hi)]


def fold(value, stride, axis):
    shape = value.shape
    halves = value.reshape(shape[:axis] + (shape[axis] // 2, 2) + shape[axis + 1 :])
    away = low(lax.index_in_dim(halves, 1, axis + 1, keepdims=False))
    return lax.index_in_dim(halves, 0, axis + 1, keepdims=False), away, send_fsdp(away, lambda i: i ^ stride)


def sum_all(value):
    stride = 2
    while stride < lax.axis_size("fsdp"):
        value = value + send_fsdp(value, lambda i: i ^ stride)
        stride *= 2
    value = value + swap_near(value)
    return value + swap_tp(value)


def scatter_any(keep, send):
    full = wide(jnp.concatenate([keep, send], axis=2)[:, 0])
    full = lax.psum_scatter(full, "tp", scatter_dimension=0, tiled=True)
    return lax.psum_scatter(full, "fsdp", scatter_dimension=1, tiled=True)[0]


def local(
    layer_input,
    cotangent,
    attend_weight,
    attend_moment,
    attend_square,
    shifts_weight,
    shifts_moment,
    shifts_square,
    output_weight,
    output_moment,
    output_square,
    expand_weight,
    expand_moment,
    expand_square,
    offset_weight,
    offset_moment,
    offset_square,
    reduce_weight,
    reduce_moment,
    reduce_square,
    vectors_weight,
    vectors_moment,
    vectors_square,
):
    size = lax.axis_size("fsdp")
    quick = size == 8
    core, half, at = lax.axis_index("ctx"), lax.axis_index("tp"), lax.axis_index("fsdp")
    first_core, first_tp = core == 0, half == 0
    _, frames, width = layer_input.shape
    period = -(-frames // ROWS) * ROWS
    pad = lambda a: jnp.pad(a, ((0, period - frames), (0, 0)))
    shard = attend_weight.shape[0]
    cols = attend_weight.shape[2] // 2
    units = expand_weight.shape[1] // 2
    layout = (size // 2, shard) if quick else (1, width // 2)
    base = jnp.stack([half, at // 2, at % 2]).astype(jnp.int32)
    if not quick:
        base = jnp.zeros_like(base)

    small = jnp.concatenate(
        [low(shifts_weight).reshape(-1), low(offset_weight).reshape(-1), low(vectors_weight).reshape(-1)]
    )
    small = small.reshape(shard, -1)
    small_cols = small.shape[1]
    mine = lax.dynamic_slice_in_dim(low(attend_weight), core * cols, cols, 2)
    pack_one = jnp.concatenate(
        [mine[:, p, :LANES] for p in range(3)]
        + [mine[:, p, LANES:] for p in range(3)]
        + [small, jnp.zeros((shard, HD - small_cols), bfloat)],
        axis=1,
    )
    pieces = gather_quick(pack_one)
    core_next = after(core, pack_one)
    expand_mine = lax.dynamic_slice_in_dim(low(expand_weight), core_next * units, units, 1)
    reduce_mine = lax.dynamic_slice_in_dim(low(reduce_weight), core_next * units, units, 0).T
    output_mine = lax.dynamic_slice_in_dim(low(output_weight), core_next * cols, cols, 0).T
    pack_two = jnp.concatenate(
        [expand_mine, reduce_mine, output_mine, jnp.zeros((shard, HD), bfloat)], axis=1
    )
    all_two = lax.all_gather(pack_two, ("tp", "fsdp"), axis=0, tiled=True).reshape(2, width, -1)

    x_mine, g_mine = pad(take(layer_input, half)), pad(take(cotangent, half))
    x_other, g_other = swap_core(x_mine), swap_core(g_mine)

    n_shift, n_offset = shifts_weight.size, offset_weight.size
    n_other = n_shift + n_offset

    def table(places):
        out = []
        for n in places:
            halves = pieces[2 * n : 2 * n + 2] if quick else pieces[2 * n : 2 * n + 1]
            out += [p[:, :, 3 * cols : 3 * cols + small_cols].reshape(p.shape[0], -1) for p in halves]
        out = jnp.concatenate(out).reshape(len(places) // 2, 2, -1, small_cols * shard)
        if not quick:
            return out.reshape(-1, size, small_cols * shard)
        out = jnp.where(at % 2 == 0, out, out[:, ::-1])
        turn = lax.rem(size // 2 - at // 2, size // 2)
        out = lax.dynamic_slice_in_dim(jnp.concatenate([out, out], axis=2), turn, size // 2, 2)
        return out.transpose(0, 2, 1, 3).reshape(-1, size, small_cols * shard)

    vectors = table((0, 1))[0, :, n_other:].reshape((size,) + vectors_weight.shape)
    vectors = wide(vectors.transpose(1, 0, 2).reshape(-1, width))
    rest = table((0, 1, 2, 3))[:, :, :n_other]
    if quick:
        rest = jnp.where(first_tp, rest, rest[::-1])
    shifts = rest[:, :, :n_shift].reshape((2, size) + shifts_weight.shape)
    shifts = shifts.transpose(0, 2, 3, 1, 4).reshape(2, 2, 2, cols)
    shifts = wide(take(shifts, core, 2))
    blank = jnp.zeros((LANES,), single)
    bias = [[shifts[t, 0, :LANES], blank, shifts[t, 1, :LANES]] for t in range(2)]
    last = [shifts[0, 0, LANES:], shifts[1, 0, LANES:], blank, shifts[0, 1, LANES:], shifts[1, 1, LANES:]]
    bias = jnp.concatenate(bias[0] + bias[1] + last).reshape(1, -1)
    offset = rest[:, :, n_shift:].reshape((2, size) + offset_weight.shape)
    offset = offset.transpose(0, 2, 1, 3).reshape(2, 2, units)
    offset = wide(take(offset, core, 1)).reshape(1, 2 * units)

    qkv, normed_one, w_attend = project(base, x_mine, x_other, pieces, bias, vectors)
    attended, lse = attend(qkv, period, frames)
    branch, w_output = output_project(attended, all_two, 2 * units)
    hidden_one, normed_two, mixed_turned, mixed, mixed_away, back, act, du, grad_offset = feed_forward(
        x_mine, x_other, branch, swap_core(branch), g_mine, g_other, all_two, offset, vectors
    )

    back_other, mixed_other = swap_core(back), swap_core(mixed_away)
    keep_a, send_a = expand_grad(base, layout, after(normed_two, back, mixed), du)
    block, grad_hidden, branch_turned, grad_attended, sums = middle(
        back, back_other, hidden_one, g_mine, g_other, mixed, mixed_other, w_output, vectors
    )
    block_other = swap_tp(block)
    keep_b, send_b = reduce_grad(base, layout, mixed_turned, act, branch_turned, attended)
    step = lambda j, *gates: attend_back(
        j, after(qkv, *gates), attended, lse, grad_attended, period, frames
    )
    if quick:
        near_a, near_b = swap_near(send_a), swap_near(send_b)
        grad_0 = step(0, send_a, send_b, block)
        near_a = wide(after(near_a, grad_0)) + wide(keep_a)
        away_a = low(near_a[1])
        tp_a = swap_tp(away_a)
        block_other = after(block_other, grad_0)
        grad_1 = step(1, grad_0, away_a, block_other)
        keep_c, send_c = attend_grad(base, layout, normed_one, (grad_0, grad_1))
        near_c = swap_near(send_c)
        near_b = wide(after(near_b, grad_1)) + wide(keep_b)
        away_b = low(near_b[1])
        tp_b = swap_tp(away_b)
        part_a = near_a[0] + wide(after(tp_a, grad_1))
        part_a, far_a, got_a = fold(part_a, 2, 0)
        grad_2 = step(2, grad_1, send_c, away_b, far_a)
    else:
        grad_0, grad_1, grad_2 = step(0), step(1), step(2)
        total_a, total_b = scatter_any(keep_a, send_a), scatter_any(keep_b, send_b)
    part, part_away, shift_sums = project_back((grad_0, grad_1, grad_2), w_attend)
    part_other = swap_core(part_away)
    if quick:
        part_b, far_b, got_b = fold(near_b[0] + wide(after(tp_b, part)), 2, 0)
        part_c, far_c, got_c = fold(wide(after(near_c, part)) + wide(keep_c), 2, 1)
        part_a, far_a, got_a = fold(part_a + wide(after(got_a, part)), 4, 0)
        part_other = after(part_other, far_a, far_b, far_c)
    input_own, first_sums = first_back(part, part_other, x_mine, grad_hidden, vectors)
    input_other = swap_tp(input_own)
    keep_d, send_d = attend_grad(base, layout, after(normed_one, input_own), (grad_2,))
    if quick:
        near_d = swap_near(send_d)
        part_b, far_b, got_b = fold(part_b + wide(after(got_b, send_d)), 4, 0)
        part_c, far_c, got_c = fold(part_c + wide(after(got_c, send_d)), 4, 1)

    flat = jnp.concatenate(
        [first_sums[:2].reshape(-1), sums[2:6].reshape(-1), shift_sums[0], grad_offset[0]]
    )
    n_vectors, n_flat = 6 * width, flat.size
    total_cols = TRIPLE + 2 * LANES
    flat = jnp.pad(flat, (0, 16 * total_cols - n_flat)).reshape(16, total_cols)

    if quick:
        flat = flat + swap_near(flat)

        def ride(stay, away, flat, send):
            columns = away.shape[-1]
            rows = flat.size // columns
            away = low(jnp.concatenate([away.reshape(-1, columns), flat.reshape(-1, columns)]))
            got = wide(send(away))
            return stay + got[:-rows].reshape(stay.shape), flat + got[-rows:].reshape(flat.shape), away

        part_d = wide(after(near_d, far_b, far_c)) + wide(keep_d)
        for stride in (2, 4):
            halves = part_d.reshape(2, -1, 2, *part_d.shape[2:])
            send = functools.partial(send_fsdp, target=lambda i: i ^ stride)
            part_d, flat, away_d = ride(halves[:, :, 0], halves[:, :, 1], flat, send)
        part_c = part_c + wide(after(got_c, away_d))
        part_c = jnp.concatenate([part_c, part_d], axis=3)[:, 0]
        total_c, flat, away_c = ride(part_c[0], part_c[1], flat, swap_tp)
        total_a = (part_a + wide(after(got_a, away_d)))[0]
        total_b = (part_b + wide(after(got_b, away_d)))[0]
    else:
        keep_c, send_c = attend_grad(base, layout, normed_one, (grad_0, grad_1))
        total_c = [scatter_any(keep_c, send_c), scatter_any(keep_d, send_d)]
        total_c = jnp.concatenate(total_c, axis=1)
        flat = sum_all(flat)
    last = swap_core(jnp.concatenate([total_c, flat]))
    other_c, other_flat = last[:-16], last[-16:].reshape(-1)[:n_flat]
    flat = flat.reshape(-1)[:n_flat]
    total_vectors = take((flat + other_flat)[:n_vectors].reshape(6, size, -1), at, 1)
    slots = join(flat[None, n_vectors:], other_flat[None, n_vectors:], first_core, 0)
    slot_shift = slots[:, : PAIRS * TRIPLE].reshape(2, PAIRS, 3, LANES)[:, :, ::2]
    tail = jnp.where(first_tp, slot_shift[:, 2, :, :HD], slot_shift[:, 2, :, HD:])
    total_shifts = jnp.concatenate([take(slot_shift, half, 1), tail], axis=2)
    total_shifts = total_shifts.transpose(1, 0, 2).reshape(2, -1, size, HD // size)
    total_shifts = take(total_shifts, at, 2)
    total_offset = take(slots[:, PAIRS * TRIPLE :].reshape(2, 2, units), half, 1)
    total_offset = take(total_offset.reshape(-1, size, HD // size), at, 1)

    def both(mine, other, axis):
        return join(mine, other, first_core, axis)

    other_a, other_b = swap_core(total_a), swap_core(total_b)
    total_expand = both(total_a, other_a, 1)
    total_reduce = both(total_b[:, :units], other_b[:, :units], 1).T
    total_output = both(total_b[:, units : units + cols], other_b[:, units : units + cols], 1).T

    def parts(total):
        rows = [
            jnp.concatenate(
                [
                    total[:, p * LANES : (p + 1) * LANES],
                    total[:, TRIPLE + p * HD : TRIPLE + (p + 1) * HD],
                ],
                axis=1,
            )
            for p in range(3)
        ]
        return jnp.stack(rows, axis=1)

    total_attend = both(parts(total_c), parts(other_c), 2)

    attend_new = adamw(
        attend_weight, total_attend, attend_moment, attend_square, rate_matrix, decay_matrix
    )
    shifts_new = adamw(shifts_weight, total_shifts, shifts_moment, shifts_square, rate_vector, 0.0)
    output_new = adamw(
        output_weight, total_output, output_moment, output_square, rate_matrix, decay_matrix
    )
    expand_new = adamw(
        expand_weight, total_expand, expand_moment, expand_square, rate_matrix, decay_matrix
    )
    offset_new = adamw(offset_weight, total_offset, offset_moment, offset_square, rate_vector, 0.0)
    reduce_new = adamw(
        reduce_weight, total_reduce, reduce_moment, reduce_square, rate_matrix, decay_matrix
    )
    vectors_new = adamw(
        vectors_weight, total_vectors, vectors_moment, vectors_square, rate_vector, 0.0
    )
    block = after(block, input_own)
    block_output = join(block[None, :frames], block_other[None, :frames], first_tp, 0)
    input_grad = assemble(half.astype(jnp.int32)[None], input_own, input_other, frames, single)
    return (
        block_output,
        input_grad,
        *attend_new,
        *shifts_new,
        *output_new,
        *expand_new,
        *offset_new,
        *reduce_new,
        *vectors_new,
    )


def solution(mesh):
    tokens = (P("fsdp", "ctx", None),) * 2
    params = (
        (P("fsdp", None, "tp"),) * 3
        + (P(None, "tp", "fsdp"),) * 3
        + (P("tp", "fsdp"),) * 3
        + (P("fsdp", "tp"),) * 3
        + (P("tp", "fsdp"),) * 3
        + (P("tp", "fsdp"),) * 3
        + (P(None, "fsdp"),) * 3
    )
    return jax.shard_map(
        local,
        mesh=mesh,
        in_specs=tokens + params,
        out_specs=tokens + params,
        check_vma=False,
    )
```

```python
import functools
import math

import jax
import jax.numpy as jnp
from jax import lax
from jax.experimental import pallas as pl
from jax.experimental.pallas import tpu as pltpu
from jax.sharding import PartitionSpec as P

HD = 64
STEP = 10


norm_eps = 1e-05
beta_first = 0.9
beta_second = 0.999
adam_eps = 1e-08
rate_matrix = 0.05
rate_vector = 0.5
decay_matrix = 0.01

bfloat = jnp.bfloat16
single = jnp.float32
LANES = 128
TRIPLE = 3 * LANES
PAIRS = 3
ROWS = 384
FEED_ROWS = 256
QUERY_ROWS = 768
KEY_ROWS = 768
SAFE_EXPONENT = 100.0
SWAP = [(0, 1), (1, 0)]
EXP_SCALE = HD ** (-0.5) * math.log2(math.e)
MASK = -1e30
VMEM = 56 * 1024 * 1024
NT = (((1,), (1,)), ((), ()))
TN = (((0,), (0,)), ((), ()))
PARAMS = pltpu.CompilerParams(vmem_limit_bytes=VMEM)


def dot(left, right, dims=(((1,), (0,)), ((), ()))):
    return lax.dot_general(left, right, dims, preferred_element_type=single)


def adamw(param, grad, moment, square, rate, decay):
    moment_new = beta_first * moment + (1.0 - beta_first) * grad
    square_new = beta_second * square + (1.0 - beta_second) * grad * grad
    corrected = moment_new / (1.0 - beta_first**STEP)
    normal_sq = square_new / (1.0 - beta_second**STEP)
    param_new = param - rate * (corrected / (jnp.sqrt(normal_sq) + adam_eps) + decay * param)
    return (param_new, moment_new, square_new)


def norm_parts(values):
    average = jnp.mean(values, axis=-1, keepdims=True)
    centered = values - average
    variance = jnp.mean(centered * centered, axis=-1, keepdims=True)
    inverse = lax.rsqrt(variance + norm_eps)
    return centered * inverse, inverse


def norm_back(grad, unit, inverse, gain):
    scaled = grad * gain
    first = jnp.mean(scaled, axis=-1, keepdims=True)
    second = jnp.mean(scaled * unit, axis=-1, keepdims=True)
    return (scaled - first - unit * second) * inverse


def column_sum(values):
    return jnp.sum(values, axis=0, keepdims=True)


def turned(value):
    return pltpu.roll(value, HD, 1)


def split_three(column):
    high = column.astype(bfloat).astype(single)
    rest = column - high
    middle = rest.astype(bfloat).astype(single)
    return high, middle, (rest - middle).astype(bfloat).astype(single)


def beside(values, half, extras):
    lane = lax.broadcasted_iota(jnp.int32, values.shape, 1)
    base = HD * (1 - half)
    mine = (lane >= HD) if half else (lane < HD)
    out = jnp.where(mine, values, 0.0)
    for place, extra in enumerate(extras):
        out = jnp.where(lane == base + place, extra, out)
    return out.astype(bfloat)


def pad_column(first_row, rows, period, valid):
    row = first_row + lax.broadcasted_iota(jnp.int32, (rows, 1), 0)
    return jnp.where(row % period < valid, 0.0, MASK)


def whole(shape):
    return pl.BlockSpec(shape, lambda *_: (0,) * len(shape))


def struct(shape, dtype):
    return jax.ShapeDtypeStruct(shape, dtype)


def cost(flops, bytes_accessed, transcendentals=0):
    share = 32
    return pl.CostEstimate(
        flops=int(flops) // share,
        bytes_accessed=int(bytes_accessed) // share,
        transcendentals=int(transcendentals) // share,
    )


def project_kernel(base, x_ref, o_ref, *refs):
    pieces, (bias_ref, vec_ref, qkv_ref, nt_ref, w_ref) = refs[:8], refs[8:]
    step = pl.program_id(0)
    cut, rows, _ = pieces[0].shape
    far = vec_ref.shape[1] // (2 * rows)

    @pl.when(step == 0)
    def _():
        flip = base[2] == 1
        swap = base[0] == 1
        lane = lax.broadcasted_iota(jnp.int32, (rows, LANES), 1)
        for z in range(far):
            at = lax.rem(z - base[1] + far, far)
            inner = lax.rem(at, cut)
            read = lambda n: jnp.where(at < cut, pieces[2 * n][inner], pieces[2 * n + 1][inner])
            own, near, away, across = (read(n) for n in range(4))
            for x in range(2):
                here = jnp.where(flip, own, near) if x else jnp.where(flip, near, own)
                there = jnp.where(flip, away, across) if x else jnp.where(flip, across, away)
                both = (jnp.where(swap, there, here), jnp.where(swap, here, there))
                place = slice((2 * z + x) * rows, (2 * z + x + 1) * rows)
                w_ref[0, place, :] = both[0][:, :TRIPLE]
                w_ref[1, place, :] = both[1][:, :TRIPLE]
                mixed = [b[:, TRIPLE : TRIPLE + LANES].astype(single) for b in both]
                last = [b[:, TRIPLE + LANES :].astype(single) for b in both]
                q = jnp.where(lane < HD, mixed[0], turned(mixed[1]))
                k = jnp.where(lane < HD, turned(mixed[0]), mixed[1])
                v = jnp.where(lane < HD, last[0], turned(last[1]))
                for part, value in enumerate((q, k, v)):
                    w_ref[2, place, part * LANES : (part + 1) * LANES] = value.astype(bfloat)

    x = jnp.where(step < pl.num_programs(0) // 2, x_ref[...], o_ref[...]).astype(single)
    unit, _ = norm_parts(x)
    normed = unit * vec_ref[0:1, :] + vec_ref[1:2, :]
    nt_ref[...] = normed.astype(bfloat).T
    normed = normed.astype(bfloat)
    for j in range(PAIRS):
        cols = slice(j * TRIPLE, (j + 1) * TRIPLE)
        qkv_ref[:, cols] = (dot(normed, w_ref[j]) + bias_ref[:, cols]).astype(bfloat)


def own_block(blocks):
    return lambda i, *_: (jnp.minimum(i, blocks - 1), 0)


def other_block(blocks):
    return lambda i, *_: (jnp.maximum(i - blocks, 0), 0)


def project(base, x_mine, x_other, pieces, bias, vectors):
    period, width = x_mine.shape
    blocks = period // ROWS
    rows = 2 * period
    out = PAIRS * TRIPLE
    return pl.pallas_call(
        project_kernel,
        grid_spec=pltpu.PrefetchScalarGridSpec(
            num_scalar_prefetch=1,
            grid=(2 * blocks,),
            in_specs=[
                pl.BlockSpec((ROWS, width), own_block(blocks)),
                pl.BlockSpec((ROWS, width), other_block(blocks)),
                *[whole(p.shape) for p in pieces],
                whole(bias.shape),
                whole(vectors.shape),
            ],
            out_specs=[
                pl.BlockSpec((ROWS, out), lambda i, *_: (i, 0)),
                pl.BlockSpec((width, ROWS), lambda i, *_: (0, i)),
                whole((PAIRS, width, TRIPLE)),
            ],
        ),
        out_shape=[
            struct((rows, out), bfloat),
            struct((width, rows), bfloat),
            struct((PAIRS, width, TRIPLE), bfloat),
        ],
        compiler_params=PARAMS,
        cost_estimate=cost(2 * rows * width * out, 2 * rows * (2 * width + out) + 4 * width * out),
        name="project",
    )(base, x_mine, x_other, *pieces, bias, vectors)


def attend_kernel(period, valid, q_ref, k_ref, v_ref, o_ref, lse_ref, keys, values, longest):
    def norms(value):
        square = value * value
        lane = lax.broadcasted_iota(jnp.int32, value.shape, 1)
        sums = [jnp.sum(jnp.where(mine, square, 0.0), axis=1) for mine in (lane < HD, lane >= HD)]
        return jnp.maximum(jnp.max(sums[0]), jnp.max(sums[1]))

    @pl.when(pl.program_id(1) == 0)
    def _():
        k = k_ref[...].astype(single)
        v = v_ref[...].astype(single)
        pad = pad_column(0, k.shape[0], period, valid)
        for half in range(2):
            keys[half] = beside(k, half, (pad,))
            values[half] = beside(v, half, (1.0,)).T
        longest[0] = norms(k)

    q = q_ref[...].astype(single)
    bound = norms(q) * longest[0] * (EXP_SCALE * EXP_SCALE)
    safe = bound < SAFE_EXPONENT * SAFE_EXPONENT

    def run(shift):
        outs, tops = [], []
        for half in range(2):
            scores = dot(keys[half], beside(q, half, (1.0,)), NT)
            if shift:
                top = jnp.max(scores, axis=0, keepdims=True)
                scores = scores - top
            raised = jnp.exp2(scores * EXP_SCALE)
            both = dot(values[half], raised.astype(bfloat))
            base = HD * (1 - half)
            total = both[base : base + 1, :]
            outs.append(both / total)
            low = jnp.log2(total) / EXP_SCALE
            tops.append(top + low if shift else low)
        row = lax.broadcasted_iota(jnp.int32, outs[0].shape, 0)
        o_ref[...] = jnp.where(row < HD, outs[0], outs[1]).T.astype(bfloat)
        lse_ref[...] = jnp.where(row < HD, tops[0], tops[1]).T

    @pl.when(safe)
    def _():
        run(False)

    @pl.when(jnp.logical_not(safe))
    def _():
        run(True)


def attend(qkv, period, valid):
    rows = qkv.shape[0]
    width = PAIRS * LANES
    part = lambda at: pl.BlockSpec((rows, LANES), lambda j, i: (0, 3 * j + at))
    block = pl.BlockSpec((QUERY_ROWS, LANES), lambda j, i: (i, j))
    return pl.pallas_call(
        functools.partial(attend_kernel, period, valid),
        grid=(PAIRS, rows // QUERY_ROWS),
        in_specs=[pl.BlockSpec((QUERY_ROWS, LANES), lambda j, i: (i, 3 * j)), part(1), part(2)],
        out_specs=[block, block],
        out_shape=[struct((rows, width), bfloat), struct((rows, width), single)],
        scratch_shapes=[
            pltpu.VMEM((2, rows, LANES), bfloat),
            pltpu.VMEM((2, LANES, rows), bfloat),
            pltpu.SMEM((1,), single),
        ],
        compiler_params=PARAMS,
        cost_estimate=cost(16 * rows * rows * LANES * PAIRS, 20 * rows * width, 2 * PAIRS * rows * rows),
        name="attend",
    )(qkv, qkv, qkv)


def attend_back_kernel(
    period, valid, q_ref, k_ref, v_ref, o_ref, lse_ref, g_ref,
    out_ref, queries, queries_turned, grads, grads_turned, total,
):
    step = pl.program_id(0)
    lane_all = lax.broadcasted_iota(jnp.int32, q_ref.shape, 1)

    @pl.when(step == 0)
    def _():
        q = q_ref[...].astype(single)
        g = g_ref[...].astype(single)
        product = g * o_ref[...].astype(single)
        for half in range(2):
            mine = (lane_all >= HD) if half else (lane_all < HD)
            inner = jnp.sum(jnp.where(mine, product, 0.0), axis=1, keepdims=True)
            low = jnp.max(jnp.where(mine, lse_ref[...], -jnp.inf), axis=1, keepdims=True)
            queries[half] = beside(q, half, (1.0,) + split_three(-low))
            grads[half] = beside(g, half, (0.0,) + split_three(-inner))
            queries_turned[half] = queries[half].T
            grads_turned[half] = grads[half].T
        total[...] = jnp.zeros_like(total)

    k = k_ref[...].astype(single)
    v = v_ref[...].astype(single)
    pad = pad_column(step * k.shape[0], k.shape[0], period, valid)
    dks, dvs, dqs = [], [], []
    for half in range(2):
        keys = beside(k, half, (pad, 1.0, 1.0, 1.0))
        values = beside(v, half, (1.0, 1.0, 1.0, 1.0))
        weights = jnp.exp2(dot(queries[half], keys, NT) * EXP_SCALE)
        inner = weights * dot(grads[half], values, NT)
        dvs.append(dot(grads_turned[half], weights.astype(bfloat)))
        low = inner.astype(bfloat)
        dks.append(dot(queries_turned[half], low))
        dqs.append(dot(low, keys))
    scale = HD ** (-0.5)
    here = pl.ds(pl.multiple_of(step * KEY_ROWS, KEY_ROWS), KEY_ROWS)
    row = lax.broadcasted_iota(jnp.int32, dks[0].shape, 0)
    dk = jnp.where(row < HD, dks[0], dks[1]) * scale
    out_ref[here, LANES : 2 * LANES] = dk.T.astype(bfloat)
    out_ref[here, 2 * LANES :] = jnp.where(row < HD, dvs[0], dvs[1]).T.astype(bfloat)
    total[...] += jnp.where(lane_all < HD, dqs[0], dqs[1])

    @pl.when(step == pl.num_programs(0) - 1)
    def _():
        out_ref[:, :LANES] = (total[...] * scale).astype(bfloat)


def attend_back(j, qkv, o, lse, grad, period, valid):
    rows = qkv.shape[0]
    column = lambda at: pl.BlockSpec((rows, LANES), lambda i: (0, at))
    block = lambda at: pl.BlockSpec((KEY_ROWS, LANES), lambda i: (i, at))
    return pl.pallas_call(
        functools.partial(attend_back_kernel, period, valid),
        grid=(rows // KEY_ROWS,),
        in_specs=[column(3 * j), block(3 * j + 1), block(3 * j + 2), column(j), column(j), column(j)],
        out_specs=whole((rows, TRIPLE)),
        out_shape=struct((rows, TRIPLE), bfloat),
        scratch_shapes=[
            pltpu.VMEM((2, rows, LANES), bfloat),
            pltpu.VMEM((2, LANES, rows), bfloat),
            pltpu.VMEM((2, rows, LANES), bfloat),
            pltpu.VMEM((2, LANES, rows), bfloat),
            pltpu.VMEM((rows, LANES), single),
        ],
        compiler_params=PARAMS,
        cost_estimate=cost(40 * rows * rows * LANES, 20 * rows * LANES, 2 * rows * rows),
        name=f"attend_back_{j}",
    )(qkv, qkv, qkv, o, lse, grad)


def output_kernel(o_ref, w_ref, out_ref, full_ref):
    @pl.when(pl.program_id(0) == 0)
    def _():
        lane = lax.broadcasted_iota(jnp.int32, (w_ref.shape[1], LANES), 1)
        full_ref[:, :LANES] = w_ref[0, :, :LANES]
        full_ref[:, LANES : 2 * LANES] = w_ref[1, :, :LANES]
        last = [w_ref[t, :, LANES:].astype(single) for t in range(2)]
        full_ref[:, 2 * LANES :] = jnp.where(lane < HD, last[0], turned(last[1])).astype(bfloat)

    out_ref[...] = dot(o_ref[...], full_ref[...], NT).astype(bfloat)


def output_project(o, weights, place):
    rows, width = o.shape[0], weights.shape[1]
    columns = o.shape[1]
    return pl.pallas_call(
        output_kernel,
        grid=(rows // ROWS,),
        in_specs=[
            pl.BlockSpec((ROWS, columns), lambda i: (i, 0)),
            pl.BlockSpec((2, width, 2 * LANES), lambda i: (0, 0, place // (2 * LANES))),
        ],
        out_specs=[pl.BlockSpec((ROWS, width), lambda i: (i, 0)), whole((width, columns))],
        out_shape=[struct((rows, width), bfloat), struct((width, columns), bfloat)],
        compiler_params=PARAMS,
        cost_estimate=cost(2 * rows * width * columns, 2 * rows * (width + columns)),
        name="output_project",
    )(o, weights)


def feed_kernel(
    x_ref, xo_ref, p_ref, po_ref, g_ref, go_ref, w1_ref, w2_ref, b_ref, vec_ref,
    h_ref, nt_ref, gt_ref, y_ref, yo_ref, dn_ref, act_ref, du_ref, db_ref,
):
    step = pl.program_id(0)
    mine = step < pl.num_programs(0) // 2
    x = jnp.where(mine, x_ref[...], xo_ref[...]).astype(single)
    grad = jnp.where(mine, g_ref[...], go_ref[...])
    hidden = x + (p_ref[...].astype(single) + po_ref[...].astype(single)) + vec_ref[2:3, :]
    h_ref[...] = hidden
    unit, _ = norm_parts(hidden)
    normed = unit * vec_ref[3:4, :] + vec_ref[4:5, :]
    nt_ref[...] = normed.astype(bfloat).T
    gt_ref[...] = grad.T
    normed = normed.astype(bfloat)
    count, _, units = w1_ref.shape
    mixed = back = 0.0

    @pl.when(step == 0)
    def _():
        db_ref[...] = jnp.zeros_like(db_ref)

    for part in range(count):
        cols = slice(part * units, (part + 1) * units)
        u = dot(normed, w1_ref[part]) + b_ref[:, cols]
        phi = 0.5 * (1.0 + lax.erf(u * (0.5**0.5)))
        act = (u * phi).astype(bfloat)
        slope = phi + u * (jnp.exp(-0.5 * u * u) * ((2.0 * math.pi) ** -0.5))
        du = (dot(grad, w2_ref[part]) * slope).astype(bfloat)
        act_ref[:, cols] = act
        du_ref[:, cols] = du
        db_ref[:, cols] += column_sum(du.astype(single))
        mixed = mixed + dot(act, w2_ref[part], NT)
        back = back + dot(du, w1_ref[part], NT)
    dn_ref[...] = back.astype(bfloat)

    @pl.when(mine)
    def _():
        y_ref[...] = mixed.astype(bfloat)

    @pl.when(jnp.logical_not(mine))
    def _():
        yo_ref[...] = mixed.astype(bfloat)


def feed_forward(x_mine, x_other, part, part_other, g_mine, g_other, weights, bias, vectors):
    rows, width = part.shape
    blocks = rows // FEED_ROWS // 2
    count, hidden = weights.shape[0], bias.shape[1]
    units = hidden // count
    tokens = pl.BlockSpec((FEED_ROWS, width), lambda i: (i, 0))
    crossed = pl.BlockSpec((FEED_ROWS, width), lambda i: ((i + blocks) % (2 * blocks), 0))
    wide = pl.BlockSpec((FEED_ROWS, hidden), lambda i: (i, 0))
    tall = pl.BlockSpec((width, FEED_ROWS), lambda i: (0, i))
    own = pl.BlockSpec((FEED_ROWS, width), own_block(blocks))
    other = pl.BlockSpec((FEED_ROWS, width), other_block(blocks))
    weight = lambda at: pl.BlockSpec((count, width, units), lambda i: (0, 0, at))
    return pl.pallas_call(
        feed_kernel,
        grid=(2 * blocks,),
        in_specs=[
            own, other, tokens, crossed, own, other, weight(0), weight(1),
            whole(bias.shape), whole(vectors.shape),
        ],
        out_specs=[tokens, tall, tall, own, other, tokens, wide, wide, whole((1, hidden))],
        out_shape=[
            struct((rows, width), single),
            struct((width, rows), bfloat),
            struct((width, rows), bfloat),
            struct((rows // 2, width), bfloat),
            struct((rows // 2, width), bfloat),
            struct((rows, width), bfloat),
            struct((rows, hidden), bfloat),
            struct((rows, hidden), bfloat),
            struct((1, hidden), single),
        ],
        compiler_params=PARAMS,
        cost_estimate=cost(
            8 * rows * width * hidden,
            18 * rows * width + 4 * rows * hidden + 4 * width * hidden,
            2 * rows * hidden,
        ),
        name="feed_forward",
    )(x_mine, x_other, part, part_other, g_mine, g_other, weights, weights, bias, vectors)


def put(base, keep_ref, send_ref, t, value, cols):
    far, rows = keep_ref.shape[1], keep_ref.shape[2]
    first = base[2] == 0
    for z in range(far):
        at = jnp.bitwise_xor(z, base[1])
        lo = value[2 * z * rows : (2 * z + 1) * rows].astype(bfloat)
        hi = value[(2 * z + 1) * rows : (2 * z + 2) * rows].astype(bfloat)
        keep_ref[t, at, :, cols] = jnp.where(first, lo, hi)
        send_ref[t, at, :, cols] = jnp.where(first, hi, lo)


def expand_grad_kernel(base, left_ref, right_ref, keep_ref, send_ref):
    put(base, keep_ref, send_ref, 0, dot(left_ref[...], right_ref[...]), slice(None))


def expand_grad(base, layout, left, right):
    width, rows = left.shape
    units = right.shape[1] // 2
    shape = (2,) + layout + (units,)
    out = pl.BlockSpec((1,) + layout + (units,), lambda t, base: (t, 0, 0, 0))
    return pl.pallas_call(
        expand_grad_kernel,
        grid_spec=pltpu.PrefetchScalarGridSpec(
            num_scalar_prefetch=1,
            grid=(2,),
            in_specs=[
                whole(left.shape),
                pl.BlockSpec((rows, units), lambda t, base: (0, (t + base[0]) % 2)),
            ],
            out_specs=[out, out],
        ),
        out_shape=[struct(shape, bfloat)] * 2,
        compiler_params=PARAMS,
        cost_estimate=cost(4 * rows * width * units, 2 * rows * (width + 2 * units) + 4 * width * units),
        name="expand_grad",
    )(base, left, right)


def reduce_grad_kernel(base, left_ref, right_ref, branch_ref, o_ref, keep_ref, send_ref, output):
    @pl.when(pl.program_id(0) == 0)
    def _():
        output[...] = dot(branch_ref[...], o_ref[...])

    at = lax.rem(pl.program_id(0) + base[0], 2)
    units = right_ref.shape[1]
    put(base, keep_ref, send_ref, 0, dot(left_ref[...], right_ref[...]), slice(0, units))
    mine = output[:, pl.ds(pl.multiple_of(at * LANES, LANES), LANES)]
    put(base, keep_ref, send_ref, 0, mine, slice(units, units + LANES))
    mixed = output[:, 2 * LANES :]
    mixed = jnp.where(at == 0, mixed, turned(mixed))
    put(base, keep_ref, send_ref, 0, mixed, slice(units + LANES, units + 2 * LANES))


def reduce_grad(base, layout, left, right, branch, o):
    width, rows = left.shape
    units = right.shape[1] // 2
    total = units + 2 * LANES
    shape = (2,) + layout + (total,)
    out = pl.BlockSpec((1,) + layout + (total,), lambda t, base: (t, 0, 0, 0))
    return pl.pallas_call(
        reduce_grad_kernel,
        grid_spec=pltpu.PrefetchScalarGridSpec(
            num_scalar_prefetch=1,
            grid=(2,),
            in_specs=[
                whole(left.shape),
                pl.BlockSpec((rows, units), lambda t, base: (0, (t + base[0]) % 2)),
                whole(branch.shape),
                whole(o.shape),
            ],
            out_specs=[out, out],
            scratch_shapes=[pltpu.VMEM((width, o.shape[1]), single)],
        ),
        out_shape=[struct(shape, bfloat)] * 2,
        compiler_params=PARAMS,
        cost_estimate=cost(4 * rows * width * total, 2 * rows * (2 * width + 2 * total) + 4 * width * total),
        name="reduce_grad",
    )(base, left, right, branch, o)


def pair_grad_kernel(base, left_ref, a_ref, b_ref, keep_ref, send_ref):
    left = left_ref[...]
    pairs = [dot(left, ref[...]) for ref in (a_ref, b_ref)]
    for t in range(2):
        put(base, keep_ref, send_ref, jnp.bitwise_xor(t, base[0]), pairs[t], slice(0, TRIPLE))


def mixed_grad_kernel(base, left_ref, ref, keep_ref, send_ref):
    full = dot(left_ref[...], ref[...])
    q, k, v = (full[:, part * LANES : (part + 1) * LANES] for part in range(3))
    lane = lax.broadcasted_iota(jnp.int32, q.shape, 1)
    mixed = [
        (jnp.where(lane < HD, q, turned(k)), v),
        (jnp.where(lane < HD, turned(q), k), turned(v)),
    ]
    for t in range(2):
        for place in range(2):
            cols = slice(place * LANES, (place + 1) * LANES)
            put(base, keep_ref, send_ref, jnp.bitwise_xor(t, base[0]), mixed[t][place], cols)


def attend_grad(base, layout, left, grads):
    width, rows = left.shape
    count = len(grads)
    columns = TRIPLE if count == 2 else 2 * LANES
    shape = (2,) + layout + (columns,)
    return pl.pallas_call(
        pair_grad_kernel if count == 2 else mixed_grad_kernel,
        grid_spec=pltpu.PrefetchScalarGridSpec(
            num_scalar_prefetch=1,
            grid=(1,),
            in_specs=[whole(left.shape)] + [whole(g.shape) for g in grads],
            out_specs=[whole(shape)] * 2,
        ),
        out_shape=[struct(shape, bfloat)] * 2,
        compiler_params=PARAMS,
        cost_estimate=cost(
            2 * count * rows * width * TRIPLE, 2 * rows * (width + count * TRIPLE) + 8 * width * columns
        ),
        name=f"attend_grad_{count}",
    )(base, left, *grads)


def middle_kernel(
    p_ref, po_ref, h_ref, g_ref, go_ref, y_ref, yo_ref, w_ref, vec_ref,
    out_ref, dh_ref, bt_ref, do_ref, sums_ref,
):
    step = pl.program_id(0)
    mine = step < pl.num_programs(0) // 2
    grad = jnp.where(mine, g_ref[...], go_ref[...]).astype(single)
    hidden = h_ref[...]
    unit, inverse = norm_parts(hidden)
    normed = p_ref[...].astype(single) + po_ref[...].astype(single)
    after = grad + norm_back(normed, unit, inverse, vec_ref[3:4, :])
    bt_ref[...] = after.astype(bfloat).T
    branch = after.astype(bfloat)
    do_ref[...] = dot(branch, w_ref[...]).astype(bfloat)

    @pl.when(step == 0)
    def _():
        sums_ref[...] = jnp.zeros_like(sums_ref)

    @pl.when(mine)
    def _():
        dh_ref[...] = after
        mixed = y_ref[...].astype(single) + yo_ref[...].astype(single)
        out_ref[...] = (hidden + mixed + vec_ref[5:6, :]).astype(bfloat)
        sums_ref[2:3, :] += column_sum(branch.astype(single))
        sums_ref[3:4, :] += column_sum(normed * unit)
        sums_ref[4:5, :] += column_sum(normed)
        sums_ref[5:6, :] += column_sum(grad)


def middle(part, part_other, hidden, g_mine, g_other, mixed, mixed_other, weight, vectors):
    rows, width = part.shape
    blocks = rows // ROWS // 2
    tokens = pl.BlockSpec((ROWS, width), lambda i: (i, 0))
    crossed = pl.BlockSpec((ROWS, width), lambda i: ((i + blocks) % (2 * blocks), 0))
    own = pl.BlockSpec((ROWS, width), own_block(blocks))
    other = pl.BlockSpec((ROWS, width), other_block(blocks))
    columns = weight.shape[1]
    return pl.pallas_call(
        middle_kernel,
        grid=(2 * blocks,),
        in_specs=[
            tokens, crossed, tokens, own, other, own, own, whole(weight.shape), whole(vectors.shape)
        ],
        out_specs=[
            own,
            own,
            pl.BlockSpec((width, ROWS), lambda i: (0, i)),
            pl.BlockSpec((ROWS, columns), lambda i: (i, 0)),
            whole((8, width)),
        ],
        out_shape=[
            struct((rows // 2, width), bfloat),
            struct((rows // 2, width), single),
            struct((width, rows), bfloat),
            struct((rows, columns), bfloat),
            struct((8, width), single),
        ],
        compiler_params=PARAMS,
        cost_estimate=cost(2 * rows * width * columns, 16 * rows * width),
        name="middle",
    )(part, part_other, hidden, g_mine, g_other, mixed, mixed_other, weight, vectors)


def project_back_kernel(a_ref, b_ref, c_ref, w_ref, out_ref, other_ref, sums_ref):
    @pl.when(pl.program_id(0) == 0)
    def _():
        sums_ref[...] = jnp.zeros_like(sums_ref)

    total = 0.0
    for j, ref in enumerate((a_ref, b_ref, c_ref)):
        grad = ref[...]
        total = total + dot(grad, w_ref[j], NT)
        cols = slice(j * TRIPLE, (j + 1) * TRIPLE)
        sums_ref[:, cols] += column_sum(grad.astype(single))
    mine = pl.program_id(0) < pl.num_programs(0) // 2

    @pl.when(mine)
    def _():
        out_ref[...] = total.astype(bfloat)

    @pl.when(jnp.logical_not(mine))
    def _():
        other_ref[...] = total.astype(bfloat)


def project_back(grads, weight):
    rows = grads[0].shape[0]
    width = weight.shape[1]
    block = pl.BlockSpec((ROWS, TRIPLE), lambda i: (i, 0))
    return pl.pallas_call(
        project_back_kernel,
        grid=(rows // ROWS,),
        in_specs=[block, block, block, whole(weight.shape)],
        out_specs=[
            pl.BlockSpec((ROWS, width), own_block(rows // ROWS // 2)),
            pl.BlockSpec((ROWS, width), other_block(rows // ROWS // 2)),
            whole((1, PAIRS * TRIPLE)),
        ],
        out_shape=[struct((rows // 2, width), bfloat)] * 2 + [struct((1, PAIRS * TRIPLE), single)],
        compiler_params=PARAMS,
        cost_estimate=cost(6 * rows * width * TRIPLE, 2 * rows * (width + 3 * TRIPLE)),
        name="project_back",
    )(*grads, weight)


def first_back_kernel(p_ref, po_ref, x_ref, dh_ref, vec_ref, out_ref, sums_ref):
    @pl.when(pl.program_id(0) == 0)
    def _():
        sums_ref[...] = jnp.zeros_like(sums_ref)

    unit, inverse = norm_parts(x_ref[...].astype(single))
    normed = p_ref[...].astype(single) + po_ref[...].astype(single)
    out_ref[...] = (dh_ref[...] + norm_back(normed, unit, inverse, vec_ref[0:1, :])).astype(bfloat)
    sums_ref[0:1, :] += column_sum(normed * unit)
    sums_ref[1:2, :] += column_sum(normed)


def first_back(part, part_other, x_mine, grad_hidden, vectors):
    rows, width = x_mine.shape
    tokens = pl.BlockSpec((ROWS, width), lambda i: (i, 0))
    return pl.pallas_call(
        first_back_kernel,
        grid=(rows // ROWS,),
        in_specs=[tokens, tokens, tokens, tokens, whole(vectors.shape)],
        out_specs=[tokens, whole((8, width))],
        out_shape=[struct((rows, width), bfloat), struct((8, width), single)],
        compiler_params=PARAMS,
        cost_estimate=cost(20 * rows * width, 12 * rows * width),
        name="first_back",
    )(part, part_other, x_mine, grad_hidden, vectors)


def assemble_kernel(place, mine_ref, other_ref, out_ref):
    first = place[0] == 0
    frames = out_ref.shape[0]
    mine, other = mine_ref[...].astype(single), other_ref[...].astype(single)
    out_ref[:, 0, :] = jnp.where(first, mine, other)[:frames].astype(out_ref.dtype)
    out_ref[:, 1, :] = jnp.where(first, other, mine)[:frames].astype(out_ref.dtype)


def assemble(place, mine, other, frames, dtype):
    rows, width = mine.shape
    out = pl.pallas_call(
        assemble_kernel,
        grid_spec=pltpu.PrefetchScalarGridSpec(
            num_scalar_prefetch=1,
            grid=(2,),
            in_specs=[pl.BlockSpec((rows, width // 2), lambda i, place: (0, i))] * 2,
            out_specs=pl.BlockSpec((frames, 2, width // 2), lambda i, place: (0, 0, i)),
        ),
        out_shape=struct((frames, 2, width), dtype),
        compiler_params=PARAMS,
        cost_estimate=cost(0, 12 * rows * width),
        name="assemble",
    )(place, mine, other)
    return out.transpose(1, 0, 2)


def swap_core(value):
    return lax.ppermute(value, "ctx", SWAP)


def swap_tp(value):
    return lax.ppermute(value, "tp", SWAP)


def send_fsdp(value, target):
    size = lax.axis_size("fsdp")
    return lax.ppermute(value, "fsdp", [(i, target(i) % size) for i in range(size)])


def swap_near(value):
    return send_fsdp(value, lambda i: i ^ 1)


def after(value, *others):
    return lax.optimization_barrier((value,) + others)[0]


def wide(value):
    return value.astype(single)


def low(value):
    return value.astype(bfloat)


def join(mine, other, first, axis):
    return jnp.concatenate([jnp.where(first, mine, other), jnp.where(first, other, mine)], axis=axis)


def take(value, index, axis=0):
    return lax.dynamic_index_in_dim(value, index, axis, keepdims=False)


def gather_quick(shard):
    size = lax.axis_size("fsdp")
    far = size // 2
    if size != 8:
        full = lax.all_gather(shard, ("tp", "fsdp"), axis=0, tiled=True)
        return [p[None] for p in jnp.split(full, 4) for _ in range(2)]
    steps = [send_fsdp(shard, lambda i, k=k: i + 2 * k) for k in range(1, far)]
    own = [shard] + steps[::-1]
    cut = far // 2
    lo, hi = jnp.stack(own[:cut]), jnp.stack(own[cut:])
    near_lo, away_lo, away_hi, near_hi = swap_near(lo), swap_tp(lo), swap_tp(hi), swap_near(hi)
    return [lo, hi, near_lo, near_hi, away_lo, away_hi, swap_near(away_lo), swap_tp(near_hi)]


def fold(value, stride, axis):
    shape = value.shape
    halves = value.reshape(shape[:axis] + (shape[axis] // 2, 2) + shape[axis + 1 :])
    away = low(lax.index_in_dim(halves, 1, axis + 1, keepdims=False))
    return lax.index_in_dim(halves, 0, axis + 1, keepdims=False), away, send_fsdp(away, lambda i: i ^ stride)


def sum_all(value):
    stride = 2
    while stride < lax.axis_size("fsdp"):
        value = value + send_fsdp(value, lambda i: i ^ stride)
        stride *= 2
    value = value + swap_near(value)
    return value + swap_tp(value)


def scatter_any(keep, send):
    full = wide(jnp.concatenate([keep, send], axis=2)[:, 0])
    full = lax.psum_scatter(full, "tp", scatter_dimension=0, tiled=True)
    return lax.psum_scatter(full, "fsdp", scatter_dimension=1, tiled=True)[0]


def local(
    layer_input,
    cotangent,
    attend_weight,
    attend_moment,
    attend_square,
    shifts_weight,
    shifts_moment,
    shifts_square,
    output_weight,
    output_moment,
    output_square,
    expand_weight,
    expand_moment,
    expand_square,
    offset_weight,
    offset_moment,
    offset_square,
    reduce_weight,
    reduce_moment,
    reduce_square,
    vectors_weight,
    vectors_moment,
    vectors_square,
):
    size = lax.axis_size("fsdp")
    quick = size == 8
    core, half, at = lax.axis_index("ctx"), lax.axis_index("tp"), lax.axis_index("fsdp")
    first_core, first_tp = core == 0, half == 0
    _, frames, width = layer_input.shape
    period = -(-frames // ROWS) * ROWS
    pad = lambda a: jnp.pad(a, ((0, period - frames), (0, 0)))
    shard = attend_weight.shape[0]
    cols = attend_weight.shape[2] // 2
    units = expand_weight.shape[1] // 2
    layout = (size // 2, shard) if quick else (1, width // 2)
    base = jnp.stack([half, at // 2, at % 2]).astype(jnp.int32)
    if not quick:
        base = jnp.zeros_like(base)

    small = jnp.concatenate(
        [low(shifts_weight).reshape(-1), low(offset_weight).reshape(-1), low(vectors_weight).reshape(-1)]
    )
    small = small.reshape(shard, -1)
    small_cols = small.shape[1]
    mine = lax.dynamic_slice_in_dim(low(attend_weight), core * cols, cols, 2)
    pack_one = jnp.concatenate(
        [mine[:, p, :LANES] for p in range(3)]
        + [mine[:, p, LANES:] for p in range(3)]
        + [small, jnp.zeros((shard, HD - small_cols), bfloat)],
        axis=1,
    )
    pieces = gather_quick(pack_one)
    core_next = after(core, pack_one)
    expand_mine = lax.dynamic_slice_in_dim(low(expand_weight), core_next * units, units, 1)
    reduce_mine = lax.dynamic_slice_in_dim(low(reduce_weight), core_next * units, units, 0).T
    output_mine = lax.dynamic_slice_in_dim(low(output_weight), core_next * cols, cols, 0).T
    pack_two = jnp.concatenate(
        [expand_mine, reduce_mine, output_mine, jnp.zeros((shard, HD), bfloat)], axis=1
    )
    all_two = lax.all_gather(pack_two, ("tp", "fsdp"), axis=0, tiled=True).reshape(2, width, -1)

    x_mine, g_mine = pad(take(layer_input, half)), pad(take(cotangent, half))
    x_other, g_other = swap_core(x_mine), swap_core(g_mine)

    n_shift, n_offset = shifts_weight.size, offset_weight.size
    n_other = n_shift + n_offset

    def table(places):
        out = []
        for n in places:
            halves = pieces[2 * n : 2 * n + 2] if quick else pieces[2 * n : 2 * n + 1]
            out += [p[:, :, 3 * cols : 3 * cols + small_cols].reshape(p.shape[0], -1) for p in halves]
        out = jnp.concatenate(out).reshape(len(places) // 2, 2, -1, small_cols * shard)
        if not quick:
            return out.reshape(-1, size, small_cols * shard)
        out = jnp.where(at % 2 == 0, out, out[:, ::-1])
        turn = lax.rem(size // 2 - at // 2, size // 2)
        out = lax.dynamic_slice_in_dim(jnp.concatenate([out, out], axis=2), turn, size // 2, 2)
        return out.transpose(0, 2, 1, 3).reshape(-1, size, small_cols * shard)

    vectors = table((0, 1))[0, :, n_other:].reshape((size,) + vectors_weight.shape)
    vectors = wide(vectors.transpose(1, 0, 2).reshape(-1, width))
    rest = table((0, 1, 2, 3))[:, :, :n_other]
    if quick:
        rest = jnp.where(first_tp, rest, rest[::-1])
    shifts = rest[:, :, :n_shift].reshape((2, size) + shifts_weight.shape)
    shifts = shifts.transpose(0, 2, 3, 1, 4).reshape(2, 2, 2, cols)
    shifts = wide(take(shifts, core, 2))
    blank = jnp.zeros((LANES,), single)
    bias = [[shifts[t, 0, :LANES], blank, shifts[t, 1, :LANES]] for t in range(2)]
    last = [shifts[0, 0, LANES:], shifts[1, 0, LANES:], blank, shifts[0, 1, LANES:], shifts[1, 1, LANES:]]
    bias = jnp.concatenate(bias[0] + bias[1] + last).reshape(1, -1)
    offset = rest[:, :, n_shift:].reshape((2, size) + offset_weight.shape)
    offset = offset.transpose(0, 2, 1, 3).reshape(2, 2, units)
    offset = wide(take(offset, core, 1)).reshape(1, 2 * units)

    qkv, normed_one, w_attend = project(base, x_mine, x_other, pieces, bias, vectors)
    attended, lse = attend(qkv, period, frames)
    branch, w_output = output_project(attended, all_two, 2 * units)
    hidden_one, normed_two, mixed_turned, mixed, mixed_away, back, act, du, grad_offset = feed_forward(
        x_mine, x_other, branch, swap_core(branch), g_mine, g_other, all_two, offset, vectors
    )

    back_other, mixed_other = swap_core(back), swap_core(mixed_away)
    keep_a, send_a = expand_grad(base, layout, after(normed_two, back, mixed), du)
    block, grad_hidden, branch_turned, grad_attended, sums = middle(
        back, back_other, hidden_one, g_mine, g_other, mixed, mixed_other, w_output, vectors
    )
    block_other = swap_tp(block)
    keep_b, send_b = reduce_grad(base, layout, mixed_turned, act, branch_turned, attended)
    step = lambda j, *gates: attend_back(
        j, after(qkv, *gates), attended, lse, grad_attended, period, frames
    )
    if quick:
        near_a, near_b = swap_near(send_a), swap_near(send_b)
        grad_0 = step(0, send_a, send_b, block)
        near_a = wide(after(near_a, grad_0)) + wide(keep_a)
        away_a = low(near_a[1])
        tp_a = swap_tp(away_a)
        block_other = after(block_other, grad_0)
        grad_1 = step(1, grad_0, away_a, block_other)
        keep_c, send_c = attend_grad(base, layout, normed_one, (grad_0, grad_1))
        near_c = swap_near(send_c)
        near_b = wide(after(near_b, grad_1)) + wide(keep_b)
        away_b = low(near_b[1])
        tp_b = swap_tp(away_b)
        part_a = near_a[0] + wide(after(tp_a, grad_1))
        part_a, far_a, got_a = fold(part_a, 2, 0)
        grad_2 = step(2, grad_1, send_c, away_b, far_a)
    else:
        grad_0, grad_1, grad_2 = step(0), step(1), step(2)
        total_a, total_b = scatter_any(keep_a, send_a), scatter_any(keep_b, send_b)
    part, part_away, shift_sums = project_back((grad_0, grad_1, grad_2), w_attend)
    part_other = swap_core(part_away)
    if quick:
        part_b, far_b, got_b = fold(near_b[0] + wide(after(tp_b, part)), 2, 0)
        part_c, far_c, got_c = fold(wide(after(near_c, part)) + wide(keep_c), 2, 1)
        part_a, far_a, got_a = fold(part_a + wide(after(got_a, part)), 4, 0)
        part_other = after(part_other, far_a, far_b, far_c)
    input_own, first_sums = first_back(part, part_other, x_mine, grad_hidden, vectors)
    input_other = swap_tp(input_own)
    keep_d, send_d = attend_grad(base, layout, after(normed_one, input_own), (grad_2,))
    if quick:
        near_d = swap_near(send_d)
        part_b, far_b, got_b = fold(part_b + wide(after(got_b, send_d)), 4, 0)
        part_c, far_c, got_c = fold(part_c + wide(after(got_c, send_d)), 4, 1)

    flat = jnp.concatenate(
        [first_sums[:2].reshape(-1), sums[2:6].reshape(-1), shift_sums[0], grad_offset[0]]
    )
    n_vectors, n_flat = 6 * width, flat.size
    total_cols = TRIPLE + 2 * LANES
    flat = jnp.pad(flat, (0, 16 * total_cols - n_flat)).reshape(16, total_cols)

    if quick:
        flat = flat + swap_near(flat)

        def ride(stay, away, flat, send):
            columns = away.shape[-1]
            rows = flat.size // columns
            away = low(jnp.concatenate([away.reshape(-1, columns), flat.reshape(-1, columns)]))
            got = wide(send(away))
            return stay + got[:-rows].reshape(stay.shape), flat + got[-rows:].reshape(flat.shape), away

        part_d = wide(after(near_d, far_b, far_c)) + wide(keep_d)
        for stride in (2, 4):
            halves = part_d.reshape(2, -1, 2, *part_d.shape[2:])
            send = functools.partial(send_fsdp, target=lambda i: i ^ stride)
            part_d, flat, away_d = ride(halves[:, :, 0], halves[:, :, 1], flat, send)
        part_c = part_c + wide(after(got_c, away_d))
        part_c = jnp.concatenate([part_c, part_d], axis=3)[:, 0]
        total_c, flat, away_c = ride(part_c[0], part_c[1], flat, swap_tp)
        total_a = (part_a + wide(after(got_a, away_d)))[0]
        total_b = (part_b + wide(after(got_b, away_d)))[0]
    else:
        keep_c, send_c = attend_grad(base, layout, normed_one, (grad_0, grad_1))
        total_c = [scatter_any(keep_c, send_c), scatter_any(keep_d, send_d)]
        total_c = jnp.concatenate(total_c, axis=1)
        flat = sum_all(flat)
    last = swap_core(jnp.concatenate([total_c, flat]))
    other_c, other_flat = last[:-16], last[-16:].reshape(-1)[:n_flat]
    flat = flat.reshape(-1)[:n_flat]
    total_vectors = take((flat + other_flat)[:n_vectors].reshape(6, size, -1), at, 1)
    slots = join(flat[None, n_vectors:], other_flat[None, n_vectors:], first_core, 0)
    slot_shift = slots[:, : PAIRS * TRIPLE].reshape(2, PAIRS, 3, LANES)[:, :, ::2]
    tail = jnp.where(first_tp, slot_shift[:, 2, :, :HD], slot_shift[:, 2, :, HD:])
    total_shifts = jnp.concatenate([take(slot_shift, half, 1), tail], axis=2)
    total_shifts = total_shifts.transpose(1, 0, 2).reshape(2, -1, size, HD // size)
    total_shifts = take(total_shifts, at, 2)
    total_offset = take(slots[:, PAIRS * TRIPLE :].reshape(2, 2, units), half, 1)
    total_offset = take(total_offset.reshape(-1, size, HD // size), at, 1)

    def both(mine, other, axis):
        return join(mine, other, first_core, axis)

    other_a, other_b = swap_core(total_a), swap_core(total_b)
    total_expand = both(total_a, other_a, 1)
    total_reduce = both(total_b[:, :units], other_b[:, :units], 1).T
    total_output = both(total_b[:, units : units + cols], other_b[:, units : units + cols], 1).T

    def parts(total):
        rows = [
            jnp.concatenate(
                [
                    total[:, p * LANES : (p + 1) * LANES],
                    total[:, TRIPLE + p * HD : TRIPLE + (p + 1) * HD],
                ],
                axis=1,
            )
            for p in range(3)
        ]
        return jnp.stack(rows, axis=1)

    total_attend = both(parts(total_c), parts(other_c), 2)

    attend_new = adamw(
        attend_weight, total_attend, attend_moment, attend_square, rate_matrix, decay_matrix
    )
    shifts_new = adamw(shifts_weight, total_shifts, shifts_moment, shifts_square, rate_vector, 0.0)
    output_new = adamw(
        output_weight, total_output, output_moment, output_square, rate_matrix, decay_matrix
    )
    expand_new = adamw(
        expand_weight, total_expand, expand_moment, expand_square, rate_matrix, decay_matrix
    )
    offset_new = adamw(offset_weight, total_offset, offset_moment, offset_square, rate_vector, 0.0)
    reduce_new = adamw(
        reduce_weight, total_reduce, reduce_moment, reduce_square, rate_matrix, decay_matrix
    )
    vectors_new = adamw(
        vectors_weight, total_vectors, vectors_moment, vectors_square, rate_vector, 0.0
    )
    block = after(block, input_own)
    block_output = join(block[None, :frames], block_other[None, :frames], first_tp, 0)
    input_grad = assemble(half.astype(jnp.int32)[None], input_own, input_other, frames, single)
    return (
        block_output,
        input_grad,
        *attend_new,
        *shifts_new,
        *output_new,
        *expand_new,
        *offset_new,
        *reduce_new,
        *vectors_new,
    )


def solution(mesh):
    tokens = (P("fsdp", "ctx", None),) * 2
    params = (
        (P("fsdp", None, "tp"),) * 3
        + (P(None, "tp", "fsdp"),) * 3
        + (P("tp", "fsdp"),) * 3
        + (P("fsdp", "tp"),) * 3
        + (P("tp", "fsdp"),) * 3
        + (P("tp", "fsdp"),) * 3
        + (P(None, "fsdp"),) * 3
    )
    return jax.shard_map(
        local,
        mesh=mesh,
        in_specs=tokens + params,
        out_specs=tokens + params,
        check_vma=False,
    )
```
